128 devices in a mesh: replica: 4 (over x_hi, core), shard: 32 (over z, x_lo, y).
Axes of the slice: x: 4 (x_hi: 2, x_lo: 2; x = x_hi * 2 + x_lo), y: 4, z: 4, core: 2. Of those that a mesh axis runs over, the one named last changes fastest.
Arguments:
- tokens: bfloat16 [16384, 2048], P(('replica', 'shard')), may hold values from -6 to 6
- segment_ids: int32 [128, 128], P(('replica', 'shard')), may hold values from 0 to 3, never falling along the last dimension, each value on 1 to 64 neighbouring positions
- cotangent: bfloat16 [16384, 2048], P(('replica', 'shard')), may hold values from -6 to 6
- ln1_gain: bfloat16 [2048], P('shard'), may hold values from 0.5 to 1.5
- ln1_bias: bfloat16 [2048], P('shard'), may hold values from -2 to 2
- qkv_weight: bfloat16 [2048, 6144], P('shard'), may hold values from -0.125 to 0.125
- qkv_bias: bfloat16 [6144], P('shard'), may hold values from -3 to 3
- out_weight: bfloat16 [2048, 2048], P('shard'), may hold values from -0.375 to 0.375
- ln2_gain: bfloat16 [2048], P('shard'), may hold values from 0.5 to 1.5
- ln2_bias: bfloat16 [2048], P('shard'), may hold values from -2 to 2
- gate_weight: bfloat16 [2048, 5632], P('shard'), may hold values from -0.125 to 0.125
- up_weight: bfloat16 [2048, 5632], P('shard'), may hold values from -0.125 to 0.125
- down_weight: bfloat16 [5632, 2048], P('shard'), may hold values from -0.15625 to 0.15625
Outputs:
- activations: bfloat16 [16384, 2048], P(('replica', 'shard'))
- input_grad: bfloat16 [16384, 2048], P(('replica', 'shard'))
- ln1_gain_grad: float32 [2048], P('shard')
- ln1_bias_grad: float32 [2048], P('shard')
- qkv_weight_grad: float32 [2048, 6144], P('shard')
- qkv_bias_grad: float32 [6144], P('shard')
- out_weight_grad: float32 [2048, 2048], P('shard')
- ln2_gain_grad: float32 [2048], P('shard')
- ln2_bias_grad: float32 [2048], P('shard')
- gate_weight_grad: float32 [2048, 5632], P('shard')
- up_weight_grad: float32 [2048, 5632], P('shard')
- down_weight_grad: float32 [5632, 2048], P('shard')
The draws below stay inside these ranges and needn't reach their ends.
Inputs may be any that keep to these rules, and one draw needn't show every extreme that they name: `segment_ids`: in each sequence the ids never fall from one position to the next; each segment holds 1 to half of 128 positions, and one holds exactly that many.
All inputs are finite; a program needn't handle non-finite values.
Results may differ from the reference program's by a relative error of at most 0.029.
Values may be sent and summed in bfloat16 or wider, within the bound.
A program may use at most 384 MiB of HBM per device.

```python
import math
import jax
import jax.numpy as jnp
import numpy as np
from jax import lax

D = 2048
HEADS = 32
HEAD_DIM = 64
FF = 5632
ROT = 16
LEN = 128
SEQS = 128
TOKENS = 16384


def shard_levels(key, dims, pieces, low, top_value):
    def one(axis_at, parts):
        heights = jax.random.uniform(jax.random.fold_in(jax.random.fold_in(key, 6), axis_at), (parts,), jnp.float32, low / len(pieces), top_value / len(pieces))
        return jnp.repeat(jnp.exp(heights), dims[axis_at] // parts).reshape((-1,) + (1,) * (len(dims) - axis_at - 1))

    loudness = one(*pieces[0])
    for cut in pieces[1:]:
        loudness = loudness * one(*cut)
    return loudness


def length_profile(number_of, total, most, lean):
    portions = [(1 << 20) // math.isqrt(standing ** lean) + 1 for standing in range(2, number_of + 1)]
    surplus, given = total - most - (number_of - 1), [1] * (number_of - 1)
    while surplus > 0:
        candidates = [i for i in range(number_of - 1) if given[i] < most]
        pool, left = sum([portions[i] for i in candidates]), surplus
        for i in candidates:
            addition = min(most - given[i], max(1, left * portions[i] // pool), surplus)
            given[i] = given[i] + addition
            surplus = surplus - addition
    return np.array([most] + given)


def ragged(stream_key, amount, total, most, lean):
    if amount == 2:
        one = jax.random.randint(stream_key, (), max(1, total - most), min(most, total - 1) + 1)
        return jnp.stack([one, total - one])
    lengths = jnp.asarray(length_profile(amount, total, most, lean), jnp.int32)
    pairs = (amount - 1) // 2
    donor, sink = lengths[1:1 + 2 * pairs:2], lengths[2:2 + 2 * pairs:2]
    slack = jnp.minimum(donor - 1, most - sink)
    passed = jax.random.randint(jax.random.fold_in(stream_key, 1), (pairs,), 0, 1 << 20) % (slack + 1)
    lengths = lengths.at[1:1 + 2 * pairs:2].set(donor - passed).at[2:2 + 2 * pairs:2].set(sink + passed)
    return lengths[jax.random.permutation(jax.random.fold_in(stream_key, 2), amount)]


def noise(stream_key, dims, deviation, limit, split=(), kind=jnp.bfloat16):
    level = shard_levels(stream_key, dims, split, -0.22, 0.18) if split else 1.0
    values = jax.random.normal(stream_key, dims, jnp.float32) * deviation * level
    return jnp.minimum(jnp.maximum(values, -limit), limit).astype(kind)


def setup_inputs(seed: int = 0) -> dict:
    splits = jax.random.split(jax.random.key(seed), 14)
    return {
        "tokens": noise(splits[0], (TOKENS, D), 1.0, 6.0, ((0, 128),)),
        "segment_ids": jax.vmap(lambda own: jnp.searchsorted(jnp.cumsum(ragged(own, 4, LEN, LEN // 2, 0)), jnp.arange(LEN), side="right"))(jax.random.split(splits[1], SEQS)).reshape((SEQS, LEN)).astype(jnp.int32),
        "cotangent": noise(splits[2], (TOKENS, D), 1.0, 6.0, ((0, 128),)),
        "ln1_gain": jnp.clip(1.0 + 0.1 * jax.random.normal(splits[3], (D,), jnp.float32), 0.5, 1.5).astype(jnp.bfloat16),
        "ln1_bias": noise(splits[4], (D,), 0.3, 2.0, ((0, 32),)),
        "qkv_weight": noise(splits[5], (D, 3 * D), D ** -0.5, 0.125, ((0, 32),)),
        "qkv_bias": noise(splits[6], (3 * D,), 0.5, 3.0, ((0, 32),)),
        "out_weight": noise(splits[7], (D, D), (D // 8) ** -0.5, 0.375, ((0, 32),)),
        "ln2_gain": jnp.clip(1.0 + 0.1 * jax.random.normal(splits[8], (D,), jnp.float32), 0.5, 1.5).astype(jnp.bfloat16),
        "ln2_bias": noise(splits[9], (D,), 0.3, 2.0, ((0, 32),)),
        "gate_weight": noise(splits[10], (D, FF), D ** -0.5, 0.125, ((0, 32),)),
        "up_weight": noise(splits[11], (D, FF), D ** -0.5, 0.125, ((0, 32),)),
        "down_weight": noise(splits[12], (FF, D), (FF // 4) ** -0.5, 0.15625, ((0, 32),)),
    }


@jax.custom_vjp
def low(v):
    return lax.optimization_barrier(v.astype(jnp.bfloat16)).astype(jnp.float32)

@jax.custom_vjp
def low_back(v):
    return v

def low_keep(v):
    return (low(v), None)

def low_pass(kept, grad):
    return (grad,)

def back_keep(v):
    return (v, None)

def back_low(kept, grad):
    return (low(grad),)
low.defvjp(low_keep, low_pass)
low_back.defvjp(back_keep, back_low)
highest = lax.Precision.HIGHEST
norm_epsilon = 1e-05
masked_score = -1000000000.0

def layer_norm(values, gain, shift):
    center = values - lax.optimization_barrier(jnp.mean(values, axis=-1, keepdims=True))
    variance = lax.optimization_barrier(jnp.mean(center * center, axis=-1, keepdims=True))
    return center * lax.rsqrt(variance + norm_epsilon) * gain + shift

def matmul(left, right):
    return jnp.dot(left, right, precision=highest, preferred_element_type=jnp.float32)

def layout(segments):
    length = segments.shape[1]
    same = segments[:, :, None] == segments[:, None, :]
    query_index = lax.broadcasted_iota(jnp.int32, (length, length), 0)
    key_index = lax.broadcasted_iota(jnp.int32, (length, length), 1)
    allowed = same & (key_index <= query_index)[None]
    places = lax.optimization_barrier(jnp.sum((same & (key_index < query_index)[None]).astype(jnp.int32), axis=-1)).astype(jnp.float32)
    half_rot = ROT // 2
    freqs = 10000.0 ** (-(jnp.arange(half_rot, dtype=jnp.float32) * 2.0) / ROT)
    angles = places[:, :, None, None] * freqs
    return (allowed[:, None], jnp.cos(angles), jnp.sin(angles))

def rotate(values, cosine, sine):
    half_rot = ROT // 2
    first = values[..., :half_rot]
    second = values[..., half_rot:ROT]
    return jnp.concatenate([first * cosine - second * sine, second * cosine + first * sine, values[..., ROT:]], axis=-1)

def forward(inputs, allowed, cosine, sine, params):
    gain_one, bias_one, weight_qkv, bias_qkv, weight_out, gain_two, bias_two, weight_gate, weight_up, weight_down = params
    group, length = (inputs.shape[0], inputs.shape[1])
    entry_one = low(layer_norm(inputs, gain_one, bias_one))
    projected = low_back(matmul(entry_one, weight_qkv) + bias_qkv)
    projected = projected.reshape(group, length, 3, HEADS, HEAD_DIM)
    queries = low(rotate(projected[:, :, 0], cosine, sine))
    keys = low(rotate(projected[:, :, 1], cosine, sine))
    values = low(projected[:, :, 2])
    scores = low_back(jnp.einsum('slhd,smhd->shlm', queries, keys, precision=highest) * HEAD_DIM ** (-0.5))
    scores = jnp.where(allowed, scores, masked_score)
    probs = jax.nn.softmax(scores, axis=-1)
    mixed = jnp.einsum('shlm,smhd->slhd', low(probs), values, precision=highest).reshape(group, length, D)
    mixed = low_back(low(mixed))
    middle = inputs + low_back(matmul(mixed, weight_out))
    entry_two = low(layer_norm(middle, gain_two, bias_two))
    gate = low_back(matmul(entry_two, weight_gate))
    upward = low_back(matmul(entry_two, weight_up))
    hidden = low_back(low(jax.nn.silu(gate) * upward))
    return middle + low_back(matmul(hidden, weight_down))

def reference(tokens, segment_ids, cotangent, ln1_gain, ln1_bias, qkv_weight, qkv_bias, out_weight, ln2_gain, ln2_bias, gate_weight, up_weight, down_weight):
    params = tuple((item.astype(jnp.float32) for item in (ln1_gain, ln1_bias, qkv_weight, qkv_bias, out_weight, ln2_gain, ln2_bias, gate_weight, up_weight, down_weight)))
    group = math.gcd(SEQS, max(1, 4096 // LEN))
    blocks = SEQS // group
    inputs_all = tokens.astype(jnp.float32).reshape(blocks, group, LEN, D)
    grads_all = cotangent.astype(jnp.float32).reshape(blocks, group, LEN, D)
    segments_all = segment_ids.reshape(blocks, group, LEN)

    def accumulate(totals, items):
        block_inputs, block_grads, block_segments = items
        allowed, cosine, sine = layout(block_segments)
        result, pullback = jax.vjp(lambda given, weights: forward(given, allowed, cosine, sine, weights), block_inputs, params)
        grad_inputs, grad_params = pullback(block_grads)
        totals = jax.tree.map(lambda total, extra: total + extra, totals, grad_params)
        return (totals, (result.astype(jnp.bfloat16), grad_inputs.astype(jnp.bfloat16)))
    zeros = tuple((jnp.zeros_like(item) for item in params))
    totals, (results, grad_inputs) = lax.scan(accumulate, zeros, (inputs_all, grads_all, segments_all))
    gain_one, bias_one, weight_qkv, bias_qkv, weight_out, gain_two, bias_two, weight_gate, weight_up, weight_down = totals
    return (results.reshape(TOKENS, D), grad_inputs.reshape(TOKENS, D), gain_one, bias_one, weight_qkv, bias_qkv, weight_out, gain_two, bias_two, weight_gate, weight_up, weight_down)
```

```python
import functools
import jax, jax.numpy as jnp
from jax import lax
from jax.sharding import PartitionSpec as P, Mesh
from jax.experimental import pallas as pl
from jax.experimental.pallas import tpu as pltpu

AXES = ("xh", "c", "z", "xl", "y")


class Place:
    def __init__(self):
        self.xh, self.c, self.z, self.xl, self.y = (lax.axis_index(a) for a in AXES)
        self.x = self.xh * 2 + self.xl

    def at(self, dx=0, dy=0, dz=0, dc=0):
        x = lax.rem(self.x + dx + 4, 4) if dx else self.x
        return (
            x // 2 if dx else self.xh,
            lax.rem(self.c + dc, 2) if dc else self.c,
            lax.rem(self.z + dz + 4, 4) if dz else self.z,
            lax.rem(x, 2) if dx else self.xl,
            lax.rem(self.y + dy + 4, 4) if dy else self.y,
        )


def barrier(targets):
    sem = pltpu.get_barrier_semaphore()
    for target in targets:
        pl.semaphore_signal(sem, inc=1, device_id=target, device_id_type=pl.DeviceIdType.MESH)
    pl.semaphore_wait(sem, len(targets))


class Copies:
    def __init__(self, send, recv):
        self.send, self.recv, self.used, self.all = send, recv, 0, []

    def push(self, src, dst, target):
        copy = pltpu.make_async_remote_copy(
            src_ref=src, dst_ref=dst, send_sem=self.send.at[self.used],
            recv_sem=self.recv.at[self.used], device_id=target, device_id_type=pl.DeviceIdType.MESH)
        self.used += 1
        self.all.append(copy)
        copy.start()
        return copy

    def finish(self):
        for copy in self.all:
            copy.wait_send()


N_REMOTE, N_LOCAL = 96, 16


def gather_kernel(tok, cot, seg, wq, sm, wg, wu, wo, wd,
                  toks, cots, segs, gq, gs, gg, gu, go, gd, send, recv, lsem):
    p = Place()
    barrier([p.at(dy=d) for d in (1, 2, 3)] + [p.at(dz=d) for d in (1, 2, 3)] + [p.at(dx=1), p.at(dx=-1), p.at(dc=1)])
    cp = Copies(send, recv)
    locals_ = []

    def local(src, dst):
        copy = pltpu.make_async_copy(src, dst, lsem.at[len(locals_)])
        copy.start()
        locals_.append(copy)
        return copy

    x1, x3, sib = p.at(dx=1), p.at(dx=-1), p.at(dc=1)
    half = pl.ds(pl.multiple_of(p.c * 32, 32), 32)
    cols = pl.ds(pl.multiple_of(p.c * 1024, 1024), 1024)
    acts = []

    def share(src, dst):
        local(src, dst.at[p.y])
        for d in (1, 3, 2):
            acts.append(cp.push(src, dst.at[p.y], p.at(dy=d)))

    rows = [dict(src=s, g=g) for s, g in ((wq, gq), (sm, gs), (wg, gg), (wu, gu))]
    plane = [dict(src=s, g=g, cut=c) for s, g, c in ((wo, go, 32), (wd, gd, 96))]

    def stage_y(a):
        a["local"] = local(a["src"].at[p.y, half], a["g"].at[p.z, p.xl, p.y, half])
        a["y"] = [cp.push(a["src"].at[lax.rem(p.y + d, 4), half], a["g"].at[p.z, p.xl, p.y, half], p.at(dy=d)) for d in (1, 3, 2)]

    def stage_z(a):
        if "cut" in a:
            a["local"] = local(a["src"].at[:, cols], a["g"].at[p.z, p.xl, :, cols])
            a["z"] = [cp.push(a["src"].at[:, cols], a["g"].at[p.z, p.xl, :, cols], p.at(dz=d)) for d in (1, 3, 2)]
        else:
            a["local"].wait()
            for c in a["y"]:
                c.wait_recv()
            a["z"] = [cp.push(a["g"].at[p.z, p.xl, :, half], a["g"].at[p.z, p.xl, :, half], p.at(dz=d)) for d in (1, 3, 2)]

    def parts(a, xl):
        g = a["g"]
        if "cut" in a:
            k = a["cut"]
            r = g.shape[2]
            return g.at[:, xl, 0:k, cols], g.at[:, xl, k:r, cols], g.at[:, xl, :, cols]
        return g.at[:, xl, 0:2, half], g.at[:, xl, 2:4, half], g.at[:, xl, :, half]

    def stage_x(a):
        if "cut" in a:
            a["local"].wait()
        for c in a["z"]:
            c.wait_recv()
        lo, hi, full = parts(a, p.xl)
        a["x"] = [cp.push(lo, lo, x1), cp.push(hi, hi, x3)]
        a["c"] = [cp.push(full, full, sib)]

    def stage_c(a):
        lo, hi, full = parts(a, 1 - p.xl)
        a["x"][0].wait_recv()
        a["c"].append(cp.push(lo, lo, sib))
        a["x"][1].wait_recv()
        a["c"].append(cp.push(hi, hi, sib))

    q, s, g, u = rows
    o, d = plane
    stage_y(q); stage_y(s)
    share(tok, toks)
    share(seg, segs)
    stage_y(g); stage_y(u)
    share(cot, cots)
    stage_z(q); stage_z(s); stage_z(o)
    stage_z(g); stage_z(u); stage_z(d)
    for a in (q, s, o, g, u, d):
        stage_x(a)
    for a in (q, s, o, g, u, d):
        stage_c(a)
    for c in acts:
        c.wait_recv()
    for a in (q, s, o, g, u, d):
        for c in a["c"]:
            c.wait_recv()
    cp.finish()
    for copy in locals_[:]:
        if not any(copy is a["local"] for a in rows + plane):
            copy.wait()


def gather(tok, cot, seg, wq, sm, wg, wu, wo, wd):
    bf = jnp.bfloat16
    S = jax.ShapeDtypeStruct
    hbm = pl.BlockSpec(memory_space=pl.ANY)
    outs = (S((4, 128, 2048), bf), S((4, 128, 2048), bf), S((4, 8, 128), jnp.float32),
            S((4, 2, 4, 64, 1536), bf), S((4, 2, 4, 64, 128), bf), S((4, 2, 4, 64, 1408), bf), S((4, 2, 4, 64, 1408), bf),
            S((4, 2, 64, 2048), bf), S((4, 2, 176, 2048), bf))
    return pl.pallas_call(
        gather_kernel, out_shape=outs, in_specs=[hbm] * 9, out_specs=(hbm,) * 9,
        scratch_shapes=[pltpu.SemaphoreType.DMA((N_REMOTE,)), pltpu.SemaphoreType.DMA((N_REMOTE,)), pltpu.SemaphoreType.DMA((N_LOCAL,))],
        compiler_params=pltpu.CompilerParams(collective_id=1, has_side_effects=True),
        name="gather",
    )(tok, cot, seg, wq, sm, wg, wu, wo, wd)


def add_into(out, parts):
    total = parts[0][...].astype(jnp.float32)
    for part in parts[1:]:
        total = total + part[...].astype(jnp.float32)
    out[...] = total.astype(out.dtype)


class Reduce:
    def __init__(self, p, cp, source, bufs, out, cut=None):
        self.p, self.cp, self.source, self.out, self.cut = p, cp, source, out, cut
        self.h, self.rc, self.rx, self.rz, self.rxh, self.ky = bufs
        if cut is None:
            self.mine = lambda ref, c: ref.at[:, :, :, pl.ds(pl.multiple_of(c * 32, 32), 32)]
        else:
            self.mine = lambda ref, c: ref.at[:, :, :, pl.ds(pl.multiple_of(c * 1024, 1024), 1024)]

    def start(self, sem):
        p = self.p
        self.load = pltpu.make_async_copy(self.mine(self.source, p.c), self.h, sem)
        self.load.start()
        self.core = self.cp.push(self.mine(self.source, 1 - p.c), self.rc, p.at(dc=1))

    def blocks(self, ref):
        return (ref.shape[-2] if self.cut is not None else ref.shape[-3])

    def stage_x(self):
        p, h, rc = self.p, self.h, self.rc
        self.load.wait()
        self.core.wait_recv()

        def foreign(i, _):
            add_into(h.at[i, 1 - p.xl], (h.at[i, 1 - p.xl], rc.at[i, 1 - p.xl]))
            return 0

        lax.fori_loop(0, 4, foreign, 0)
        k, n = (2, 4) if self.cut is None else (self.cut, h.shape[2])
        self.x = [
            self.cp.push(h.at[:, 1 - p.xl, 0:k], self.rx.at[:, 0:k], p.at(dx=1)),
            self.cp.push(h.at[:, 1 - p.xl, k:n], self.rx.at[:, k:n], p.at(dx=-1)),
        ]

    def stage_z(self):
        p, h, rc, rx = self.p, self.h, self.rc, self.rx
        for c in self.x:
            c.wait_recv()

        def own(i, _):
            add_into(h.at[i, p.xl], (h.at[i, p.xl], rc.at[i, p.xl], rx.at[i]))
            return 0

        lax.fori_loop(0, 4, own, 0)
        self.zs = [self.cp.push(h.at[lax.rem(p.z + d, 4), p.xl], self.rz.at[d - 1], p.at(dz=d)) for d in (1, 3, 2)]

    def stage_xh(self):
        p, h, rz = self.p, self.h, self.rz
        for c in self.zs:
            c.wait_recv()
        add_into(h.at[p.z, p.xl], (h.at[p.z, p.xl], rz.at[0], rz.at[1], rz.at[2]))
        self.xh = self.cp.push(h.at[p.z, p.xl], self.rxh, p.at(dx=2))

    def stage_y(self, sem):
        p = self.p
        self.xh.wait_recv()
        add_into(self.ky, (self.h.at[p.z, p.xl], self.rxh))
        if self.cut is None:
            half = pl.ds(pl.multiple_of(p.c * 32, 32), 32)
            self.own = pltpu.make_async_copy(self.ky.at[p.y], self.out.at[p.y, half], sem)
            self.own.start()
            self.ys = [
                self.cp.push(self.ky.at[lax.rem(p.y + d, 4)], self.out.at[p.y, half], p.at(dy=d)) for d in (1, 3, 2)
            ]
        else:
            cols = pl.ds(pl.multiple_of(p.c * 1024, 1024), 1024)
            self.own = pltpu.make_async_copy(self.ky, self.out.at[:, cols], sem)
            self.own.start()
            self.ys = [self.cp.push(self.ky, self.out.at[:, cols], p.at(dc=1))]

    def stage_end(self):
        p = self.p
        for c in self.ys:
            c.wait_recv()
        self.own.wait()
        if self.cut is None:
            half = pl.ds(pl.multiple_of(p.c * 32, 32), 32)
            self.last = self.cp.push(self.out.at[:, half], self.out.at[:, half], p.at(dc=1))
        else:
            self.last = None

    def finish(self):
        if self.last is not None:
            self.last.wait_recv()


def reduce_scratch(shape, plane):
    bf = jnp.bfloat16
    if plane:
        rows = shape[2]
        tail = (rows, 1024)
    else:
        tail = (4, 32, shape[-1])
    return [pltpu.VMEM((4, 2) + tail, bf), pltpu.VMEM((4, 2) + tail, bf), pltpu.VMEM((4,) + tail, bf),
            pltpu.VMEM((3,) + tail, bf), pltpu.VMEM(tail, bf), pltpu.VMEM(tail, bf)]


def run_reduces(reduces, sems):
    for r in reduces:
        r.stage_x()
    for r in reduces:
        r.stage_z()
    for r in reduces:
        r.stage_xh()
    for i, r in enumerate(reduces):
        r.stage_y(sems.at[i])
    for r in reduces:
        r.stage_end()
    for r in reduces:
        r.finish()


def peers(p):
    return [p.at(dy=d) for d in (1, 2, 3)] + [p.at(dz=d) for d in (1, 2, 3)] + [p.at(dx=d) for d in (1, 2, -1)] + [p.at(dc=1)]


ROWS = 16


def middle_kernel(part, tok, gains, mid, ents, recv_a, own, ent, send, recv, lsem):
    p = Place()
    barrier([p.at(dy=d) for d in (1, 2, 3)])
    cp = Copies(send, recv)
    load = pltpu.make_async_copy(part.at[p.y], own, lsem.at[0])
    load.start()
    ins = [cp.push(part.at[lax.rem(p.y + d, 4)], recv_a.at[d - 1], p.at(dy=d)) for d in (1, 3, 2)]
    load.wait()
    for c in ins:
        c.wait_recv()

    def block(i, _):
        r = pl.ds(pl.multiple_of(i * ROWS, ROWS), ROWS)
        f = jnp.float32
        m = tok[r].astype(f) + own[r].astype(f) + recv_a[0, r].astype(f) + recv_a[1, r].astype(f) + recv_a[2, r].astype(f)
        mid[r] = m
        m = m - jnp.mean(m, axis=-1, keepdims=True)
        m = m * lax.rsqrt(jnp.mean(m * m, axis=-1, keepdims=True) + norm_epsilon)
        ent[r] = (m * gains[0:1, :] + gains[1:2, :]).astype(jnp.bfloat16)
        return 0

    lax.fori_loop(0, 128 // ROWS, block, 0)
    keep = pltpu.make_async_copy(ent, ents.at[p.y], lsem.at[0])
    keep.start()
    outs = [cp.push(ent, ents.at[p.y], p.at(dy=d)) for d in (1, 3, 2)]
    keep.wait()
    for c in outs:
        c.wait_recv()
    cp.finish()


def middle_step(part, tok, gains):
    bf = jnp.bfloat16
    S = jax.ShapeDtypeStruct
    hbm, vm = pl.BlockSpec(memory_space=pl.ANY), pl.BlockSpec(memory_space=pltpu.VMEM)
    return pl.pallas_call(
        middle_kernel, out_shape=(S((128, 2048), jnp.float32), S((4, 128, 2048), bf)),
        in_specs=[hbm, vm, vm], out_specs=(vm, hbm),
        scratch_shapes=[pltpu.VMEM((3, 128, 2048), bf), pltpu.VMEM((128, 2048), bf), pltpu.VMEM((128, 2048), bf),
                        pltpu.SemaphoreType.DMA((6,)), pltpu.SemaphoreType.DMA((6,)), pltpu.SemaphoreType.DMA((1,))],
        compiler_params=pltpu.CompilerParams(collective_id=2, has_side_effects=True, vmem_limit_bytes=32 * 2**20),
        name="middle_step",
    )(part, tok, gains)


def back_kernel(gpart, rpart, mid, cot, gains, dg, du, dd,
                act, gmid, gmls, sums, og, ou, od,
                recv_g, recv_r, own_g, own_r, low, send, recv, lsem, *bufs):
    p = Place()
    f = jnp.float32
    barrier(peers(p))
    cp = Copies(send, recv)
    loads = [pltpu.make_async_copy(gpart.at[p.y], own_g, lsem.at[0]), pltpu.make_async_copy(rpart.at[p.y], own_r, lsem.at[1])]
    for load in loads:
        load.start()
    gs = [cp.push(gpart.at[lax.rem(p.y + d, 4)], recv_g.at[d - 1], p.at(dy=d)) for d in (1, 3, 2)]
    reduces = [Reduce(p, cp, dd, bufs[0:6], od, 96), Reduce(p, cp, dg, bufs[6:12], og), Reduce(p, cp, du, bufs[12:18], ou)]
    for i, r in enumerate(reduces):
        r.start(lsem.at[2 + i])
    for load in loads:
        load.wait()
    for c in gs:
        c.wait_recv()
    sums[...] = jnp.zeros_like(sums)

    def block(i, _):
        r = pl.ds(pl.multiple_of(i * ROWS, ROWS), ROWS)
        g = own_g[r].astype(f) + recv_g[0, r].astype(f) + recv_g[1, r].astype(f) + recv_g[2, r].astype(f)
        m = mid[r]
        m = m - jnp.mean(m, axis=-1, keepdims=True)
        inv = lax.rsqrt(jnp.mean(m * m, axis=-1, keepdims=True) + norm_epsilon)
        m = m * inv
        sums[0:1] += jnp.sum(g * m, axis=0, keepdims=True)
        sums[1:2] += jnp.sum(g, axis=0, keepdims=True)
        e = g * gains[0:1, :]
        out = cot[r].astype(f) + inv * (e - jnp.mean(e, axis=-1, keepdims=True) - m * jnp.mean(e * m, axis=-1, keepdims=True))
        gmid[r] = out
        low[r] = out.astype(jnp.bfloat16)
        return 0

    lax.fori_loop(0, 128 // ROWS, block, 0)
    keep = pltpu.make_async_copy(low, gmls.at[p.y], lsem.at[0])
    keep.start()
    ls = [cp.push(low, gmls.at[p.y], p.at(dy=d)) for d in (1, 3, 2)]
    rs = [cp.push(rpart.at[lax.rem(p.y + d, 4)], recv_r.at[d - 1], p.at(dy=d)) for d in (1, 3, 2)]
    run_reduces(reduces, lsem.at[pl.ds(5, 3)])
    for c in rs:
        c.wait_recv()

    def final(i, _):
        r = pl.ds(pl.multiple_of(i * ROWS, ROWS), ROWS)
        act[r] = (mid[r] + own_r[r].astype(f) + recv_r[0, r].astype(f) + recv_r[1, r].astype(f) + recv_r[2, r].astype(f)).astype(jnp.bfloat16)
        return 0

    lax.fori_loop(0, 128 // ROWS, final, 0)
    keep.wait()
    for c in ls:
        c.wait_recv()
    cp.finish()


def back_step(gpart, rpart, mid, cot, gains, dg, du, dd):
    bf = jnp.bfloat16
    S = jax.ShapeDtypeStruct
    hbm, vm = pl.BlockSpec(memory_space=pl.ANY), pl.BlockSpec(memory_space=pltpu.VMEM)
    return pl.pallas_call(
        back_kernel,
        out_shape=(S((128, 2048), bf), S((128, 2048), jnp.float32), S((4, 128, 2048), bf), S((8, 2048), jnp.float32),
                   S((4, 64, 1408), bf), S((4, 64, 1408), bf), S((176, 2048), bf)),
        in_specs=[hbm, hbm, vm, vm, vm, hbm, hbm, hbm], out_specs=(vm, vm, hbm, vm, hbm, hbm, hbm),
        scratch_shapes=[pltpu.VMEM((3, 128, 2048), bf), pltpu.VMEM((3, 128, 2048), bf), pltpu.VMEM((128, 2048), bf),
                        pltpu.VMEM((128, 2048), bf), pltpu.VMEM((128, 2048), bf),
                        pltpu.SemaphoreType.DMA((48,)), pltpu.SemaphoreType.DMA((48,)), pltpu.SemaphoreType.DMA((8,))]
        + reduce_scratch(dd.shape, True) + reduce_scratch(dg.shape, False) + reduce_scratch(du.shape, False),
        compiler_params=pltpu.CompilerParams(collective_id=3, has_side_effects=True, vmem_limit_bytes=56 * 2**20),
        name="back_step",
    )(gpart, rpart, mid, cot, gains, dg, du, dd)


def last_kernel(gpart, tok, gmid, gains, rows, dq, do,
                ing, oq, os, oo,
                recv_g, own_g, wide, small, send, recv, lsem, *bufs):
    p = Place()
    f = jnp.float32
    barrier(peers(p))
    cp = Copies(send, recv)
    load = pltpu.make_async_copy(gpart.at[p.y], own_g, lsem.at[0])
    load.start()
    gs = [cp.push(gpart.at[lax.rem(p.y + d, 4)], recv_g.at[d - 1], p.at(dy=d)) for d in (1, 3, 2)]
    rq = Reduce(p, cp, dq, bufs[0:6], oq)
    ro = Reduce(p, cp, do, bufs[6:12], oo, 32)
    rs = Reduce(p, cp, small, bufs[12:18], os)
    rq.start(lsem.at[1])
    ro.start(lsem.at[2])
    wide[...] = jnp.zeros_like(wide)
    wide[0:8] = rows[...]
    load.wait()
    for c in gs:
        c.wait_recv()

    def block(i, _):
        r = pl.ds(pl.multiple_of(i * ROWS, ROWS), ROWS)
        g = own_g[r].astype(f) + recv_g[0, r].astype(f) + recv_g[1, r].astype(f) + recv_g[2, r].astype(f)
        m = tok[r].astype(f)
        m = m - jnp.mean(m, axis=-1, keepdims=True)
        inv = lax.rsqrt(jnp.mean(m * m, axis=-1, keepdims=True) + norm_epsilon)
        m = m * inv
        wide[0:1] += jnp.sum(g * m, axis=0, keepdims=True)
        wide[1:2] += jnp.sum(g, axis=0, keepdims=True)
        e = g * gains[0:1, :]
        out = gmid[r] + inv * (e - jnp.mean(e, axis=-1, keepdims=True) - m * jnp.mean(e * m, axis=-1, keepdims=True))
        ing[r] = out.astype(jnp.bfloat16)
        return 0

    lax.fori_loop(0, 128 // ROWS, block, 0)
    for i in range(16):
        z, xl, y = i // 4, (i // 2) % 2, (i % 2) * 2
        piece = jnp.transpose(wide[:, i * 128:(i + 1) * 128]).astype(jnp.bfloat16)
        small[z, xl, y] = piece[0:64]
        small[z, xl, y + 1] = piece[64:128]
    rs.start(lsem.at[3])
    run_reduces([ro, rq, rs], lsem.at[pl.ds(4, 3)])
    cp.finish()


def last_step(gpart, tok, gmid, gains, rows, dq, do):
    bf = jnp.bfloat16
    S = jax.ShapeDtypeStruct
    hbm, vm = pl.BlockSpec(memory_space=pl.ANY), pl.BlockSpec(memory_space=pltpu.VMEM)
    return pl.pallas_call(
        last_kernel,
        out_shape=(S((128, 2048), bf), S((4, 64, 1536), bf), S((4, 64, 128), bf), S((64, 2048), bf)),
        in_specs=[hbm, vm, vm, vm, vm, hbm, hbm], out_specs=(vm, hbm, hbm, hbm),
        scratch_shapes=[pltpu.VMEM((3, 128, 2048), bf), pltpu.VMEM((128, 2048), bf), pltpu.VMEM((128, 2048), jnp.float32),
                        pltpu.VMEM((4, 2, 4, 64, 128), bf),
                        pltpu.SemaphoreType.DMA((48,)), pltpu.SemaphoreType.DMA((48,)), pltpu.SemaphoreType.DMA((8,))]
        + reduce_scratch(dq.shape, False) + reduce_scratch(do.shape, True) + reduce_scratch((4, 2, 4, 64, 128), False),
        compiler_params=pltpu.CompilerParams(collective_id=4, has_side_effects=True, vmem_limit_bytes=56 * 2**20),
        name="last_step",
    )(gpart, tok, gmid, gains, rows, dq, do)


norm_epsilon = 1e-05
masked_score = -1000000000.0
HEADS = 8
HEAD_DIM = 64
ROT = 16


def layout(segments):
    length = segments.shape[1]
    same = segments[:, :, None] == segments[:, None, :]
    query_index = lax.broadcasted_iota(jnp.int32, (length, length), 0)
    key_index = lax.broadcasted_iota(jnp.int32, (length, length), 1)
    allowed = same & (key_index <= query_index)[None]
    places = jnp.sum((same & (key_index < query_index)[None]).astype(jnp.int32), axis=-1).astype(jnp.float32)
    half_rot = ROT // 2
    freqs = 10000.0 ** (-(jnp.arange(half_rot, dtype=jnp.float32) * 2.0) / ROT)
    angles = places[:, :, None, None] * freqs
    return (allowed[:, None], jnp.cos(angles), jnp.sin(angles))


def rotate(values, cosine, sine):
    half_rot = ROT // 2
    first = values[..., :half_rot]
    second = values[..., half_rot:ROT]
    return jnp.concatenate(
        [first * cosine - second * sine, second * cosine + first * sine, values[..., ROT:]], axis=-1
    )


def local(tokens, segment_ids, cotangent, ln1_gain, ln1_bias, qkv_weight, qkv_bias, out_weight,
          ln2_gain, ln2_bias, gate_weight, up_weight, down_weight):
    f, bf = jnp.float32, jnp.bfloat16
    scale = HEAD_DIM ** (-0.5)
    y = lax.axis_index("y")
    wq = qkv_weight.reshape(64, 3, 8, 4, 64).transpose(3, 0, 1, 2, 4).reshape(4, 64, 1536)
    wg = gate_weight.reshape(64, 8, 4, 176).transpose(2, 0, 1, 3).reshape(4, 64, 1408)
    wu = up_weight.reshape(64, 8, 4, 176).transpose(2, 0, 1, 3).reshape(4, 64, 1408)
    small = jnp.concatenate([jnp.stack([ln1_gain, ln1_bias, ln2_gain, ln2_bias], axis=1), qkv_bias.reshape(3, 64).T,
                             jnp.zeros((64, 121), bf)], axis=1)
    small = jnp.broadcast_to(small[None], (4, 64, 128))
    seg = jnp.broadcast_to(segment_ids.astype(f), (8, 128))
    toks, cots, segs, gq, gs, gg, gu, go, gd = gather(tokens, cotangent, seg, wq, small, wg, wu, out_weight, down_weight)
    gq, gg, gu = gq.reshape(2048, 1536), gg.reshape(2048, 1408), gu.reshape(2048, 1408)
    go, gd = go.reshape(512, 2048), gd.reshape(1408, 2048)
    gs = gs.reshape(2048, 128)[:, :8].astype(f).T
    bias = gs[4:7].reshape(3, 32, 64).transpose(1, 0, 2).reshape(3, 8, 4, 64)
    bias = lax.dynamic_index_in_dim(bias, y, 2, False).reshape(1536)
    gains_two = jnp.concatenate([gs[2:4], jnp.zeros((6, 2048), f)])
    allowed, cosine, sine = layout(segs[:, 0, :])

    x = toks.reshape(512, 2048).astype(f)
    x = x - jnp.mean(x, axis=-1, keepdims=True)
    x = x * lax.rsqrt(jnp.mean(x * x, axis=-1, keepdims=True) + norm_epsilon)
    entry_one = (x * gs[0] + gs[1]).astype(bf)
    projected = jnp.dot(entry_one, gq, preferred_element_type=f) + bias
    projected = projected.reshape(4, 128, 3, HEADS, HEAD_DIM)
    queries = rotate(projected[:, :, 0], cosine, sine).astype(bf)
    keys = rotate(projected[:, :, 1], cosine, sine).astype(bf)
    values = projected[:, :, 2].astype(bf)
    scores = jnp.einsum("slhd,smhd->shlm", queries, keys, preferred_element_type=f) * scale
    scores = jnp.where(allowed, scores, masked_score)
    peak = jnp.max(scores, axis=-1, keepdims=True)
    expos = jnp.exp(scores - peak)
    probs = expos / jnp.sum(expos, axis=-1, keepdims=True)
    mixed = jnp.einsum("shlm,smhd->slhd", probs.astype(bf), values, preferred_element_type=f)
    mixed = mixed.reshape(512, 512).astype(bf)
    out_part = jnp.dot(mixed, go, preferred_element_type=f).astype(bf).reshape(4, 128, 2048)
    mid, ents = middle_step(out_part, tokens, gains_two)

    entry_two = ents.reshape(512, 2048)
    gate = jnp.dot(entry_two, gg, preferred_element_type=f)
    upward = jnp.dot(entry_two, gu, preferred_element_type=f)
    sigmoid = jax.nn.sigmoid(gate)
    hidden = (gate * sigmoid * upward).astype(bf)
    result_part = jnp.dot(hidden, gd, preferred_element_type=f).astype(bf).reshape(4, 128, 2048)
    cot = cots.reshape(512, 2048)
    dd = jnp.einsum("tf,td->fd", hidden, cot, preferred_element_type=f).astype(bf)
    grad_hidden = jnp.einsum("td,fd->tf", cot, gd, preferred_element_type=f).astype(bf).astype(f)
    grad_gate = (grad_hidden * upward * sigmoid * (1.0 + gate * (1.0 - sigmoid))).astype(bf)
    grad_up = (grad_hidden * gate * sigmoid).astype(bf)
    dg = jnp.einsum("td,tf->df", entry_two, grad_gate, preferred_element_type=f).astype(bf)
    du = jnp.einsum("td,tf->df", entry_two, grad_up, preferred_element_type=f).astype(bf)
    ge2 = jnp.einsum("tf,df->td", grad_gate, gg, preferred_element_type=f)
    ge2 = ge2 + jnp.einsum("tf,df->td", grad_up, gu, preferred_element_type=f)
    act, gmid, gmls, sums, og, ou, od = back_step(
        ge2.astype(bf).reshape(4, 128, 2048), result_part, mid, cotangent, gains_two,
        dg.reshape(4, 2, 4, 64, 1408), du.reshape(4, 2, 4, 64, 1408), dd.reshape(4, 2, 176, 2048))

    gml = gmls.reshape(512, 2048)
    do = jnp.einsum("td,te->de", mixed, gml, preferred_element_type=f).astype(bf)
    grad_mixed = jnp.einsum("te,de->td", gml, go, preferred_element_type=f).astype(bf).reshape(4, 128, HEADS, HEAD_DIM)
    grad_values = jnp.einsum("shlm,slhd->smhd", probs.astype(bf), grad_mixed, preferred_element_type=f)
    grad_probs = jnp.einsum("slhd,smhd->shlm", grad_mixed, values, preferred_element_type=f)
    grad_scores = (probs * (grad_probs - jnp.sum(probs * grad_probs, axis=-1, keepdims=True))).astype(bf)
    grad_queries = jnp.einsum("shlm,smhd->slhd", grad_scores, keys, preferred_element_type=f) * scale
    grad_keys = jnp.einsum("shlm,slhd->smhd", grad_scores, queries, preferred_element_type=f) * scale
    grad_queries = rotate(grad_queries, cosine, -sine)
    grad_keys = rotate(grad_keys, cosine, -sine)
    grad_projected = jnp.stack([grad_queries, grad_keys, grad_values], axis=2).reshape(512, 1536).astype(bf)
    bias_grad = jnp.sum(grad_projected.astype(f), axis=0).reshape(3, 8, 1, 64)
    here = (lax.broadcasted_iota(jnp.int32, (3, 8, 4, 64), 2) == y).astype(f)
    bias_grad = (bias_grad * here).reshape(32, 3, 64).transpose(1, 0, 2).reshape(3, 2048)
    dq = jnp.einsum("td,te->de", entry_one, grad_projected, preferred_element_type=f).astype(bf)
    ge1 = jnp.einsum("te,de->td", grad_projected, gq, preferred_element_type=f).astype(bf).reshape(4, 128, 2048)
    zero = jnp.zeros((2, 2048), f)
    rows = jnp.concatenate([zero, sums[0:2], bias_grad, zero[:1]])
    gains_one = jnp.concatenate([gs[0:2], jnp.zeros((6, 2048), f)])
    ing, oq, os, oo = last_step(ge1, tokens, gmid, gains_one, rows, dq.reshape(4, 2, 4, 64, 1536), do.reshape(4, 2, 64, 2048))

    os = jnp.sum(os[:, :, :8].astype(f), axis=0)
    qkv_grad = oq.reshape(4, 64, 3, 8, 64).transpose(1, 2, 3, 0, 4).reshape(64, 6144).astype(f)
    gate_grad = og.reshape(4, 64, 8, 176).transpose(1, 2, 0, 3).reshape(64, 5632).astype(f)
    up_grad = ou.reshape(4, 64, 8, 176).transpose(1, 2, 0, 3).reshape(64, 5632).astype(f)
    return (act, ing, os[:, 0], os[:, 1], qkv_grad, os[:, 4:7].T.reshape(192), oo.astype(f),
            os[:, 2], os[:, 3], gate_grad, up_grad, od.astype(f))


def solution(mesh):
    fine = Mesh(mesh.devices.reshape(2, 2, 4, 2, 4), AXES)
    whole, rows = P(AXES, None), P(("z", "xl", "y"), None)
    vector = P(("z", "xl", "y"))
    return jax.shard_map(
        local, mesh=fine,
        in_specs=(whole, whole, whole, vector, vector, rows, vector, rows, vector, vector, rows, rows, rows),
        out_specs=(whole, whole, vector, vector, rows, vector, rows, vector, vector, rows, rows, rows),
        check_vma=False,
    )
```

```python
import functools
import jax, jax.numpy as jnp
from jax import lax
from jax.sharding import PartitionSpec as P, Mesh
from jax.experimental import pallas as pl
from jax.experimental.pallas import tpu as pltpu

AXES = ("xh", "c", "z", "xl", "y")


class Place:
    def __init__(self):
        self.xh, self.c, self.z, self.xl, self.y = (lax.axis_index(a) for a in AXES)
        self.x = self.xh * 2 + self.xl

    def at(self, dx=0, dy=0, dz=0, dc=0):
        x = lax.rem(self.x + dx + 4, 4) if dx else self.x
        return (
            x // 2 if dx else self.xh,
            lax.rem(self.c + dc, 2) if dc else self.c,
            lax.rem(self.z + dz + 4, 4) if dz else self.z,
            lax.rem(x, 2) if dx else self.xl,
            lax.rem(self.y + dy + 4, 4) if dy else self.y,
        )


def barrier(targets):
    sem = pltpu.get_barrier_semaphore()
    for target in targets:
        pl.semaphore_signal(sem, inc=1, device_id=target, device_id_type=pl.DeviceIdType.MESH)
    pl.semaphore_wait(sem, len(targets))


class Copies:
    def __init__(self, send, recv):
        self.send, self.recv, self.used, self.all = send, recv, 0, []

    def push(self, src, dst, target):
        copy = pltpu.make_async_remote_copy(
            src_ref=src, dst_ref=dst, send_sem=self.send.at[self.used],
            recv_sem=self.recv.at[self.used], device_id=target, device_id_type=pl.DeviceIdType.MESH)
        self.used += 1
        self.all.append(copy)
        copy.start()
        return copy

    def finish(self):
        for copy in self.all:
            copy.wait_send()


def add_into(out, parts):
    total = parts[0][...].astype(jnp.float32)
    for part in parts[1:]:
        total = total + part[...].astype(jnp.float32)
    out[...] = total.astype(out.dtype)


def peers(p):
    return [p.at(dy=d) for d in (1, 2, 3)] + [p.at(dz=d) for d in (1, 2, 3)] + [p.at(dx=d) for d in (1, 2, -1)] + [p.at(dc=1)]


class Gather:
    def __init__(self, p, cp, src, dst, lsem, cols=None, cut=None):
        self.p, self.cp, self.src, self.dst, self.lsem, self.cut = p, cp, src, dst, lsem, cut
        self.cols = cols
        if cut is None:
            self.half = pl.ds(pl.multiple_of(p.c * 32, 32), 32)
        else:
            self.half = pl.ds(pl.multiple_of(p.c * 1024, 1024), 1024)

    def start(self):
        p, src, dst, half = self.p, self.src, self.dst, self.half
        if self.cut is None:
            cols = self.cols
            here = dst.at[p.z, p.xl, p.y, half, cols]
            self.local = pltpu.make_async_copy(src.at[p.y, half, cols], here, self.lsem)
            self.local.start()
            self.ys = [self.cp.push(src.at[lax.rem(p.y + d, 4), half, cols], here, p.at(dy=d)) for d in (1, 3, 2)]
        else:
            here = dst.at[p.z, p.xl, :, half]
            self.local = pltpu.make_async_copy(src.at[:, half], here, self.lsem)
            self.local.start()
            self.zs = [self.cp.push(src.at[:, half], here, p.at(dz=d)) for d in (1, 3, 2)]

    def stage_z(self):
        p = self.p
        self.local.wait()
        for c in self.ys:
            c.wait_recv()
        here = self.dst.at[p.z, p.xl, :, self.half, self.cols]
        self.zs = [self.cp.push(here, here, p.at(dz=d)) for d in (1, 3, 2)]

    def parts(self, xl):
        g = self.dst
        if self.cut is not None:
            k, r = self.cut, g.shape[2]
            return g.at[:, xl, 0:k, self.half], g.at[:, xl, k:r, self.half], g.at[:, xl, :, self.half]
        return (g.at[:, xl, 0:2, self.half, self.cols], g.at[:, xl, 2:4, self.half, self.cols],
                g.at[:, xl, :, self.half, self.cols])

    def stage_x(self):
        p = self.p
        if self.cut is not None:
            self.local.wait()
        for c in self.zs:
            c.wait_recv()
        lo, hi, full = self.parts(p.xl)
        self.xs = [self.cp.push(lo, lo, p.at(dx=1)), self.cp.push(hi, hi, p.at(dx=-1))]
        self.cs = [self.cp.push(full, full, p.at(dc=1))]

    def stage_c(self):
        p = self.p
        lo, hi, full = self.parts(1 - p.xl)
        self.xs[0].wait_recv()
        self.cs.append(self.cp.push(lo, lo, p.at(dc=1)))
        self.xs[1].wait_recv()
        self.cs.append(self.cp.push(hi, hi, p.at(dc=1)))

    def finish(self):
        for c in self.cs:
            c.wait_recv()


ROWS = 16
norm_epsilon = 1e-05
masked_score = -1000000000.0
HEADS = 8
HEAD_DIM = 64
ROT = 16
SCALE = HEAD_DIM ** (-0.5)


def norm_rows(m):
    m = m - jnp.mean(m, axis=-1, keepdims=True)
    inv = lax.rsqrt(jnp.mean(m * m, axis=-1, keepdims=True) + norm_epsilon)
    return m * inv, inv


def allowed_of(seg_row):
    keys = jnp.broadcast_to(seg_row, (128, 128))
    queries = jnp.transpose(keys)
    q = lax.broadcasted_iota(jnp.int32, (128, 128), 0)
    k = lax.broadcasted_iota(jnp.int32, (128, 128), 1)
    same = keys == queries
    places = jnp.sum(jnp.where(same & (k < q), 1.0, 0.0), axis=-1, keepdims=True)
    return same & (k <= q), places


def turn(x, cosine, sine):
    lane = lax.broadcasted_iota(jnp.int32, (128, 128), 1)
    other = jnp.where(lax.rem(lane, 64) < 8, pltpu.roll(x, 120, 1), pltpu.roll(x, 8, 1))
    return x * cosine + other * sine


def stack_heads(x):
    lane = lax.broadcasted_iota(jnp.int32, (128, 128), 1)
    zero = jnp.zeros_like(x)
    return jnp.concatenate([jnp.where(lane < 64, x, zero), jnp.where(lane < 64, zero, x)], axis=0)


def merge_heads(x):
    lane = lax.broadcasted_iota(jnp.int32, (128, 128), 1)
    return jnp.where(lane < 64, x[:128], x[128:])


def dot_nt(a, b):
    return lax.dot_general(a, b, (((1,), (1,)), ((), ())), preferred_element_type=jnp.float32)


def dot_tn(a, b):
    return lax.dot_general(a, b, (((0,), (0,)), ((), ())), preferred_element_type=jnp.float32)


def first_kernel(tok, cot, seg, wq, sm, wgu, wo, wd, freqs,
                 cots, gq, ggu, go, gd, e1, qkv, prb, mix, tab, gains, mid, ents,
                 vq, vs, vo, x, segs, proj, qkvb, probs, mixed, tabs, part, recv_a, own, ent, bias,
                 send, recv, lsem):
    p = Place()
    f, bf = jnp.float32, jnp.bfloat16
    barrier([p.at(dy=d) for d in (1, 2, 3)] + [p.at(dz=d) for d in (1, 2, 3)] + [p.at(dx=1), p.at(dx=-1), p.at(dc=1)])
    cp = Copies(send, recv)
    locals_ = []

    def local(src, dst):
        copy = pltpu.make_async_copy(src, dst, lsem.at[len(locals_)])
        copy.start()
        locals_.append(copy)
        return copy

    def sem():
        locals_.append(None)
        return lsem.at[len(locals_) - 1]

    def share(src, dst):
        return [local(src, dst.at[p.y])], [cp.push(src, dst.at[p.y], p.at(dy=d)) for d in (1, 3, 2)]

    q0 = Gather(p, cp, wq, vq, sem(), cols=pl.ds(0, 768))
    q1 = Gather(p, cp, wq, vq, sem(), cols=pl.ds(768, 768))
    s = Gather(p, cp, sm, vs, sem(), cols=pl.ds(0, 256))
    u0 = Gather(p, cp, wgu, ggu, sem(), cols=pl.ds(0, 1408))
    u1 = Gather(p, cp, wgu, ggu, sem(), cols=pl.ds(1408, 1408))
    o = Gather(p, cp, wo, vo, sem(), cut=32)
    d = Gather(p, cp, wd, gd, sem(), cut=96)

    s.start(); q0.start(); q1.start(); o.start()
    own_load = local(tok, own)
    x_here, x_in = share(tok, x)
    s_here, s_in = share(seg, segs)
    s.stage_z(); q0.stage_z(); q1.stage_z()
    u0.start(); u1.start()
    for c in s_here:
        c.wait()
    for c in s_in:
        c.wait_recv()

    lane = lax.broadcasted_iota(jnp.int32, (128, 128), 1)
    low = lax.rem(lane, 64)

    def table(i, _):
        _, places = allowed_of(segs[i, 0:1, :])
        angle = places * freqs[0:1, :]
        tabs[i, 0] = jnp.where(low < ROT, jnp.cos(angle), 1.0)
        sine = jnp.sin(angle)
        tabs[i, 1] = jnp.where(low < ROT // 2, -sine, jnp.where(low < ROT, sine, 0.0))
        return 0

    lax.fori_loop(0, 4, table, 0)
    local(tabs, tab)
    s.stage_x(); q0.stage_x(); q1.stage_x(); o.stage_x()
    d.start()
    s.stage_c()
    u0.stage_z(); u1.stage_z()
    c_here, c_in = share(cot, cots)
    s.finish()

    for i in range(16):
        z, xl, y = i // 4, (i // 2) % 2, (i % 2) * 2
        piece = jnp.concatenate([vs[z, xl, y, :, 0:128], vs[z, xl, y + 1, :, 0:128]], axis=0)
        gains[:, i * 128:(i + 1) * 128] = jnp.transpose(piece.astype(f))[0:8]
    total = jnp.zeros((16, 128), f)
    for i in range(32):
        total = total + vs[i // 8, (i // 4) % 2, i % 4, 0:16, 128:256].astype(f)
    bias[...] = total

    def entry(i, block_in):
        def block(b, _):
            r = pl.ds(pl.multiple_of(b * ROWS, ROWS), ROWS)
            n, _inv = norm_rows(x[i, r].astype(f))
            x[i, r] = (n * gains[0:1, :] + gains[1:2, :]).astype(bf)
            return 0
        lax.fori_loop(0, 128 // ROWS, block, 0)
        return 0

    for c in x_here:
        c.wait()
    for c in x_in:
        c.wait_recv()
    lax.fori_loop(0, 4, entry, 0)
    local(x, e1)
    q0.stage_c(); q1.stage_c(); o.stage_c()
    q0.finish(); q1.finish()
    local(vq, gq)

    def project(n, _):
        cols = pl.ds(pl.multiple_of(n * 512, 512), 512)
        w = vq[:, :, :, :, cols].reshape(2048, 512)
        out = jnp.dot(x[...].reshape(512, 2048), w, preferred_element_type=f)
        b = jnp.concatenate([bias[pl.ds(n * 4 + k, 1), :] for k in range(4)], axis=1)
        proj[:, :, cols] = (out + b).reshape(4, 128, 512)
        return 0

    lax.fori_loop(0, 3, project, 0)
    d.stage_x(); u0.stage_x()

    def attend(i, _):
        allowed, _places = allowed_of(segs[i, 0:1, :])
        allowed = jnp.concatenate([allowed, allowed], axis=0)
        cosine, sine = tabs[i, 0], tabs[i, 1]

        def pair(n, _):
            a, b, c = (pl.ds(pl.multiple_of(n * 128 + k * 512, 128), 128) for k in range(3))
            q = turn(proj[i, :, a], cosine, sine).astype(bf)
            k = turn(proj[i, :, b], cosine, sine).astype(bf)
            v = proj[i, :, c].astype(bf)
            qkvb[i, :, a] = q
            qkvb[i, :, b] = k
            qkvb[i, :, c] = v
            scores = dot_nt(stack_heads(q), k) * SCALE
            scores = jnp.where(allowed, scores, masked_score)
            expos = jnp.exp(scores - jnp.max(scores, axis=-1, keepdims=True))
            prob = expos / jnp.sum(expos, axis=-1, keepdims=True)
            probs[i, n] = prob
            got = jnp.dot(prob.astype(bf), v, preferred_element_type=f)
            mixed[i, :, a] = merge_heads(got).astype(bf)
            return 0

        lax.fori_loop(0, 4, pair, 0)
        return 0

    lax.fori_loop(0, 4, attend, 0)
    local(qkvb, qkv); local(probs, prb); local(mixed, mix)
    u1.stage_x()
    o.finish()
    local(vo, go)
    ins = []
    for n in range(4):
        cols = pl.ds(n * 512, 512)
        out = jnp.dot(mixed[...].reshape(512, 512), vo[:, :, :, cols].reshape(512, 512), preferred_element_type=f)
        part[:, :, cols] = out.astype(bf).reshape(4, 128, 512)
        ins += [cp.push(part.at[lax.rem(p.y + k, 4), :, cols], recv_a.at[k - 1, :, cols], p.at(dy=k)) for k in (1, 3, 2)]
    d.stage_c(); u0.stage_c()
    own_load.wait()
    for c in ins:
        c.wait_recv()

    def block(i, _):
        r = pl.ds(pl.multiple_of(i * ROWS, ROWS), ROWS)
        m = own[r].astype(f) + part[p.y, r].astype(f) + recv_a[0, r].astype(f) + recv_a[1, r].astype(f) + recv_a[2, r].astype(f)
        mid[r] = m
        n, _inv = norm_rows(m)
        ent[r] = (n * gains[2:3, :] + gains[3:4, :]).astype(bf)
        return 0

    lax.fori_loop(0, 128 // ROWS, block, 0)
    e_here, e_in = share(ent, ents)
    u1.stage_c()
    for c in c_in + e_in:
        c.wait_recv()
    for g in (o, d, u0, u1):
        if g is not o:
            g.finish()
    cp.finish()
    for copy in locals_:
        if copy is not None and not any(copy is done for done in x_here + s_here + [own_load]):
            copy.wait()


def first_step(tok, cot, seg, wq, sm, wgu, wo, wd, freqs):
    f, bf = jnp.float32, jnp.bfloat16
    S = jax.ShapeDtypeStruct
    hbm, vm = pl.BlockSpec(memory_space=pl.ANY), pl.BlockSpec(memory_space=pltpu.VMEM)
    outs = (S((4, 128, 2048), bf), S((4, 2, 4, 64, 1536), bf), S((4, 2, 4, 64, 2816), bf), S((4, 2, 64, 2048), bf),
            S((4, 2, 176, 2048), bf), S((4, 128, 2048), bf), S((4, 128, 1536), bf), S((4, 4, 256, 128), f),
            S((4, 128, 512), bf), S((4, 2, 128, 128), f), S((8, 2048), f), S((128, 2048), f), S((4, 128, 2048), bf))
    return pl.pallas_call(
        first_kernel, out_shape=outs, in_specs=[hbm] * 8 + [vm],
        out_specs=(hbm,) * 10 + (vm, vm, hbm),
        scratch_shapes=[
            pltpu.VMEM((4, 2, 4, 64, 1536), bf), pltpu.VMEM((4, 2, 4, 64, 256), bf), pltpu.VMEM((4, 2, 64, 2048), bf),
            pltpu.VMEM((4, 128, 2048), bf), pltpu.VMEM((4, 8, 128), f), pltpu.VMEM((4, 128, 1536), f),
            pltpu.VMEM((4, 128, 1536), bf), pltpu.VMEM((4, 4, 256, 128), f), pltpu.VMEM((4, 128, 512), bf),
            pltpu.VMEM((4, 2, 128, 128), f), pltpu.VMEM((4, 128, 2048), bf), pltpu.VMEM((3, 128, 2048), bf),
            pltpu.VMEM((128, 2048), bf), pltpu.VMEM((128, 2048), bf), pltpu.VMEM((16, 128), f),
            pltpu.SemaphoreType.DMA((104,)), pltpu.SemaphoreType.DMA((104,)), pltpu.SemaphoreType.DMA((24,))],
        compiler_params=pltpu.CompilerParams(collective_id=1, has_side_effects=True, vmem_limit_bytes=48 * 2**20),
        name="first_step",
    )(tok, cot, seg, wq, sm, wgu, wo, wd, freqs)


class Sum:
    def __init__(self, p, cp, parts, rc, rx, rz, cut):
        self.p, self.cp, self.parts, self.rc, self.rx, self.rz, self.cut = p, cp, parts, rc, rx, rz, cut

    def start(self):
        self.core = self.cp.push(self.parts.at[1 - self.p.c], self.rc, self.p.at(dc=1))

    def stage_x(self):
        p, rc, k = self.p, self.rc, self.cut
        h = self.parts.at[p.c]
        self.core.wait_recv()

        def foreign(i, _):
            add_into(h.at[i, 1 - p.xl], (h.at[i, 1 - p.xl], rc.at[i, 1 - p.xl]))
            return 0

        lax.fori_loop(0, 4, foreign, 0)
        n = h.shape[2]
        self.xs = [
            self.cp.push(h.at[:, 1 - p.xl, 0:k], self.rx.at[:, 0:k], p.at(dx=1)),
            self.cp.push(h.at[:, 1 - p.xl, k:n], self.rx.at[:, k:n], p.at(dx=-1)),
        ]

    def stage_own(self):
        p, rc, rx = self.p, self.rc, self.rx
        h = self.parts.at[p.c]
        for c in self.xs:
            c.wait_recv()

        def own(i, _):
            add_into(h.at[i, p.xl], (h.at[i, p.xl], rc.at[i, p.xl], rx.at[i]))
            return 0

        lax.fori_loop(0, 4, own, 0)

    def stage_z(self):
        p = self.p
        h = self.parts.at[p.c]
        self.stage_own()
        self.zs = [self.cp.push(h.at[lax.rem(p.z + d, 4), p.xl], self.rz.at[d - 1], p.at(dz=d)) for d in (1, 3, 2)]

    def stage_sum(self):
        p, rz = self.p, self.rz
        here = self.parts.at[p.c, p.z, p.xl]
        for c in self.zs:
            c.wait_recv()
        add_into(here, (here, rz.at[0], rz.at[1], rz.at[2]))
        return here


def second_kernel(ggu, gd, ents, cots, mid, cot, gains,
                  rpart, gmid, gmls, sums, jd, j0, i1,
                  vgu, vd, ent, cts, hid, dgu, gpart, recv_g, low, dd, d0, d1, rcd, rxd, rzd, rx0, rz0, rx1,
                  send, recv, lsem, ready):
    p = Place()
    f, bf = jnp.float32, jnp.bfloat16
    sib = p.at(dc=1)
    loads = [(ents, ent), (cots, cts)]
    loads += [(gd, vd)]
    for n in range(6):
        cols = pl.ds(n * 512, 512 if n < 5 else 256)
        loads.append((ggu.at[:, :, :, :, cols], vgu.at[:, :, :, :, cols]))
    loads = [pltpu.make_async_copy(a, b, lsem.at[i]) for i, (a, b) in enumerate(loads)]
    for c in loads:
        c.start()
    barrier([p.at(dy=d) for d in (1, 2, 3)] + [p.at(dz=d) for d in (1, 2, 3)] + [p.at(dx=1), p.at(dx=-1), sib])
    cp = Copies(send, recv)
    for c in loads[:3]:
        c.wait()

    def hidden_tile(first, width):
        w = vgu[:, :, :, :, pl.ds(2 * first, 2 * width)].reshape(2048, 2 * width)
        gu = jnp.dot(ent[...].reshape(512, 2048), w, preferred_element_type=f)
        gh = dot_nt(cts[...].reshape(512, 2048), vd[pl.ds(first, width), :]).astype(bf).astype(f)
        for k in range(width // 128):
            gate, up = gu[:, k * 256:k * 256 + 128], gu[:, k * 256 + 128:k * 256 + 256]
            g = gh[:, k * 128:(k + 1) * 128]
            sig = 1.0 / (1.0 + jnp.exp(-gate))
            silu = gate * sig
            hid[:, pl.ds(first + k * 128, 128)] = (silu * up).astype(bf)
            dgu[:, pl.ds(2 * first + k * 256, 128)] = (g * up * sig * (1.0 + gate * (1.0 - sig))).astype(bf)
            dgu[:, pl.ds(2 * first + k * 256 + 128, 128)] = (g * silu).astype(bf)

    def tile(n, _):
        cols = pl.ds(pl.multiple_of(n * 512, 512), 512)
        pltpu.make_async_copy(ggu.at[:, :, :, :, cols], vgu.at[:, :, :, :, cols], lsem.at[3 + n]).wait()
        hidden_tile(pl.multiple_of(n * 256, 256), 256)
        return 0

    lax.fori_loop(0, 5, tile, 0)
    loads[8].wait()
    hidden_tile(1280, 128)

    gs = []
    for n in range(4):
        out = dot_nt(dgu[...], vgu[n].reshape(512, 2816))
        cols = pl.ds(n * 512, 512)
        gpart[:, :, cols] = out.astype(bf).reshape(4, 128, 512)
        gs += [cp.push(gpart.at[lax.rem(p.y + k, 4), :, cols], recv_g.at[k - 1, :, cols], p.at(dy=k)) for k in (1, 3, 2)]
    pl.semaphore_signal(ready, inc=1, device_id=sib, device_id_type=pl.DeviceIdType.MESH)

    def down_tile(t, _):
        rows = pl.ds(pl.multiple_of(t * 128, 128), 128)
        for h in range(2):
            out = dot_tn(hid[:, rows], cts[:, :, h * 1024:(h + 1) * 1024].reshape(512, 1024)).astype(bf)
            for k in range(8):
                g = t * 8 + k
                dd[h, g // 22, lax.rem(g // 11, 2), lax.rem(g, 11)] = out[k * 16:(k + 1) * 16]
        return 0

    lax.fori_loop(0, 11, down_tile, 0)
    sd = Sum(p, cp, dd, rcd, rxd, rzd, 6)
    s0 = Sum(p, cp, d0, vgu.at[:, :, :, 0:32, 0:1408], rx0, rz0, 2)
    s1 = Sum(p, cp, d1, vgu.at[:, :, :, 0:32, 1408:2816], rx1, None, 2)
    sd.start()
    pl.semaphore_wait(ready, 1)

    def up_tile(first, d):
        def body(i, _):
            rows = pl.ds(pl.multiple_of(i * 256, 256), 256)
            out = dot_tn(ent[:, :, rows].reshape(512, 256), dgu[:, first:first + 1408]).astype(bf).reshape(4, 2, 32, 1408)
            d[0, i // 2, lax.rem(i, 2)] = out[:, 0]
            d[1, i // 2, lax.rem(i, 2)] = out[:, 1]
            return 0
        lax.fori_loop(0, 8, body, 0)

    up_tile(0, d0)
    s0.start()
    sd.stage_x()
    up_tile(1408, d1)
    s1.start()
    for c in gs:
        c.wait_recv()
    sums[...] = jnp.zeros_like(sums)

    def block(i, _):
        r = pl.ds(pl.multiple_of(i * ROWS, ROWS), ROWS)
        g = gpart[p.y, r].astype(f) + recv_g[0, r].astype(f) + recv_g[1, r].astype(f) + recv_g[2, r].astype(f)
        m, inv = norm_rows(mid[r])
        sums[0:1] += jnp.sum(g * m, axis=0, keepdims=True)
        sums[1:2] += jnp.sum(g, axis=0, keepdims=True)
        e = g * gains[2:3, :]
        out = cot[r].astype(f) + inv * (e - jnp.mean(e, axis=-1, keepdims=True) - m * jnp.mean(e * m, axis=-1, keepdims=True))
        gmid[r] = out
        low[r] = out.astype(bf)
        return 0

    lax.fori_loop(0, 128 // ROWS, block, 0)
    keep = pltpu.make_async_copy(low, gmls.at[p.y], lsem.at[0])
    keep.start()
    ls = [cp.push(low, gmls.at[p.y], p.at(dy=d)) for d in (1, 3, 2)]
    s0.stage_x()
    sd.stage_z()
    s1.stage_x()

    def result(n, _):
        cols = pl.ds(pl.multiple_of(n * 512, 512), 512)
        out = jnp.dot(hid[...], vd[:, cols], preferred_element_type=f)
        ent[:, :, cols] = out.astype(bf).reshape(4, 128, 512)
        return 0

    lax.fori_loop(0, 4, result, 0)
    keeps = [pltpu.make_async_copy(ent, rpart, lsem.at[1])]
    keeps[0].start()
    s0.stage_z()
    here = sd.stage_sum()
    keeps.append(pltpu.make_async_copy(here, jd, lsem.at[2]))
    keeps[-1].start()
    s1.stage_own()
    keeps.append(pltpu.make_async_copy(d1.at[p.c, :, p.xl], i1, lsem.at[3]))
    keeps[-1].start()
    here = s0.stage_sum()
    keeps.append(pltpu.make_async_copy(here, j0, lsem.at[4]))
    keeps[-1].start()
    for c in ls:
        c.wait_recv()
    cp.finish()
    keep.wait()
    for c in keeps:
        c.wait()


def second_step(ggu, gd, ents, cots, mid, cot, gains):
    f, bf = jnp.float32, jnp.bfloat16
    S = jax.ShapeDtypeStruct
    hbm, vm = pl.BlockSpec(memory_space=pl.ANY), pl.BlockSpec(memory_space=pltpu.VMEM)
    V = pltpu.VMEM
    return pl.pallas_call(
        second_kernel,
        out_shape=(S((4, 128, 2048), bf), S((128, 2048), f), S((4, 128, 2048), bf), S((8, 2048), f),
                   S((11, 16, 1024), bf), S((4, 32, 1408), bf), S((4, 4, 32, 1408), bf)),
        in_specs=[hbm, hbm, hbm, hbm, vm, vm, vm], out_specs=(hbm, vm, hbm, vm, hbm, hbm, hbm),
        scratch_shapes=[
            V((4, 2, 4, 64, 2816), bf), V((1408, 2048), bf), V((4, 128, 2048), bf), V((4, 128, 2048), bf),
            V((512, 1408), bf), V((512, 2816), bf), V((4, 128, 2048), bf), V((3, 128, 2048), bf), V((128, 2048), bf),
            V((2, 4, 2, 11, 16, 1024), bf), V((2, 4, 2, 4, 32, 1408), bf), V((2, 4, 2, 4, 32, 1408), bf),
            V((4, 2, 11, 16, 1024), bf), V((4, 11, 16, 1024), bf), V((3, 11, 16, 1024), bf),
            V((4, 4, 32, 1408), bf), V((3, 4, 32, 1408), bf), V((4, 4, 32, 1408), bf),
            pltpu.SemaphoreType.DMA((40,)), pltpu.SemaphoreType.DMA((40,)), pltpu.SemaphoreType.DMA((12,)),
            pltpu.SemaphoreType.REGULAR],
        compiler_params=pltpu.CompilerParams(collective_id=3, has_side_effects=True, vmem_limit_bytes=63 * 2**20),
        name="second_step",
    )(ggu, gd, ents, cots, mid, cot, gains)


class Finish:
    def __init__(self, p, cp, here, rxh, total, out, lsem, plane):
        self.p, self.cp, self.here, self.rxh, self.total, self.out, self.lsem, self.plane = p, cp, here, rxh, total, out, lsem, plane

    def stage_xh(self):
        self.xh = self.cp.push(self.here, self.rxh, self.p.at(dx=2))

    def stage_y(self):
        p, cp, out = self.p, self.cp, self.out
        self.xh.wait_recv()
        add_into(self.total, (self.here, self.rxh))
        if self.plane:
            there = out.at[..., pl.ds(pl.multiple_of(p.c * 1024, 1024), 1024)]
            self.own = pltpu.make_async_copy(self.total, there, self.lsem)
            self.own.start()
            self.ys = [cp.push(self.total, there, p.at(dc=1))]
        else:
            half = pl.ds(pl.multiple_of(p.c * 32, 32), 32)
            self.own = pltpu.make_async_copy(self.total.at[p.y], out.at[p.y, half], self.lsem)
            self.own.start()
            self.ys = [cp.push(self.total.at[lax.rem(p.y + d, 4)], out.at[p.y, half], p.at(dy=d)) for d in (1, 3, 2)]

    def stage_c(self):
        p, out = self.p, self.out
        for c in self.ys:
            c.wait_recv()
        self.own.wait()
        self.last = []
        if not self.plane:
            half = pl.ds(pl.multiple_of(p.c * 32, 32), 32)
            self.last = [self.cp.push(out.at[:, half], out.at[:, half], p.at(dc=1))]

    def finish(self):
        for c in self.last:
            c.wait_recv()


def third_kernel(gmls, go, gq, e1, qkv, prb, mix, tab, rpart, mid, tok, gmid, gains, sums, jd, j0, i1,
                 act, ing, od, o0, o1, oq, oo, os,
                 vgml, vo, vq, ve, vqkv, vprb, vmix, vtab, vgm, gp, gpart, recv_g, recv_r, own_r, wide,
                 vjd, rxd, td, vj0, rx0, t0, vi1, rz1, rx1, t1,
                 dq, rcq, rxq, rzq, rxhq, tq, dw, rco, rxo, rzo, rxho, to, ds, rcs, rxs, rzs, rxhs, ts,
                 send, recv, lsem):
    p = Place()
    f, bf = jnp.float32, jnp.bfloat16
    pairs_in = [(gmls, vgml), (go, vo), (mix, vmix), (qkv, vqkv), (prb, vprb), (tab, vtab), (e1, ve), (gq, vq),
                (jd, vjd), (j0, vj0), (i1, vi1), (rpart.at[p.y], own_r)]
    loads = [pltpu.make_async_copy(a, b, lsem.at[i]) for i, (a, b) in enumerate(pairs_in)]
    for c in loads:
        c.start()
    barrier(peers(p))
    cp = Copies(send, recv)
    for c in loads[8:11]:
        c.wait()
    fd = Finish(p, cp, vjd, rxd, td, od, lsem.at[12], True)
    f0 = Finish(p, cp, vj0, rx0, t0, o0, lsem.at[13], False)
    fd.stage_xh()
    f0.stage_xh()
    zs = [cp.push(vi1.at[lax.rem(p.z + d, 4)], rz1.at[d - 1], p.at(dz=d)) for d in (1, 3, 2)]
    rs = [cp.push(rpart.at[lax.rem(p.y + d, 4)], recv_r.at[d - 1], p.at(dy=d)) for d in (1, 3, 2)]
    for c in loads[0:8] + loads[11:]:
        c.wait()

    vgm[...] = dot_nt(vgml[...].reshape(512, 2048), vo[...].reshape(512, 2048)).astype(bf).reshape(4, 128, 512)

    def out_tile(h, _):
        cols = pl.ds(pl.multiple_of(h * 512, 512), 512)
        out = dot_tn(vmix[...].reshape(512, 512), vgml[:, :, cols].reshape(512, 512)).astype(bf)
        dw[h // 2, :, :, :, pl.ds(pl.multiple_of(lax.rem(h, 2) * 512, 512), 512)] = out.reshape(4, 2, 64, 512)
        return 0

    lax.fori_loop(0, 4, out_tile, 0)
    so = Sum(p, cp, dw, rco, rxo, rzo, 32)
    so.start()

    def attend(i, _):
        cosine, sine = vtab[i, 0], -vtab[i, 1]

        def pair(n, _):
            a, b, c = (pl.ds(pl.multiple_of(n * 128 + k * 512, 128), 128) for k in range(3))
            q, k, v = vqkv[i, :, a], vqkv[i, :, b], vqkv[i, :, c]
            prob = vprb[i, n]
            g = stack_heads(vgm[i, :, a])
            gv = dot_tn(prob.astype(bf), g)
            gprob = dot_nt(g, v)
            gs = (prob * (gprob - jnp.sum(prob * gprob, axis=-1, keepdims=True))).astype(bf)
            gq_ = merge_heads(jnp.dot(gs, k, preferred_element_type=f)) * SCALE
            gk = dot_tn(gs, stack_heads(q)) * SCALE
            gp[i, :, a] = turn(gq_, cosine, sine).astype(bf)
            gp[i, :, b] = turn(gk, cosine, sine).astype(bf)
            gp[i, :, c] = gv.astype(bf)
            return 0

        lax.fori_loop(0, 4, pair, 0)
        return 0

    lax.fori_loop(0, 4, attend, 0)

    def qkv_tile(i, _):
        rows = pl.ds(pl.multiple_of(i * 256, 256), 256)
        out = dot_tn(ve[:, :, rows].reshape(512, 256), gp[...].reshape(512, 1536)).astype(bf).reshape(4, 2, 32, 1536)
        dq[0, i // 2, lax.rem(i, 2)] = out[:, 0]
        dq[1, i // 2, lax.rem(i, 2)] = out[:, 1]
        return 0

    lax.fori_loop(0, 8, qkv_tile, 0)
    sq = Sum(p, cp, dq, rcq, rxq, rzq, 2)
    sq.start()
    so.stage_x()
    gs = []
    for n in range(4):
        out = dot_nt(gp[...].reshape(512, 1536), vq[n].reshape(512, 1536))
        cols = pl.ds(n * 512, 512)
        gpart[:, :, cols] = out.astype(bf).reshape(4, 128, 512)
        gs += [cp.push(gpart.at[lax.rem(p.y + k, 4), :, cols], recv_g.at[k - 1, :, cols], p.at(dy=k)) for k in (1, 3, 2)]
    sq.stage_x()
    so.stage_z()
    for c in zs:
        c.wait_recv()
    here1 = vi1.at[p.z]
    add_into(here1, (here1, rz1.at[0], rz1.at[1], rz1.at[2]))
    f1 = Finish(p, cp, here1, rx1, t1, o1, lsem.at[14], False)
    f1.stage_xh()

    wide[...] = jnp.zeros_like(wide)
    rows = []
    for n in range(12):
        rows.append(jnp.sum(gp[:, :, n * 128:(n + 1) * 128].reshape(512, 128).astype(f), axis=0, keepdims=True))
    rows = jnp.concatenate(rows + [jnp.zeros((20, 128), f)], axis=0).astype(bf)
    for i in range(8):
        for y in range(4):
            ds[0, i // 2, i % 2, y, :, 128:256] = rows
            ds[1, i // 2, i % 2, y, :, 128:256] = jnp.zeros_like(rows)
    for c in gs:
        c.wait_recv()
    wide[2:4] = sums[0:2]

    def block(i, _):
        r = pl.ds(pl.multiple_of(i * ROWS, ROWS), ROWS)
        g = gpart[p.y, r].astype(f) + recv_g[0, r].astype(f) + recv_g[1, r].astype(f) + recv_g[2, r].astype(f)
        m, inv = norm_rows(tok[r].astype(f))
        wide[0:1] += jnp.sum(g * m, axis=0, keepdims=True)
        wide[1:2] += jnp.sum(g, axis=0, keepdims=True)
        e = g * gains[0:1, :]
        out = gmid[r] + inv * (e - jnp.mean(e, axis=-1, keepdims=True) - m * jnp.mean(e * m, axis=-1, keepdims=True))
        ing[r] = out.astype(bf)
        return 0

    lax.fori_loop(0, 128 // ROWS, block, 0)
    for i in range(16):
        z, xl, y = i // 4, (i // 2) % 2, (i % 2) * 2
        piece = jnp.transpose(wide[:, i * 128:(i + 1) * 128]).astype(bf)
        for k in range(4):
            ds[k % 2, z, xl, y + k // 2, :, 0:128] = piece[k * 32:(k + 1) * 32]
    ss = Sum(p, cp, ds, rcs, rxs, rzs, 2)
    ss.start()
    so_here = so.stage_sum()
    fo = Finish(p, cp, so_here, rxho, to, oo, lsem.at[15], True)
    fo.stage_xh()
    sq.stage_z()
    fd.stage_y()
    f0.stage_y()
    f1.stage_y()
    ss.stage_x()
    for c in rs:
        c.wait_recv()

    def final(i, _):
        r = pl.ds(pl.multiple_of(i * ROWS, ROWS), ROWS)
        act[r] = (mid[r] + own_r[r].astype(f) + recv_r[0, r].astype(f) + recv_r[1, r].astype(f) + recv_r[2, r].astype(f)).astype(bf)
        return 0

    lax.fori_loop(0, 128 // ROWS, final, 0)
    ss.stage_z()
    here = sq.stage_sum()
    fq = Finish(p, cp, here, rxhq, tq, oq, lsem.at[16], False)
    fq.stage_xh()
    here = ss.stage_sum()
    fs = Finish(p, cp, here, rxhs, ts, os, lsem.at[17], False)
    fs.stage_xh()
    fd.stage_c()
    f0.stage_c()
    f1.stage_c()
    fo.stage_y()
    fq.stage_y()
    fs.stage_y()
    fo.stage_c()
    fq.stage_c()
    fs.stage_c()
    for x in (fd, f0, f1, fo, fq, fs):
        x.finish()
    cp.finish()


def third_step(*args):
    f, bf = jnp.float32, jnp.bfloat16
    S = jax.ShapeDtypeStruct
    hbm, vm = pl.BlockSpec(memory_space=pl.ANY), pl.BlockSpec(memory_space=pltpu.VMEM)
    V = pltpu.VMEM

    def sums(tail):
        return [V((2, 4, 2) + tail, bf), V((4, 2) + tail, bf), V((4,) + tail, bf), V((3,) + tail, bf), V(tail, bf), V(tail, bf)]

    return pl.pallas_call(
        third_kernel,
        out_shape=(S((128, 2048), bf), S((128, 2048), bf), S((11, 16, 2048), bf), S((4, 64, 1408), bf), S((4, 64, 1408), bf),
                   S((4, 64, 1536), bf), S((64, 2048), bf), S((4, 64, 256), bf)),
        in_specs=[hbm] * 9 + [vm] * 5 + [hbm] * 3, out_specs=(vm, vm) + (hbm,) * 6,
        scratch_shapes=[
            V((4, 128, 2048), bf), V((4, 2, 64, 2048), bf), V((4, 2, 4, 64, 1536), bf), V((4, 128, 2048), bf),
            V((4, 128, 1536), bf), V((4, 4, 256, 128), f), V((4, 128, 512), bf), V((4, 2, 128, 128), f),
            V((4, 128, 512), bf), V((4, 128, 1536), bf), V((4, 128, 2048), bf), V((3, 128, 2048), bf), V((3, 128, 2048), bf),
            V((128, 2048), bf), V((128, 2048), f),
            V((11, 16, 1024), bf), V((11, 16, 1024), bf), V((11, 16, 1024), bf),
            V((4, 32, 1408), bf), V((4, 32, 1408), bf), V((4, 32, 1408), bf),
            V((4, 4, 32, 1408), bf), V((3, 4, 32, 1408), bf), V((4, 32, 1408), bf), V((4, 32, 1408), bf)]
        + sums((4, 32, 1536)) + sums((64, 1024)) + sums((4, 32, 256))
        + [pltpu.SemaphoreType.DMA((64,)), pltpu.SemaphoreType.DMA((64,)), pltpu.SemaphoreType.DMA((18,))],
        compiler_params=pltpu.CompilerParams(collective_id=4, has_side_effects=True, vmem_limit_bytes=62 * 2**20),
        name="third_step",
    )(*args)


def small_parameters(ln1_gain, ln1_bias, ln2_gain, ln2_bias, qkv_bias):
    f = jnp.float32
    norms = jnp.concatenate([jnp.stack([ln1_gain, ln1_bias, ln2_gain, ln2_bias], axis=1), jnp.zeros((64, 124), jnp.bfloat16)], axis=1)
    shard = (lax.axis_index("z") * 2 + lax.axis_index("xl")) * 4 + lax.axis_index("y")
    place = lax.broadcasted_iota(jnp.int32, (3, 8, 4), 0) * 32 + lax.broadcasted_iota(jnp.int32, (3, 8, 4), 1) * 4 + lax.broadcasted_iota(jnp.int32, (3, 8, 4), 2)
    own = qkv_bias.reshape(3, 64).astype(f)
    full = sum(jnp.where((place == shard * 3 + k)[..., None], own[k], 0.0) for k in range(3))
    bias = full.transpose(2, 0, 1, 3).reshape(4, 12, 128).astype(jnp.bfloat16)
    bias = jnp.pad(bias, ((0, 0), (0, 52), (0, 0)))
    return jnp.concatenate([jnp.broadcast_to(norms[None], (4, 64, 128)), bias], axis=2)


def local(tokens, segment_ids, cotangent, ln1_gain, ln1_bias, qkv_weight, qkv_bias, out_weight,
          ln2_gain, ln2_bias, gate_weight, up_weight, down_weight):
    f, bf = jnp.float32, jnp.bfloat16
    wq = qkv_weight.reshape(64, 3, 8, 4, 64).transpose(3, 0, 1, 2, 4).reshape(4, 64, 1536)
    wg = gate_weight.reshape(64, 8, 4, 176).transpose(2, 0, 1, 3).reshape(4, 64, 11, 1, 128)
    wu = up_weight.reshape(64, 8, 4, 176).transpose(2, 0, 1, 3).reshape(4, 64, 11, 1, 128)
    wgu = jnp.concatenate([wg, wu], axis=3).reshape(4, 64, 2816)
    small = small_parameters(ln1_gain, ln1_bias, ln2_gain, ln2_bias, qkv_bias)
    seg = jnp.broadcast_to(segment_ids.astype(f), (8, 128))
    lane = jnp.arange(128) % 8
    freqs = jnp.broadcast_to(10000.0 ** (-(lane.astype(f) * 2.0) / ROT), (8, 128))
    cots, gq, ggu, go, gd, e1, qkv, prb, mix, tab, gains, mid, ents = first_step(
        tokens, cotangent, seg, wq, small, wgu, out_weight, down_weight, freqs)
    rpart, gmid, gmls, sums, jd, j0, i1 = second_step(ggu, gd.reshape(1408, 2048), ents, cots, mid, cotangent, gains)
    act, ing, od, o0, o1, oq, oo, os = third_step(
        gmls, go, gq, e1, qkv, prb, mix, tab, rpart, mid, tokens, gmid, gains, sums, jd, j0, i1)

    os = os.astype(f)
    norms = jnp.sum(os[:, :, :4], axis=0)
    shard = (lax.axis_index("z") * 2 + lax.axis_index("xl")) * 4 + lax.axis_index("y")
    bias = os[:, :12, 128:].reshape(4, 3, 8, 64).transpose(1, 2, 0, 3).reshape(6144)
    bias = lax.dynamic_slice_in_dim(bias, shard * 192, 192, 0)
    qkv_grad = oq.reshape(4, 64, 3, 8, 64).transpose(1, 2, 3, 0, 4).reshape(64, 6144).astype(f)
    ogu = jnp.concatenate([o0, o1], axis=2).reshape(4, 64, 11, 2, 128)
    gate_grad = ogu[:, :, :, 0].reshape(4, 64, 8, 176).transpose(1, 2, 0, 3).reshape(64, 5632).astype(f)
    up_grad = ogu[:, :, :, 1].reshape(4, 64, 8, 176).transpose(1, 2, 0, 3).reshape(64, 5632).astype(f)
    return (act, ing, norms[:, 0], norms[:, 1], qkv_grad, bias, oo.astype(f),
            norms[:, 2], norms[:, 3], gate_grad, up_grad, od.reshape(176, 2048).astype(f))


def solution(mesh):
    fine = Mesh(mesh.devices.reshape(2, 2, 4, 2, 4), AXES)
    whole, rows = P(AXES, None), P(("z", "xl", "y"), None)
    vector = P(("z", "xl", "y"))
    return jax.shard_map(
        local, mesh=fine,
        in_specs=(whole, whole, whole, vector, vector, rows, vector, rows, vector, vector, rows, rows, rows),
        out_specs=(whole, whole, vector, vector, rows, vector, rows, vector, vector, rows, rows, rows),
        check_vma=False,
    )
```

```python
import functools
import jax, jax.numpy as jnp
from jax import lax
from jax.sharding import PartitionSpec as P, Mesh
from jax.experimental import pallas as pl
from jax.experimental.pallas import tpu as pltpu

AXES = ("xh", "c", "z", "xl", "y")


class Place:
    def __init__(self):
        self.xh, self.c, self.z, self.xl, self.y = (lax.axis_index(a) for a in AXES)
        self.x = self.xh * 2 + self.xl

    def at(self, dx=0, dy=0, dz=0, dc=0):
        x = lax.rem(self.x + dx + 4, 4) if dx else self.x
        return (
            x // 2 if dx else self.xh,
            lax.rem(self.c + dc, 2) if dc else self.c,
            lax.rem(self.z + dz + 4, 4) if dz else self.z,
            lax.rem(x, 2) if dx else self.xl,
            lax.rem(self.y + dy + 4, 4) if dy else self.y,
        )


def barrier(targets):
    sem = pltpu.get_barrier_semaphore()
    for target in targets:
        pl.semaphore_signal(sem, inc=1, device_id=target, device_id_type=pl.DeviceIdType.MESH)
    pl.semaphore_wait(sem, len(targets))


class Copies:
    def __init__(self, send, recv):
        self.send, self.recv, self.used, self.all = send, recv, 0, []

    def push(self, src, dst, target):
        copy = pltpu.make_async_remote_copy(
            src_ref=src, dst_ref=dst, send_sem=self.send.at[self.used],
            recv_sem=self.recv.at[self.used], device_id=target, device_id_type=pl.DeviceIdType.MESH)
        self.used += 1
        self.all.append(copy)
        copy.start()
        return copy

    def sent(self, copy):
        copy.wait_send()
        self.all = [c for c in self.all if c is not copy]

    def finish(self):
        for copy in self.all:
            copy.wait_send()


def add_into(out, parts):
    total = parts[0][...].astype(jnp.float32)
    for part in parts[1:]:
        total = total + part[...].astype(jnp.float32)
    out[...] = total.astype(out.dtype)


def peers(p):
    return [p.at(dy=d) for d in (1, 2, 3)] + [p.at(dz=d) for d in (1, 2, 3)] + [p.at(dx=d) for d in (1, 2, -1)] + [p.at(dc=1)]


class Gather:
    def __init__(self, p, cp, src, dst, lsem, cols=None, cut=None, unit=32):
        self.p, self.cp, self.src, self.dst, self.lsem, self.cut = p, cp, src, dst, lsem, cut
        self.cols = cols
        if cut is None:
            self.half = pl.ds(pl.multiple_of(p.c * unit, unit), unit)
        else:
            self.half = pl.ds(pl.multiple_of(p.c * 1024, 1024), 1024)

    def start(self):
        p, src, dst, half = self.p, self.src, self.dst, self.half
        if self.cut is None:
            cols = self.cols
            here = dst.at[p.z, p.xl, p.y, half, cols]
            self.local = pltpu.make_async_copy(src.at[p.y, half, cols], here, self.lsem)
            self.local.start()
            self.ys = [self.cp.push(src.at[lax.rem(p.y + d, 4), half, cols], here, p.at(dy=d)) for d in (1, 3, 2)]
        else:
            here = dst.at[p.z, p.xl, :, half]
            self.local = pltpu.make_async_copy(src.at[:, half], here, self.lsem)
            self.local.start()
            self.zs = [self.cp.push(src.at[:, half], here, p.at(dz=d)) for d in (1, 3, 2)]

    def stage_y(self):
        self.local.wait()
        for c in self.ys:
            c.wait_recv()

    def stage_z(self):
        p = self.p
        self.stage_y()
        here = self.dst.at[p.z, p.xl, :, self.half, self.cols]
        self.zs = [self.cp.push(here, here, p.at(dz=d)) for d in (1, 3, 2)]

    def parts(self, xl):
        g = self.dst
        if self.cut is not None:
            k, r = self.cut, g.shape[2]
            return g.at[:, xl, 0:k, self.half], g.at[:, xl, k:r, self.half], g.at[:, xl, :, self.half]
        return (g.at[:, xl, 0:2, self.half, self.cols], g.at[:, xl, 2:4, self.half, self.cols],
                g.at[:, xl, :, self.half, self.cols])

    def stage_x(self):
        p = self.p
        if self.cut is not None:
            self.local.wait()
        for c in self.zs:
            c.wait_recv()
        lo, hi, full = self.parts(p.xl)
        self.xs = [self.cp.push(lo, lo, p.at(dx=1)), self.cp.push(hi, hi, p.at(dx=-1))]
        self.cs = [self.cp.push(full, full, p.at(dc=1))]

    def stage_c(self):
        p = self.p
        lo, hi, full = self.parts(1 - p.xl)
        self.xs[0].wait_recv()
        self.cs.append(self.cp.push(lo, lo, p.at(dc=1)))
        self.xs[1].wait_recv()
        self.cs.append(self.cp.push(hi, hi, p.at(dc=1)))

    def finish(self):
        for c in self.cs:
            c.wait_recv()


class Spread:
    def __init__(self, p, cp, src, dst):
        self.p, self.cp, self.src, self.dst = p, cp, src, dst

    def start(self):
        p = self.p
        self.near = [self.cp.push(self.src, self.dst.at[p.y], p.at(dy=d)) for d in (1, 3)]

    def relay(self, k):
        p = self.p
        self.near[k].wait_recv()
        half = self.dst.at[lax.rem(p.y + (3, 1)[k], 4), pl.ds(64 * k, 64)]
        copy = self.cp.push(half, half, p.at(dy=(1, 3)[k]))
        self.far = [copy] if k == 0 else self.far + [copy]

    def finish(self):
        for c in self.far:
            c.wait_recv()


ROWS = 16
norm_epsilon = 1e-05
masked_score = -1000000000.0
HEADS = 8
HEAD_DIM = 64
ROT = 16
SCALE = HEAD_DIM ** (-0.5)


def norm_rows(m):
    m = m - jnp.mean(m, axis=-1, keepdims=True)
    inv = lax.rsqrt(jnp.mean(m * m, axis=-1, keepdims=True) + norm_epsilon)
    return m * inv, inv


def allowed_of(seg_row):
    keys = jnp.broadcast_to(seg_row, (128, 128))
    queries = jnp.transpose(keys)
    q = lax.broadcasted_iota(jnp.int32, (128, 128), 0)
    k = lax.broadcasted_iota(jnp.int32, (128, 128), 1)
    same = keys == queries
    places = jnp.sum(jnp.where(same & (k < q), 1.0, 0.0), axis=-1, keepdims=True)
    return same & (k <= q), places


def turn(x, cosine, sine):
    lane = lax.broadcasted_iota(jnp.int32, (128, 128), 1)
    other = jnp.where(lax.rem(lane, 64) < 8, pltpu.roll(x, 120, 1), pltpu.roll(x, 8, 1))
    return x * cosine + other * sine


def stack_heads(x):
    lane = lax.broadcasted_iota(jnp.int32, (128, 128), 1)
    zero = jnp.zeros_like(x)
    return jnp.concatenate([jnp.where(lane < 64, x, zero), jnp.where(lane < 64, zero, x)], axis=0)


def merge_heads(x):
    lane = lax.broadcasted_iota(jnp.int32, (128, 128), 1)
    return jnp.where(lane < 64, x[:128], x[128:])


def dot_nt(a, b):
    return lax.dot_general(a, b, (((1,), (1,)), ((), ())), preferred_element_type=jnp.float32)


def dot_tn(a, b):
    return lax.dot_general(a, b, (((0,), (0,)), ((), ())), preferred_element_type=jnp.float32)


def moved_lanes(pieces, load):
    out = None
    for first, end, source, column in pieces:
        while first < end:
            group, at = divmod(column, 128)
            width = min(end - first, 128 - at)
            value = load(source, group)
            shift = (first - at) % 128
            if shift:
                value = pltpu.roll(value, shift, 1)
            if out is None:
                out = value
            else:
                lane = lax.broadcasted_iota(jnp.int32, value.shape, 1)
                out = jnp.where((lane >= first) & (lane < first + width), value, out)
            first, column = first + width, column + width
    return out


def hidden_pieces(part, group):
    pieces, at = [], 0
    while at < 128:
        block, rest = divmod(group * 128 + at, 176)
        width = min(128 - at, 176 - rest)
        pieces.append((at, at + width, 0, (4 * block + part) * 176 + rest))
        at += width
    return pieces


def shard_pieces(group):
    pieces, at = [], 0
    while at < 128:
        shard, rest = divmod(group * 128 + at, 176)
        width = min(128 - at, 176 - rest)
        pieces.append((at, at + width, shard % 4, (shard // 4) * 176 + rest))
        at += width
    return pieces


def first_kernel(tok, cot, seg, wq, sm, wg, wu, wo, wd,
                 cots, gq, ggu, go, gd, e1, qkv, prb, mix, tab, gains_out, mid_out, ent_out,
                 rq, rg, ru, pq, pgu, vq, vs, vo, x, xe, segv, segs, proj, qkvb, probs, mixed, tabs, masks, part, recv_a, own, bias, gains, mid, ent,
                 send, recv, lsem):
    p = Place()
    f, bf = jnp.float32, jnp.bfloat16
    locals_ = []

    def local(src, dst):
        copy = pltpu.make_async_copy(src, dst, lsem.at[len(locals_)])
        copy.start()
        locals_.append(copy)
        return copy

    def sem():
        locals_.append(None)
        return lsem.at[len(locals_) - 1]

    raw = [local(wq, rq), local(wg, rg), local(wu, ru), local(tok, own)]
    barrier([p.at(dy=d) for d in (1, 2, 3)] + [p.at(dz=d) for d in (1, 2, 3)] + [p.at(dx=1), p.at(dx=-1), p.at(dc=1)])
    cp = Copies(send, recv)

    def share(src, dst):
        return [local(src, dst.at[p.y])], [cp.push(src, dst.at[p.y], p.at(dy=d)) for d in (1, 3, 2)]

    q = [Gather(p, cp, pq, vq, sem(), cols=pl.ds(n * 384, 384)) for n in range(4)]
    s = Gather(p, cp, sm, vs, sem(), cols=pl.ds(0, 128), unit=16)
    u0 = Gather(p, cp, pgu, ggu, sem(), cols=pl.ds(0, 512))
    u1 = Gather(p, cp, pgu, ggu, sem(), cols=pl.ds(512, 512))
    u2 = Gather(p, cp, pgu, ggu, sem(), cols=pl.ds(1024, 1792))
    o = Gather(p, cp, wo, vo, sem(), cut=32)
    d = Gather(p, cp, wd, gd, sem(), cut=96)
    xs = Spread(p, cp, tok, x)
    cs = Spread(p, cp, cot, cots)

    s.start()
    segv[...] = jnp.broadcast_to(seg[...].astype(f), (8, 128))
    s_here, s_in = share(segv, segs)
    raw[0].wait()
    for n in range(4):
        for j in range(4):
            for k in range(3):
                pieces = [(0, 64, 0, k * 2048 + (8 * n + j) * 64), (64, 128, 0, k * 2048 + (8 * n + 4 + j) * 64)]
                got = moved_lanes(pieces, lambda _, g: rq[:, g * 128:(g + 1) * 128].astype(f))
                pq[j, :, n * 384 + k * 128:n * 384 + (k + 1) * 128] = got.astype(bf)
        q[n].start()
    xs.start()
    x_here = [local(tok, x.at[p.y])]
    raw[1].wait()
    raw[2].wait()
    for j in range(4):
        for t in range(11):
            for k, r in enumerate((rg, ru)):
                got = moved_lanes(hidden_pieces(j, t), lambda _, g: r[:, g * 128:(g + 1) * 128].astype(f))
                pgu[j, :, t * 256 + k * 128:t * 256 + (k + 1) * 128] = got.astype(bf)
    s.stage_z()
    q[0].stage_z()
    q[1].stage_z()
    for c in s_here:
        c.wait()
    for c in s_in:
        c.wait_recv()

    lane = lax.broadcasted_iota(jnp.int32, (128, 128), 1)
    low = lax.rem(lane, 64)

    freqs = jnp.zeros((1, 128), f)
    for k in range(ROT // 2):
        freqs = jnp.where(lax.rem(lane[0:1], ROT // 2) == k, 10000.0 ** (-2.0 * k / ROT), freqs)

    def table(i, _):
        allowed, places = allowed_of(segs[i, 0:1, :])
        masks[i] = jnp.where(allowed, 1.0, 0.0)
        angle = places * freqs
        tabs[i, 0] = jnp.where(low < ROT, jnp.cos(angle), 1.0)
        sine = jnp.sin(angle)
        tabs[i, 1] = jnp.where(low < ROT // 2, -sine, jnp.where(low < ROT, sine, 0.0))
        return 0

    lax.fori_loop(0, 4, table, 0)
    local(tabs, tab)
    s.stage_x()
    s.stage_c()
    q[0].stage_x()
    q[2].stage_z()
    s.finish()

    half_lane = lax.broadcasted_iota(jnp.int32, (8, 128), 1) < 64
    for i in range(16):
        z, xl, y = i // 4, (i // 2) % 2, (i % 2) * 2
        a = vs[z, xl, y, 0:16].astype(f)[0:8]
        b = pltpu.roll(vs[z, xl, y + 1, 0:16].astype(f)[0:8], 64, 1)
        gains[:, i * 128:(i + 1) * 128] = jnp.where(half_lane, a, b)
    total = jnp.zeros((16, 128), f)
    for i in range(32):
        total = total + vs[i // 8, (i // 4) % 2, i % 4, 16:32].astype(f)
    bias[...] = total

    local(gains, gains_out)

    def entry(i):
        def block(b, _):
            r = pl.ds(pl.multiple_of(b * ROWS, ROWS), ROWS)
            n, _inv = norm_rows(x[i, r].astype(f))
            xe[i, r] = (n * gains[0:1, :] + gains[1:2, :]).astype(bf)
            return 0
        lax.fori_loop(0, 128 // ROWS, block, 0)

    q[1].stage_x()
    q[3].stage_z()
    x_here[0].wait()
    entry(p.y)
    xs.relay(0)
    xs.relay(1)
    q[0].stage_c()
    q[2].stage_x()
    o.start()
    entry(lax.rem(p.y + 3, 4))
    q[1].stage_c()
    q[3].stage_x()
    d.start()
    entry(lax.rem(p.y + 1, 4))
    q[2].stage_c()
    u0.start()
    u1.start()
    xs.finish()
    entry(lax.rem(p.y + 2, 4))
    cs.start()
    c_here = [local(cot, cots.at[p.y])]
    local(xe, e1)

    def heads(n):
        q[n].finish()
        first = n * 384
        w = vq[:, :, :, :, first:first + 384].reshape(2048, 384)
        out = jnp.dot(xe[...].reshape(512, 2048), w, preferred_element_type=f)
        b = jnp.concatenate([bias[k * 4 + n:k * 4 + n + 1, :] for k in range(3)], axis=1)
        proj[...] = (out + b).reshape(4, 128, 384)

        def attend(i, _):
            allowed = masks[i] > 0.5
            allowed = jnp.concatenate([allowed, allowed], axis=0)
            cosine, sine = tabs[i, 0], tabs[i, 1]
            qr = turn(proj[i, :, 0:128], cosine, sine).astype(bf)
            kr = turn(proj[i, :, 128:256], cosine, sine).astype(bf)
            v = proj[i, :, 256:384].astype(bf)
            qkvb[i, :, first:first + 128] = qr
            qkvb[i, :, first + 128:first + 256] = kr
            qkvb[i, :, first + 256:first + 384] = v
            scores = dot_nt(stack_heads(qr), kr) * SCALE
            scores = jnp.where(allowed, scores, masked_score)
            expos = jnp.exp(scores - jnp.max(scores, axis=-1, keepdims=True))
            prob = expos / jnp.sum(expos, axis=-1, keepdims=True)
            probs[i, n] = prob
            got = jnp.dot(prob.astype(bf), v, preferred_element_type=f)
            mixed[i, :, n * 128:(n + 1) * 128] = merge_heads(got).astype(bf)
            return 0

        lax.fori_loop(0, 4, attend, 0)

    heads(0)
    q[3].stage_c()
    o.stage_x()
    heads(1)
    heads(2)
    cs.relay(0)
    cs.relay(1)
    u2.start()
    heads(3)
    o.stage_c()
    d.stage_x()
    u0.stage_z()
    u1.stage_z()
    o.finish()
    ins = []
    for n in range(4):
        cols = pl.ds(n * 512, 512)
        out = jnp.dot(mixed[...].reshape(512, 512), vo[:, :, :, cols].reshape(512, 512), preferred_element_type=f)
        part[:, :, cols] = out.astype(bf).reshape(4, 128, 512)
        ins += [cp.push(part.at[lax.rem(p.y + k, 4), :, cols], recv_a.at[k - 1, :, cols], p.at(dy=k)) for k in (1, 3, 2)]
    u2.stage_z()
    local(vo, go)
    local(vq, gq)
    local(qkvb, qkv)
    local(probs, prb)
    local(mixed, mix)
    u0.stage_x()
    u1.stage_x()
    d.stage_c()
    for c in ins:
        c.wait_recv()

    def block(i, _):
        r = pl.ds(pl.multiple_of(i * ROWS, ROWS), ROWS)
        m = own[r].astype(f) + part[p.y, r].astype(f) + recv_a[0, r].astype(f) + recv_a[1, r].astype(f) + recv_a[2, r].astype(f)
        mid[r] = m
        n, _inv = norm_rows(m)
        ent[r] = (n * gains[2:3, :] + gains[3:4, :]).astype(bf)
        return 0

    raw[3].wait()
    lax.fori_loop(0, 128 // ROWS, block, 0)
    local(mid, mid_out)
    local(ent, ent_out)
    u0.stage_c()
    u1.stage_c()
    for c in u2.zs:
        c.wait_recv()
    cs.finish()
    for g in (d, u0, u1):
        g.finish()
    cp.finish()
    for copy in locals_:
        if copy is not None and not any(copy is done for done in x_here + s_here + raw):
            copy.wait()


def first_step(tok, cot, seg, wq, sm, wg, wu, wo, wd):
    f, bf = jnp.float32, jnp.bfloat16
    S = jax.ShapeDtypeStruct
    hbm, vm = pl.BlockSpec(memory_space=pl.ANY), pl.BlockSpec(memory_space=pltpu.VMEM)
    V = pltpu.VMEM
    outs = (S((4, 128, 2048), bf), S((4, 2, 4, 64, 1536), bf), S((4, 2, 4, 64, 2816), bf), S((4, 2, 64, 2048), bf),
            S((4, 2, 176, 2048), bf), S((4, 128, 2048), bf), S((4, 128, 1536), bf), S((4, 4, 256, 128), f),
            S((4, 128, 512), bf), S((4, 2, 128, 128), f), S((8, 2048), f), S((128, 2048), f), S((128, 2048), bf))
    return pl.pallas_call(
        first_kernel, out_shape=outs, in_specs=[hbm, hbm, vm] + [hbm] * 6,
        out_specs=(hbm,) * 13,
        scratch_shapes=[
            V((64, 6144), bf), V((64, 5632), bf), V((64, 5632), bf), V((4, 64, 1536), bf), V((4, 64, 2816), bf),
            V((4, 2, 4, 64, 1536), bf), V((4, 2, 4, 32, 128), bf), V((4, 2, 64, 2048), bf),
            V((4, 128, 2048), bf), V((4, 128, 2048), bf), V((8, 128), f), V((4, 8, 128), f), V((4, 128, 384), f),
            V((4, 128, 1536), bf), V((4, 4, 256, 128), f), V((4, 128, 512), bf),
            V((4, 2, 128, 128), f), V((4, 128, 128), f), V((4, 128, 2048), bf), V((3, 128, 2048), bf),
            V((128, 2048), bf), V((16, 128), f), V((8, 2048), f), V((128, 2048), f), V((128, 2048), bf),
            pltpu.SemaphoreType.DMA((128,)), pltpu.SemaphoreType.DMA((128,)), pltpu.SemaphoreType.DMA((32,))],
        compiler_params=pltpu.CompilerParams(collective_id=1, has_side_effects=True, vmem_limit_bytes=56 * 2**20),
        name="first_step",
    )(tok, cot, seg, wq, sm, wg, wu, wo, wd)


class Sum:
    def __init__(self, p, cp, terms, rx, rz, cut, rc=None, other=None):
        self.p, self.cp, self.h, self.other, self.rc, self.rx, self.rz, self.cut = p, cp, terms, other, rc, rx, rz, cut

    def start(self, first=0, stop=4):
        part = pl.ds(first, stop - first)
        self.core = ([] if first == 0 else self.core) + [self.cp.push(self.other.at[part], self.rc.at[part], self.p.at(dc=1))]

    def stage_core(self):
        h, rc = self.h, self.rc
        for c in self.core:
            c.wait_recv()

        def both(i, _):
            add_into(h.at[i], (h.at[i], rc.at[i]))
            return 0

        lax.fori_loop(0, 4, both, 0)

    def stage_x(self):
        p, h, rc, k = self.p, self.h, self.rc, self.cut
        if rc is not None:
            for c in self.core:
                c.wait_recv()

            def foreign(i, _):
                add_into(h.at[i, 1 - p.xl], (h.at[i, 1 - p.xl], rc.at[i, 1 - p.xl]))
                return 0

            lax.fori_loop(0, 4, foreign, 0)
        n = h.shape[2]
        self.xs = [
            self.cp.push(h.at[:, 1 - p.xl, 0:k], self.rx.at[:, 0:k], p.at(dx=1)),
            self.cp.push(h.at[:, 1 - p.xl, k:n], self.rx.at[:, k:n], p.at(dx=-1)),
        ]

    def stage_own(self):
        p, h, rc, rx = self.p, self.h, self.rc, self.rx
        for c in self.xs:
            c.wait_recv()

        def own(i, _):
            here = h.at[i, p.xl]
            add_into(here, (here, rx.at[i]) if rc is None else (here, rc.at[i, p.xl], rx.at[i]))
            return 0

        lax.fori_loop(0, 4, own, 0)

    def push_z(self, blocks):
        p = self.p
        self.blocks = blocks
        self.zs = [self.cp.push(blocks.at[lax.rem(p.z + d, 4)], self.rz.at[d - 1], p.at(dz=d)) for d in (1, 3, 2)]

    def stage_z(self):
        self.stage_own()
        self.push_z(self.h.at[:, self.p.xl])

    def stage_sum(self):
        rz = self.rz
        here = self.blocks.at[self.p.z]
        for c in self.zs:
            c.wait_recv()
        add_into(here, (here, rz.at[0], rz.at[1], rz.at[2]))
        return here


def second_kernel(ggu, gd, own_ent, cots, mid_in, cot_in, gains_in,
                  rpart, gmid_out, low_out, sums_out, jd, i0, h1,
                  vgu, vd, ent, cts, hid, dgu, gpart, recv_g, dd, d0, d1, rcd, rxd, rzd, rx0, mid, cot, gains, gmid, low, sums,
                  send, recv, lsem, ready):
    p = Place()
    f, bf = jnp.float32, jnp.bfloat16
    sib = p.at(dc=1)
    own_load = pltpu.make_async_copy(own_ent, ent.at[p.y], lsem.at[0])
    loads = [pltpu.make_async_copy(a, b, lsem.at[1 + i]) for i, (a, b) in enumerate(((cots, cts), (gd, vd)))]
    tiles = []
    for n in range(2):
        cols = pl.ds(n * 512, 512)
        tiles.append(pltpu.make_async_copy(ggu.at[:, :, :, :, cols], vgu.at[:, :, :, :, cols], lsem.at[3 + n]))
    rest = [pltpu.make_async_copy(a, b, lsem.at[6 + i]) for i, (a, b) in enumerate(((mid_in, mid), (cot_in, cot), (gains_in, gains)))]
    for c in [own_load] + loads + tiles + rest:
        c.start()
    barrier([p.at(dy=d) for d in (1, 2, 3)] + [p.at(dz=d) for d in (1, 2, 3)] + [p.at(dx=1), p.at(dx=-1), sib])
    cp = Copies(send, recv)
    es = Spread(p, cp, own_ent, ent)
    es.start()
    half = pl.ds(pl.multiple_of(p.c * 32, 32), 32)
    late = [pl.ds(1024, 896), pl.ds(1920, 896)]
    mine = [pltpu.make_async_copy(ggu.at[:, p.xl, :, half, cols], vgu.at[:, p.xl, :, half, cols], lsem.at[9 + i]) for i, cols in enumerate(late)]
    for c in mine:
        c.start()
    ux = [[cp.push(ggu.at[:, p.xl, a:a + 2, half, cols], vgu.at[:, p.xl, a:a + 2, half, cols], p.at(dx=d)) for a, d in ((0, 1), (2, -1))] for cols in late]
    uc = [[cp.push(ggu.at[:, p.xl, :, half, cols], vgu.at[:, p.xl, :, half, cols], sib)] for cols in late]

    def late_c(k):
        for i in range(2):
            ux[k][i].wait_recv()
            there = vgu.at[:, 1 - p.xl, 2 * i:2 * i + 2, half, late[k]]
            uc[k].append(cp.push(there, there, sib))

    for c in loads:
        c.wait()

    def back_tile(first, width):
        out = dot_nt(cts[...].reshape(512, 2048), vd[pl.ds(first, width), :])
        hid[:, pl.ds(first, width)] = out.astype(bf)

    def back(n, _):
        back_tile(pl.multiple_of(n * 256, 256), 256)
        return 0

    lax.fori_loop(0, 5, back, 0)
    back_tile(1280, 128)

    def hidden_tile(first, width):
        w = vgu[:, :, :, :, pl.ds(2 * first, 2 * width)].reshape(2048, 2 * width)
        gu = jnp.dot(ent[...].reshape(512, 2048), w, preferred_element_type=f)
        for k in range(width // 128):
            gate, up = gu[:, k * 256:k * 256 + 128], gu[:, k * 256 + 128:k * 256 + 256]
            cols = pl.ds(first + k * 128, 128)
            g = hid[:, cols].astype(f)
            sig = 1.0 / (1.0 + jnp.exp(-gate))
            silu = gate * sig
            hid[:, cols] = (silu * up).astype(bf)
            dgu[:, pl.ds(2 * first + k * 256, 128)] = (g * up * sig * (1.0 + gate * (1.0 - sig))).astype(bf)
            dgu[:, pl.ds(2 * first + k * 256 + 128, 128)] = (g * silu).astype(bf)

    def tile(n, _):
        hidden_tile(pl.multiple_of(n * 256, 256), 256)
        return 0

    es.relay(0)
    es.relay(1)
    own_load.wait()
    for c in tiles + mine:
        c.wait()
    late_c(0)
    es.finish()
    late_c(1)
    lax.fori_loop(0, 2, tile, 0)
    for c in uc[0] + uc[1]:
        c.wait_recv()
    lax.fori_loop(2, 5, tile, 0)
    hidden_tile(1280, 128)

    def down_half(h):
        cols = pl.ds(pl.multiple_of(h * 1024, 1024), 1024)

        def down_tile(t, _):
            rows = pl.ds(pl.multiple_of(t * 128, 128), 128)
            out = dot_tn(hid[:, rows], cts[:, :, cols].reshape(512, 1024)).astype(bf)
            for k in range(8):
                g = t * 8 + k
                dd[h, g // 22, lax.rem(g // 11, 2), lax.rem(g, 11)] = out[k * 16:(k + 1) * 16]
            return 0

        lax.fori_loop(0, 11, down_tile, 0)

    sd = Sum(p, cp, dd.at[p.c], rxd, rzd, 6, rcd, dd.at[1 - p.c])
    s0 = Sum(p, cp, d0.at[p.c], rx0, None, 2, vgu.at[:, :, :, 0:32, 0:1408], d0.at[1 - p.c])
    s1 = Sum(p, cp, d1.at[p.c], None, None, 2, vgu.at[:, :, :, 0:32, 1408:2816], d1.at[1 - p.c])
    down_half(1 - p.c)
    sd.start()
    down_half(p.c)
    gs = []
    for n in range(4):
        out = dot_nt(dgu[...], vgu[n].reshape(512, 2816))
        cols = pl.ds(n * 512, 512)
        gpart[:, :, cols] = out.astype(bf).reshape(4, 128, 512)
        gs += [cp.push(gpart.at[lax.rem(p.y + k, 4), :, cols], recv_g.at[k - 1, :, cols], p.at(dy=k)) for k in (1, 3, 2)]
        if n == 0:
            sd.stage_x()
    for c in sum(ux + uc, []):
        cp.sent(c)
    pl.semaphore_signal(ready, inc=1, device_id=sib, device_id_type=pl.DeviceIdType.MESH)

    def up_tile(first, d, start, stop):
        def body(i, _):
            rows = pl.ds(pl.multiple_of(i * 256, 256), 256)
            out = dot_tn(ent[:, :, rows].reshape(512, 256), dgu[:, first:first + 1408]).astype(bf).reshape(4, 2, 32, 1408)
            d[0, i // 2, lax.rem(i, 2)] = out[:, 0]
            d[1, i // 2, lax.rem(i, 2)] = out[:, 1]
            return 0
        lax.fori_loop(start, stop, body, 0)

    up_tile(0, d0, 0, 4)
    pl.semaphore_wait(ready, 1)
    s0.start(0, 2)
    up_tile(0, d0, 4, 8)
    s0.start(2, 4)
    up_tile(1408, d1, 0, 4)
    s0.stage_x()
    up_tile(1408, d1, 4, 8)
    s1.start()
    sd.stage_z()

    def result(n, _):
        cols = pl.ds(pl.multiple_of(n * 512, 512), 512)
        out = jnp.dot(hid[...], vd[:, cols], preferred_element_type=f)
        ent[:, :, cols] = out.astype(bf).reshape(4, 128, 512)
        return 0

    for c in es.far:
        cp.sent(c)
    lax.fori_loop(0, 4, result, 0)
    keeps = [pltpu.make_async_copy(ent, rpart, lsem.at[1])]
    keeps[0].start()
    for c in gs:
        c.wait_recv()
    for c in rest:
        c.wait()
    sums[...] = jnp.zeros_like(sums)

    def block(i, _):
        r = pl.ds(pl.multiple_of(i * ROWS, ROWS), ROWS)
        g = gpart[p.y, r].astype(f) + recv_g[0, r].astype(f) + recv_g[1, r].astype(f) + recv_g[2, r].astype(f)
        m, inv = norm_rows(mid[r])
        sums[0:1] += jnp.sum(g * m, axis=0, keepdims=True)
        sums[1:2] += jnp.sum(g, axis=0, keepdims=True)
        e = g * gains[2:3, :]
        out = cot[r].astype(f) + inv * (e - jnp.mean(e, axis=-1, keepdims=True) - m * jnp.mean(e * m, axis=-1, keepdims=True))
        gmid[r] = out
        low[r] = out.astype(bf)
        return 0

    lax.fori_loop(0, 128 // ROWS, block, 0)
    for a, b in ((gmid, gmid_out), (low, low_out), (sums, sums_out)):
        keeps.append(pltpu.make_async_copy(a, b, lsem.at[1 + len(keeps)]))
        keeps[-1].start()
    s1.stage_core()
    keeps.append(pltpu.make_async_copy(d1.at[p.c], h1, lsem.at[1 + len(keeps)]))
    keeps[-1].start()
    keeps.append(pltpu.make_async_copy(sd.stage_sum(), jd, lsem.at[1 + len(keeps)]))
    keeps[-1].start()
    s0.stage_own()
    keeps.append(pltpu.make_async_copy(d0.at[p.c, :, p.xl], i0, lsem.at[1 + len(keeps)]))
    keeps[-1].start()
    cp.finish()
    for c in keeps:
        c.wait()


def second_step(ggu, gd, ent, cots, mid, cot, gains):
    f, bf = jnp.float32, jnp.bfloat16
    S = jax.ShapeDtypeStruct
    hbm, vm = pl.BlockSpec(memory_space=pl.ANY), pl.BlockSpec(memory_space=pltpu.VMEM)
    V = pltpu.VMEM
    return pl.pallas_call(
        second_kernel,
        out_shape=(S((4, 128, 2048), bf), S((128, 2048), f), S((128, 2048), bf), S((8, 2048), f),
                   S((11, 16, 1024), bf), S((4, 4, 32, 1408), bf), S((4, 2, 4, 32, 1408), bf)),
        in_specs=[hbm] * 7, out_specs=(hbm,) * 7,
        scratch_shapes=[
            V((4, 2, 4, 64, 2816), bf), V((1408, 2048), bf), V((4, 128, 2048), bf), V((4, 128, 2048), bf),
            V((512, 1408), bf), V((512, 2816), bf), V((4, 128, 2048), bf), V((3, 128, 2048), bf),
            V((2, 4, 2, 11, 16, 1024), bf), V((2, 4, 2, 4, 32, 1408), bf), V((2, 4, 2, 4, 32, 1408), bf),
            V((4, 2, 11, 16, 1024), bf), V((4, 11, 16, 1024), bf), V((3, 11, 16, 1024), bf), V((4, 4, 32, 1408), bf),
            V((128, 2048), f), V((128, 2048), bf), V((8, 2048), f), V((128, 2048), f), V((128, 2048), bf), V((8, 2048), f),
            pltpu.SemaphoreType.DMA((40,)), pltpu.SemaphoreType.DMA((40,)), pltpu.SemaphoreType.DMA((12,)),
            pltpu.SemaphoreType.REGULAR],
        compiler_params=pltpu.CompilerParams(collective_id=3, has_side_effects=True, vmem_limit_bytes=64 * 2**20 - 2**18),
        name="second_step",
    )(ggu, gd, ent, cots, mid, cot, gains)


class Finish:
    def __init__(self, p, cp, here, rxh, via, total, out, lsem, plane, unit=32):
        self.via, self.cut = via, (here.shape[0] + 1) // 2
        self.unit = unit
        self.p, self.cp, self.here, self.rxh, self.total, self.out, self.lsem, self.plane = p, cp, here, rxh, total, out, lsem, plane

    def stage_xh(self):
        p, k, n = self.p, self.cut, self.here.shape[0]
        self.steps = [self.cp.push(self.here.at[0:k], self.via.at[0:k], p.at(dx=1)),
                      self.cp.push(self.here.at[k:n], self.via.at[k:n], p.at(dx=-1))]

    def stage_relay(self):
        p, k, n = self.p, self.cut, self.here.shape[0]
        self.steps[0].wait_recv()
        last = [self.cp.push(self.via.at[0:k], self.rxh.at[0:k], p.at(dx=1))]
        self.steps[1].wait_recv()
        self.last_xh = last + [self.cp.push(self.via.at[k:n], self.rxh.at[k:n], p.at(dx=-1))]

    def stage_y(self):
        p, cp, out = self.p, self.cp, self.out
        for c in self.last_xh:
            c.wait_recv()
        add_into(self.total, (self.here, self.rxh))
        if self.plane:
            there = out.at[..., pl.ds(pl.multiple_of(p.c * 1024, 1024), 1024)]
            self.own = pltpu.make_async_copy(self.total, there, self.lsem)
            self.own.start()
            self.ys = [cp.push(self.total, there, p.at(dc=1))]
        else:
            half = pl.ds(pl.multiple_of(p.c * self.unit, self.unit), self.unit)
            self.own = pltpu.make_async_copy(self.total.at[p.y], out.at[p.y, half], self.lsem)
            self.own.start()
            self.ys = [cp.push(self.total.at[lax.rem(p.y + d, 4)], out.at[p.y, half], p.at(dy=d)) for d in (1, 3, 2)]

    def stage_c(self):
        p, out = self.p, self.out
        for c in self.ys:
            c.wait_recv()
        self.own.wait()
        self.last = []
        if not self.plane:
            half = pl.ds(pl.multiple_of(p.c * self.unit, self.unit), self.unit)
            self.last = [self.cp.push(out.at[:, half], out.at[:, half], p.at(dc=1))]

    def finish(self):
        for c in self.last:
            c.wait_recv()


def third_kernel(low, go, gq, e1, qkv, prb, mix, tab, rpart, mid_in, tok_in, gmid_in, gains_in, sums_in, jd, i0, h1,
                 act_out, ing_out, od, o0, o1, oq0, oq1, oo, os,
                 vgml, vo, vq, ve, vqkv, vprb, vmix, vtab, gp, gpart, recv_g, recv_r, own_r, wide,
                 mid, tok, gmid, gains, sums, act, ing,
                 vjd, rxd, ved, td, vi0, rz0, rx0, ve0, t0, vh1, rxx1, rz1, rx1, ve1, t1,
                 dq0, rcq0, rxq0, rzq0, rxhq0, vq0, tq0, dq1, rcq1, rxq1, rzq1, rxhq1, vq1, tq1,
                 dw, rco, rxo, rzo, rxho, veo, to, ds, rcs, rxs, rzs, rxhs, ves, ts,
                 send, recv, lsem):
    p = Place()
    f, bf = jnp.float32, jnp.bfloat16
    pairs_in = [(low, vgml.at[p.y]), (h1, vh1), (i0, vi0), (go, vo), (qkv, vqkv), (prb, vprb), (tab, vtab),
                (jd, vjd), (e1, ve), (mix, vmix), (gq, vq), (rpart.at[p.y], own_r),
                (mid_in, mid), (tok_in, tok), (gmid_in, gmid), (gains_in, gains), (sums_in, sums)]
    loads = [pltpu.make_async_copy(a, b, lsem.at[i]) for i, (a, b) in enumerate(pairs_in)]
    for c in loads[:7]:
        c.start()
    barrier(peers(p))
    cp = Copies(send, recv)
    ls = Spread(p, cp, low, vgml)
    ls.start()
    s0 = Sum(p, cp, None, None, rz0, 2)
    s1 = Sum(p, cp, vh1, rxx1, rz1, 2)
    fd = Finish(p, cp, vjd, rxd, ved, td, od, lsem.at[18], True)
    loads[1].wait()
    s1.stage_x()
    loads[2].wait()
    s0.push_z(vi0)
    for c in loads[7:]:
        c.start()
    loads[0].wait()
    for c in loads[3:7]:
        c.wait()

    def attend(i):
        gm = dot_nt(vgml[i], vo[...].reshape(512, 2048)).astype(bf)
        cosine, sine = vtab[i, 0], -vtab[i, 1]
        for n in range(4):
            a, b, c = (slice(n * 384 + k * 128, n * 384 + (k + 1) * 128) for k in range(3))
            q, k, v = vqkv[i, :, a], vqkv[i, :, b], vqkv[i, :, c]
            prob = vprb[i, n]
            g = stack_heads(gm[:, n * 128:(n + 1) * 128])
            gv = dot_tn(prob.astype(bf), g)
            gprob = dot_nt(g, v)
            gs = (prob * (gprob - jnp.sum(prob * gprob, axis=-1, keepdims=True))).astype(bf)
            gq_ = merge_heads(jnp.dot(gs, k, preferred_element_type=f)) * SCALE
            gk = dot_tn(gs, stack_heads(q)) * SCALE
            gp[i, :, a] = turn(gq_, cosine, sine).astype(bf)
            gp[i, :, b] = turn(gk, cosine, sine).astype(bf)
            gp[i, :, c] = gv.astype(bf)

    attend(p.y)
    loads[7].wait()
    ls.relay(0)
    ls.relay(1)
    attend(lax.rem(p.y + 3, 4))
    fd.stage_xh()
    attend(lax.rem(p.y + 1, 4))
    f0 = Finish(p, cp, s0.stage_sum(), rx0, ve0, t0, o0, lsem.at[19], False)
    f0.stage_xh()
    s1.stage_z()
    ls.finish()
    attend(lax.rem(p.y + 2, 4))
    fd.stage_relay()
    loads[8].wait()

    def qkv_tile(first, dq):
        def body(i, _):
            rows = pl.ds(pl.multiple_of(i * 256, 256), 256)
            out = dot_tn(ve[:, :, rows].reshape(512, 256), gp[:, :, first:first + 768].reshape(512, 768))
            out = out.astype(bf).reshape(4, 2, 32, 768)
            dq[0, i // 2, lax.rem(i, 2)] = out[:, 0]
            dq[1, i // 2, lax.rem(i, 2)] = out[:, 1]
            return 0
        lax.fori_loop(0, 8, body, 0)

    qkv_tile(0, dq0)
    sq0 = Sum(p, cp, dq0.at[p.c], rxq0, rzq0, 2, rcq0, dq0.at[1 - p.c])
    sq0.start()
    f0.stage_relay()
    qkv_tile(768, dq1)
    sq1 = Sum(p, cp, dq1.at[p.c], rxq1, rzq1, 2, rcq1, dq1.at[1 - p.c])
    sq1.start()
    sq0.stage_x()
    for c in loads[9:]:
        c.wait()
    gs = []
    for n in range(4):
        out = dot_nt(gp[...].reshape(512, 1536), vq[n].reshape(512, 1536))
        cols = pl.ds(n * 512, 512)
        gpart[:, :, cols] = out.astype(bf).reshape(4, 128, 512)
        gs += [cp.push(gpart.at[lax.rem(p.y + k, 4), :, cols], recv_g.at[k - 1, :, cols], p.at(dy=k)) for k in (1, 3, 2)]

    def out_tile(h, _):
        cols = pl.ds(pl.multiple_of(h * 512, 512), 512)
        out = dot_tn(vmix[...].reshape(512, 512), vgml[:, :, cols].reshape(512, 512)).astype(bf)
        dw[h // 2, :, :, :, pl.ds(pl.multiple_of(lax.rem(h, 2) * 512, 512), 512)] = out.reshape(4, 2, 64, 512)
        return 0

    lax.fori_loop(0, 4, out_tile, 0)
    so = Sum(p, cp, dw.at[p.c], rxo, rzo, 32, rco, dw.at[1 - p.c])
    so.start()
    sq1.stage_x()

    rows = []
    for k in range(3):
        for n in range(4):
            first = n * 384 + k * 128
            rows.append(jnp.sum(gp[:, :, first:first + 128].reshape(512, 128).astype(f), axis=0, keepdims=True))
    rows = jnp.concatenate(rows + [jnp.zeros((4, 128), f)], axis=0).astype(bf)
    for i in range(8):
        for y in range(4):
            ds[1, i // 2, i % 2, y] = rows
    so.stage_x()
    fd.stage_y()
    sq0.stage_z()
    sq1.stage_z()
    so.stage_z()
    f1 = Finish(p, cp, s1.stage_sum(), rx1, ve1, t1, o1, lsem.at[20], False)
    f1.stage_xh()
    f0.stage_y()
    wide[...] = jnp.zeros_like(wide)
    wide[2:4] = sums[0:2]
    for c in gs:
        c.wait_recv()

    def block(i, _):
        r = pl.ds(pl.multiple_of(i * ROWS, ROWS), ROWS)
        g = gpart[p.y, r].astype(f) + recv_g[0, r].astype(f) + recv_g[1, r].astype(f) + recv_g[2, r].astype(f)
        m, inv = norm_rows(tok[r].astype(f))
        wide[0:1] += jnp.sum(g * m, axis=0, keepdims=True)
        wide[1:2] += jnp.sum(g, axis=0, keepdims=True)
        e = g * gains[0:1, :]
        out = gmid[r] + inv * (e - jnp.mean(e, axis=-1, keepdims=True) - m * jnp.mean(e * m, axis=-1, keepdims=True))
        ing[r] = out.astype(bf)
        return 0

    lax.fori_loop(0, 128 // ROWS, block, 0)
    keeps = [pltpu.make_async_copy(ing, ing_out, lsem.at[1])]
    keeps[0].start()
    for i in range(16):
        z, xl, y = i // 4, (i // 2) % 2, (i % 2) * 2
        piece = wide[:, i * 128:(i + 1) * 128]
        ds[0, z, xl, y] = piece.astype(bf)
        ds[0, z, xl, y + 1] = pltpu.roll(piece, 64, 1).astype(bf)
    ss = Sum(p, cp, ds.at[p.c], rxs, rzs, 2, rcs, ds.at[1 - p.c])
    ss.start()
    rs = [cp.push(rpart.at[lax.rem(p.y + d, 4)], recv_r.at[d - 1], p.at(dy=d)) for d in (1, 3, 2)]
    ss.stage_x()
    fq0 = Finish(p, cp, sq0.stage_sum(), rxhq0, vq0, tq0, oq0, lsem.at[22], False)
    fq0.stage_xh()
    f1.stage_relay()
    fq1 = Finish(p, cp, sq1.stage_sum(), rxhq1, vq1, tq1, oq1, lsem.at[0], False)
    fq1.stage_xh()
    fq0.stage_relay()
    ss.stage_z()
    fo = Finish(p, cp, so.stage_sum(), rxho, veo, to, oo, lsem.at[21], True)
    fo.stage_xh()
    fq1.stage_relay()
    f1.stage_y()
    fs = Finish(p, cp, ss.stage_sum(), rxhs, ves, ts, os, lsem.at[23], False, 16)
    fs.stage_xh()
    fo.stage_relay()
    fq0.stage_y()
    fd.stage_c()
    f0.stage_c()
    fs.stage_relay()
    for c in rs:
        c.wait_recv()

    def final(i, _):
        r = pl.ds(pl.multiple_of(i * ROWS, ROWS), ROWS)
        act[r] = (mid[r] + own_r[r].astype(f) + recv_r[0, r].astype(f) + recv_r[1, r].astype(f) + recv_r[2, r].astype(f)).astype(bf)
        return 0

    lax.fori_loop(0, 128 // ROWS, final, 0)
    keeps.append(pltpu.make_async_copy(act, act_out, lsem.at[2]))
    keeps[1].start()
    fq1.stage_y()
    fo.stage_y()
    fs.stage_y()
    f1.stage_c()
    fq0.stage_c()
    fq1.stage_c()
    fo.stage_c()
    fs.stage_c()
    for g in (fd, f0, f1, fq0, fq1, fo, fs):
        g.finish()
    cp.finish()
    for c in keeps:
        c.wait()


def third_step(*args):
    f, bf = jnp.float32, jnp.bfloat16
    S = jax.ShapeDtypeStruct
    hbm, vm = pl.BlockSpec(memory_space=pl.ANY), pl.BlockSpec(memory_space=pltpu.VMEM)
    V = pltpu.VMEM

    def sums(tail):
        return [V((2, 4, 2) + tail, bf), V((4, 2) + tail, bf), V((4,) + tail, bf), V((3,) + tail, bf), V(tail, bf), V(tail, bf), V(tail, bf)]

    return pl.pallas_call(
        third_kernel,
        out_shape=(S((128, 2048), bf), S((128, 2048), bf), S((11, 16, 2048), bf), S((4, 64, 1408), bf), S((4, 64, 1408), bf),
                   S((4, 64, 768), bf), S((4, 64, 768), bf), S((64, 2048), bf), S((4, 32, 128), bf)),
        in_specs=[hbm] * 17, out_specs=(hbm,) * 9,
        scratch_shapes=[
            V((4, 128, 2048), bf), V((4, 2, 64, 2048), bf), V((4, 2, 4, 64, 1536), bf), V((4, 128, 2048), bf),
            V((4, 128, 1536), bf), V((4, 4, 256, 128), f), V((4, 128, 512), bf), V((4, 2, 128, 128), f),
            V((4, 128, 1536), bf), V((4, 128, 2048), bf), V((3, 128, 2048), bf), V((3, 128, 2048), bf),
            V((128, 2048), bf), V((16, 2048), f),
            V((128, 2048), f), V((128, 2048), bf), V((128, 2048), f), V((8, 2048), f), V((8, 2048), f), V((128, 2048), bf), V((128, 2048), bf),
            V((11, 16, 1024), bf), V((11, 16, 1024), bf), V((11, 16, 1024), bf), V((11, 16, 1024), bf),
            V((4, 4, 32, 1408), bf), V((3, 4, 32, 1408), bf), V((4, 32, 1408), bf), V((4, 32, 1408), bf), V((4, 32, 1408), bf),
            V((4, 2, 4, 32, 1408), bf), V((4, 4, 32, 1408), bf), V((3, 4, 32, 1408), bf), V((4, 32, 1408), bf), V((4, 32, 1408), bf), V((4, 32, 1408), bf)]
        + sums((4, 32, 768)) * 2 + sums((64, 1024)) + sums((4, 16, 128))
        + [pltpu.SemaphoreType.DMA((110,)), pltpu.SemaphoreType.DMA((110,)), pltpu.SemaphoreType.DMA((24,))],
        compiler_params=pltpu.CompilerParams(collective_id=4, has_side_effects=True, vmem_limit_bytes=62 * 2**20),
        name="third_step",
    )(*args)


def layout_kernel(oq0_in, oq1_in, o0_in, o1_in, oo_in, od_in, os_in, act_in, ing_in, act, ing, qkv_out, out_out, gate_out, up_out, down_out, small,
                  oq0, oq1, o0, o1, oo, od, os, vact, ving, qkv, out, gate, up, down, sems):
    f = jnp.float32
    copies = ((oq0_in, oq0), (oq1_in, oq1), (o0_in, o0), (o1_in, o1), (oo_in, oo), (od_in, od), (os_in, os), (act_in, vact), (ing_in, ving))
    copies = [pltpu.make_async_copy(a, b, sems.at[i]) for i, (a, b) in enumerate(copies)]
    for c in copies:
        c.start()
    keeps = []

    def keep(src, dst):
        keeps.append(pltpu.make_async_copy(src, dst, sems.at[len(keeps) + 9]))
        keeps[-1].start()

    copies[0].wait()
    copies[1].wait()
    for g in range(48):
        k, h = g // 16, 2 * (g % 16)
        pieces = []
        for m in range(2):
            head = h + m
            pieces.append((m * 64, m * 64 + 64, head % 4, (head // 8) * 384 + k * 128 + ((head // 4) % 2) * 64))
        def load(j, t):
            src, at = (oq0, t) if t < 6 else (oq1, t - 6)
            return src[j, :, at * 128:(at + 1) * 128].astype(f)
        qkv[:, g * 128:(g + 1) * 128] = moved_lanes(pieces, load)
    keep(qkv, qkv_out)
    copies[2].wait()
    copies[3].wait()
    for n, dst in enumerate((gate, up)):
        def load(j, t):
            t = 2 * t + n
            src, at = (o0, t) if t < 11 else (o1, t - 11)
            return src[j, :, at * 128:(at + 1) * 128].astype(f)
        for g in range(44):
            dst[:, g * 128:(g + 1) * 128] = moved_lanes(shard_pieces(g), load)
        keep(dst, (gate_out, up_out)[n])
    for c in copies[4:]:
        c.wait()
    keep(vact, act)
    keep(ving, ing)
    out[...] = oo[...].astype(f)
    keep(out, out_out)
    down[...] = od[...].reshape(176, 2048).astype(f)
    keep(down, down_out)
    norms = os[0, 0:16].astype(f) + os[1, 0:16].astype(f) + os[2, 0:16].astype(f) + os[3, 0:16].astype(f)
    small[0:4] = norms[0:4]
    shard = (lax.axis_index("z") * 2 + lax.axis_index("xl")) * 4 + lax.axis_index("y")
    row = lax.broadcasted_iota(jnp.int32, (16, 128), 0)
    lane = lax.broadcasted_iota(jnp.int32, (16, 128), 1)
    for m in range(3):
        total = jnp.zeros((16, 128), f)
        for j in range(4):
            place = (row // 4) * 32 + (lax.rem(row, 4) * 2 + lane // 64) * 4 + j
            total = total + jnp.where((place == shard * 3 + m) & (row < 12), os[j, 16:32].astype(f), 0.0)
        total = jnp.sum(total, axis=0, keepdims=True)
        total = total + pltpu.roll(jnp.broadcast_to(total, (8, 128)), 64, 1)[0:1]
        small[4 + m:5 + m] = total
    small[7:8] = jnp.zeros((1, 128), f)
    for c in keeps:
        c.wait()


def layout_step(*args):
    f, bf = jnp.float32, jnp.bfloat16
    S = jax.ShapeDtypeStruct
    hbm, vm = pl.BlockSpec(memory_space=pl.ANY), pl.BlockSpec(memory_space=pltpu.VMEM)
    V = pltpu.VMEM
    return pl.pallas_call(
        layout_kernel,
        out_shape=(S((128, 2048), bf), S((128, 2048), bf), S((64, 6144), f), S((64, 2048), f), S((64, 5632), f), S((64, 5632), f),
                   S((176, 2048), f), S((8, 128), f)),
        in_specs=[hbm] * 9, out_specs=(hbm,) * 7 + (vm,),
        scratch_shapes=[V((4, 64, 768), bf), V((4, 64, 768), bf), V((4, 64, 1408), bf), V((4, 64, 1408), bf), V((64, 2048), bf),
                        V((11, 16, 2048), bf), V((4, 32, 128), bf), V((128, 2048), bf), V((128, 2048), bf), V((64, 6144), f), V((64, 2048), f), V((64, 5632), f),
                        V((64, 5632), f), V((176, 2048), f), pltpu.SemaphoreType.DMA((16,))],
        compiler_params=pltpu.CompilerParams(vmem_limit_bytes=60 * 2**20),
        name="layout_step",
    )(*args)


def small_parameters(ln1_gain, ln1_bias, ln2_gain, ln2_bias, qkv_bias):
    f, bf = jnp.float32, jnp.bfloat16
    shard = (lax.axis_index("z") * 2 + lax.axis_index("xl")) * 4 + lax.axis_index("y")
    norms = jnp.pad(jnp.stack([ln1_gain, ln1_bias, ln2_gain, ln2_bias]), ((0, 12), (0, 64)))
    row = lax.broadcasted_iota(jnp.int32, (4, 16, 128), 1)
    lane = lax.broadcasted_iota(jnp.int32, (4, 16, 128), 2)
    place = (row // 4) * 32 + ((row % 4) * 2 + lane // 64) * 4 + lax.broadcasted_iota(jnp.int32, (4, 16, 128), 0)
    own = qkv_bias.reshape(3, 64)
    own = jnp.concatenate([own, own], axis=1)
    bias = jnp.zeros((4, 16, 128), bf)
    for k in range(3):
        bias = jnp.where((place == shard * 3 + k) & (row < 12), own[k], bias)
    return jnp.concatenate([jnp.broadcast_to(norms[None], (4, 16, 128)), bias], axis=1)


def local(tokens, segment_ids, cotangent, ln1_gain, ln1_bias, qkv_weight, qkv_bias, out_weight,
          ln2_gain, ln2_bias, gate_weight, up_weight, down_weight):
    small = small_parameters(ln1_gain, ln1_bias, ln2_gain, ln2_bias, qkv_bias)
    cots, gq, ggu, go, gd, e1, qkv, prb, mix, tab, gains, mid, ent = first_step(
        tokens, cotangent, segment_ids, qkv_weight, small, gate_weight, up_weight, out_weight, down_weight)
    rpart, gmid, low, sums, jd, i0, h1 = second_step(ggu, gd.reshape(1408, 2048), ent, cots, mid, cotangent, gains)
    act, ing, od, o0, o1, oq0, oq1, oo, os = third_step(
        low, go, gq, e1, qkv, prb, mix, tab, rpart, mid, tokens, gmid, gains, sums, jd, i0, h1)
    act, ing, qkv_grad, out_grad, gate_grad, up_grad, down_grad, small = layout_step(
        oq0, oq1, o0, o1, oo, od, os, act, ing)
    return (act, ing, small[0, :64], small[1, :64], qkv_grad, small[4:7, :64].reshape(192), out_grad,
            small[2, :64], small[3, :64], gate_grad, up_grad, down_grad)


def solution(mesh):
    fine = Mesh(mesh.devices.reshape(2, 2, 4, 2, 4), AXES)
    whole, rows = P(AXES, None), P(("z", "xl", "y"), None)
    vector = P(("z", "xl", "y"))
    return jax.shard_map(
        local, mesh=fine,
        in_specs=(whole, whole, whole, vector, vector, rows, vector, rows, vector, vector, rows, rows, rows),
        out_specs=(whole, whole, vector, vector, rows, vector, rows, vector, vector, rows, rows, rows),
        check_vma=False,
    )
```

```python
import functools
import jax, jax.numpy as jnp
from jax import lax
from jax.sharding import PartitionSpec as P, Mesh
from jax.experimental import pallas as pl
from jax.experimental.pallas import tpu as pltpu

AXES = ("xh", "c", "z", "xl", "y")


class Place:
    def __init__(self):
        self.xh, self.c, self.z, self.xl, self.y = (lax.axis_index(a) for a in AXES)
        self.x = self.xh * 2 + self.xl

    def at(self, dx=0, dy=0, dz=0, dc=0):
        x = lax.rem(self.x + dx + 4, 4) if dx else self.x
        return (
            x // 2 if dx else self.xh,
            lax.rem(self.c + dc, 2) if dc else self.c,
            lax.rem(self.z + dz + 4, 4) if dz else self.z,
            lax.rem(x, 2) if dx else self.xl,
            lax.rem(self.y + dy + 4, 4) if dy else self.y,
        )


def barrier(targets):
    sem = pltpu.get_barrier_semaphore()
    for target in targets:
        pl.semaphore_signal(sem, inc=1, device_id=target, device_id_type=pl.DeviceIdType.MESH)
    pl.semaphore_wait(sem, len(targets))


class Copies:
    def __init__(self, send, recv):
        self.send, self.recv, self.used, self.all = send, recv, 0, []

    def push(self, src, dst, target):
        copy = pltpu.make_async_remote_copy(
            src_ref=src, dst_ref=dst, send_sem=self.send.at[self.used],
            recv_sem=self.recv.at[self.used], device_id=target, device_id_type=pl.DeviceIdType.MESH)
        self.used += 1
        self.all.append(copy)
        copy.start()
        return copy

    def sent(self, copy):
        copy.wait_send()
        self.all = [c for c in self.all if c is not copy]

    def finish(self):
        for copy in self.all:
            copy.wait_send()


def add_into(out, parts):
    total = parts[0][...].astype(jnp.float32)
    for part in parts[1:]:
        total = total + part[...].astype(jnp.float32)
    out[...] = total.astype(out.dtype)


def peers(p):
    return [p.at(dy=d) for d in (1, 2, 3)] + [p.at(dz=d) for d in (1, 2, 3)] + [p.at(dx=d) for d in (1, 2, -1)] + [p.at(dc=1)]


class Gather:
    def __init__(self, p, cp, src, dst, lsem, cols=None, cut=None, unit=32):
        self.p, self.cp, self.src, self.dst, self.lsem, self.cut = p, cp, src, dst, lsem, cut
        self.cols = cols
        if cut is None:
            self.half = pl.ds(pl.multiple_of(p.c * unit, unit), unit)
        else:
            self.half = pl.ds(pl.multiple_of(p.c * 1024, 1024), 1024)

    def start(self):
        p, src, dst, half = self.p, self.src, self.dst, self.half
        if self.cut is None:
            cols = self.cols
            here = dst.at[p.z, p.xl, p.y, half, cols]
            self.local = pltpu.make_async_copy(src.at[p.y, half, cols], here, self.lsem)
            self.local.start()
            self.ys = [self.cp.push(src.at[lax.rem(p.y + d, 4), half, cols], here, p.at(dy=d)) for d in (1, 3, 2)]
        else:
            here = dst.at[p.z, p.xl, :, half]
            self.local = pltpu.make_async_copy(src.at[:, half], here, self.lsem)
            self.local.start()
            self.zs = [self.cp.push(src.at[:, half], here, p.at(dz=d)) for d in (1, 3, 2)]

    def stage_y(self):
        self.local.wait()
        for c in self.ys:
            c.wait_recv()

    def stage_z(self):
        p = self.p
        self.stage_y()
        here = self.dst.at[p.z, p.xl, :, self.half, self.cols]
        self.zs = [self.cp.push(here, here, p.at(dz=d)) for d in (1, 3, 2)]

    def parts(self, xl):
        g = self.dst
        if self.cut is not None:
            k, r = self.cut, g.shape[2]
            return g.at[:, xl, 0:k, self.half], g.at[:, xl, k:r, self.half], g.at[:, xl, :, self.half]
        return (g.at[:, xl, 0:2, self.half, self.cols], g.at[:, xl, 2:4, self.half, self.cols],
                g.at[:, xl, :, self.half, self.cols])

    def stage_x(self):
        p = self.p
        if self.cut is not None:
            self.local.wait()
        for c in self.zs:
            c.wait_recv()
        lo, hi, full = self.parts(p.xl)
        self.xs = [self.cp.push(lo, lo, p.at(dx=1)), self.cp.push(hi, hi, p.at(dx=-1))]
        self.cs = [self.cp.push(full, full, p.at(dc=1))]

    def stage_c(self):
        p = self.p
        lo, hi, full = self.parts(1 - p.xl)
        self.xs[0].wait_recv()
        self.cs.append(self.cp.push(lo, lo, p.at(dc=1)))
        self.xs[1].wait_recv()
        self.cs.append(self.cp.push(hi, hi, p.at(dc=1)))

    def finish(self):
        for c in self.cs:
            c.wait_recv()


class Spread:
    def __init__(self, p, cp, src, dst):
        self.p, self.cp, self.src, self.dst = p, cp, src, dst

    def start(self):
        p = self.p
        self.near = [self.cp.push(self.src, self.dst.at[p.y], p.at(dy=d)) for d in (1, 3)]

    def relay(self, k):
        p = self.p
        self.near[k].wait_recv()
        half = self.dst.at[lax.rem(p.y + (3, 1)[k], 4), pl.ds(64 * k, 64)]
        copy = self.cp.push(half, half, p.at(dy=(1, 3)[k]))
        self.far = [copy] if k == 0 else self.far + [copy]

    def finish(self):
        for c in self.far:
            c.wait_recv()


class RingSum:
    def __init__(self, p, cp, part, recv, via):
        self.p, self.cp, self.part, self.recv, self.via, self.away = p, cp, part, recv, via, []
        self.lower, self.upper = pl.ds(0, 64), pl.ds(64, 64)
        self.next, self.far, self.prev = (lax.rem(p.y + k, 4) for k in (1, 2, 3))

    def start(self, first, width):
        cols = pl.ds(first, width)
        self.away.append([self.cp.push(self.part.at[self.far, half, cols], self.via.at[k, :, cols], self.p.at(dy=dy))
                          for k, half, dy in ((0, self.lower, 1), (1, self.upper, -1))])

    def near(self):
        self.ins = [self.cp.push(self.part.at[self.next, self.upper], self.recv.at[0, self.upper], self.p.at(dy=1)),
                    self.cp.push(self.part.at[self.prev, self.lower], self.recv.at[1, self.lower], self.p.at(dy=-1))]

    def relay(self):
        for k, half, seq, dy in ((0, self.lower, self.next, 1), (1, self.upper, self.prev, -1)):
            for pair in self.away:
                pair[k].wait_recv()
            here = self.part.at[seq, half]
            add_into(here, (here, self.via.at[k]))
            self.ins.append(self.cp.push(here, self.recv.at[k, half], self.p.at(dy=dy)))

    def finish(self):
        for c in self.ins:
            c.wait_recv()


ROWS = 16
norm_epsilon = 1e-05
masked_score = -1000000000.0
HEADS = 8
HEAD_DIM = 64
ROT = 16
SCALE = HEAD_DIM ** (-0.5)


def norm_rows(m):
    m = m - jnp.mean(m, axis=-1, keepdims=True)
    inv = lax.rsqrt(jnp.mean(m * m, axis=-1, keepdims=True) + norm_epsilon)
    return m * inv, inv


def allowed_of(seg_row):
    keys = jnp.broadcast_to(seg_row, (128, 128))
    queries = jnp.transpose(keys)
    q = lax.broadcasted_iota(jnp.int32, (128, 128), 0)
    k = lax.broadcasted_iota(jnp.int32, (128, 128), 1)
    same = keys == queries
    places = jnp.sum(jnp.where(same & (k < q), 1.0, 0.0), axis=-1, keepdims=True)
    return same & (k <= q), places


def turn(x, cosine, sine):
    lane = lax.broadcasted_iota(jnp.int32, (128, 128), 1)
    other = jnp.where(lax.rem(lane, 64) < 8, pltpu.roll(x, 120, 1), pltpu.roll(x, 8, 1))
    return x * cosine + other * sine


def stack_heads(x):
    lane = lax.broadcasted_iota(jnp.int32, (128, 128), 1)
    zero = jnp.zeros_like(x)
    return jnp.concatenate([jnp.where(lane < 64, x, zero), jnp.where(lane < 64, zero, x)], axis=0)


def merge_heads(x):
    lane = lax.broadcasted_iota(jnp.int32, (128, 128), 1)
    return jnp.where(lane < 64, x[:128], x[128:])


def dot_nt(a, b):
    return lax.dot_general(a, b, (((1,), (1,)), ((), ())), preferred_element_type=jnp.float32)


def dot_tn(a, b):
    return lax.dot_general(a, b, (((0,), (0,)), ((), ())), preferred_element_type=jnp.float32)


def moved_lanes(pieces, load):
    out = None
    for first, end, source, column in pieces:
        while first < end:
            group, at = divmod(column, 128)
            width = min(end - first, 128 - at)
            value = load(source, group)
            shift = (first - at) % 128
            if shift:
                value = pltpu.roll(value, shift, 1)
            if out is None:
                out = value
            else:
                lane = lax.broadcasted_iota(jnp.int32, value.shape, 1)
                out = jnp.where((lane >= first) & (lane < first + width), value, out)
            first, column = first + width, column + width
    return out


def hidden_pieces(part, group):
    pieces, at = [], 0
    while at < 128:
        block, rest = divmod(group * 128 + at, 176)
        width = min(128 - at, 176 - rest)
        pieces.append((at, at + width, 0, (4 * block + part) * 176 + rest))
        at += width
    return pieces


def shard_pieces(group):
    pieces, at = [], 0
    while at < 128:
        shard, rest = divmod(group * 128 + at, 176)
        width = min(128 - at, 176 - rest)
        pieces.append((at, at + width, shard % 4, (shard // 4) * 176 + rest))
        at += width
    return pieces


def small_parameters(p, out, g1, b1, g2, b2, bq):
    f, bf = jnp.float32, jnp.bfloat16
    shard = (p.z * 2 + p.xl) * 4 + p.y
    row = lax.broadcasted_iota(jnp.int32, (16, 128), 0)
    lane = lax.broadcasted_iota(jnp.int32, (16, 128), 1)

    def twice(v):
        v = v.astype(f).reshape(1, 64)
        return jnp.concatenate([v, v], axis=1)

    norms = jnp.zeros((16, 128), f)
    for k, v in enumerate((g1, b1, g2, b2)):
        norms = jnp.where((row == k) & (lane < 64), twice(v[...]), norms)
    for j in range(4):
        place = (row // 4) * 32 + (lax.rem(row, 4) * 2 + lane // 64) * 4 + j
        bias = jnp.zeros((16, 128), f)
        for k in range(3):
            bias = jnp.where((place == shard * 3 + k) & (row < 12), twice(bq[k * 64:(k + 1) * 64]), bias)
        out[j, 0:16] = norms.astype(bf)
        out[j, 16:32] = bias.astype(bf)


def first_kernel(tok, cot, seg, wq, g1, b1, g2, b2, bq, wg, wu, wo, wd,
                 cots, gq, ggu, go, gd, e1, qkv, prb, mix, tab, gains_out, mid_out, ent_out,
                 rq, rg, ru, sm, pq, pgu, vq, vs, vo, x, xe, segv, segs, proj, qkvb, probs, mixed, tabs, masks, part, recv_a, relay_a, own, bias, gains, mid, ent,
                 send, recv, lsem):
    p = Place()
    f, bf = jnp.float32, jnp.bfloat16
    locals_ = []

    def local(src, dst):
        copy = pltpu.make_async_copy(src, dst, lsem.at[len(locals_)])
        copy.start()
        locals_.append(copy)
        return copy

    def sem():
        locals_.append(None)
        return lsem.at[len(locals_) - 1]

    raw = [local(wq, rq), local(wg, rg), local(wu, ru), local(tok, own)]
    barrier([p.at(dy=d) for d in (1, 2, 3)] + [p.at(dz=d) for d in (1, 2, 3)] + [p.at(dx=1), p.at(dx=-1), p.at(dc=1)])
    cp = Copies(send, recv)

    def share(src, dst):
        return [local(src, dst.at[p.y])], [cp.push(src, dst.at[p.y], p.at(dy=d)) for d in (1, 3, 2)]

    q = [Gather(p, cp, pq, vq, sem(), cols=pl.ds(n * 384, 384)) for n in range(4)]
    s = Gather(p, cp, sm, vs, sem(), cols=pl.ds(0, 128), unit=16)
    u0 = Gather(p, cp, pgu, ggu, sem(), cols=pl.ds(0, 512))
    u1 = Gather(p, cp, pgu, ggu, sem(), cols=pl.ds(512, 512))
    u2 = Gather(p, cp, pgu, ggu, sem(), cols=pl.ds(1024, 512))
    u3 = Gather(p, cp, pgu, ggu, sem(), cols=pl.ds(1536, 1280))
    o = Gather(p, cp, wo, vo, sem(), cut=32)
    d = Gather(p, cp, wd, gd, sem(), cut=96)
    xs = Spread(p, cp, tok, x)
    cs = Spread(p, cp, cot, cots)

    small_parameters(p, sm, g1, b1, g2, b2, bq)
    s.start()
    segv[...] = jnp.broadcast_to(seg[...].astype(f), (8, 128))
    s_here, s_in = share(segv, segs)
    raw[0].wait()
    for n in range(4):
        for j in range(4):
            for k in range(3):
                pieces = [(0, 64, 0, k * 2048 + (8 * n + j) * 64), (64, 128, 0, k * 2048 + (8 * n + 4 + j) * 64)]
                got = moved_lanes(pieces, lambda _, g: rq[:, g * 128:(g + 1) * 128].astype(f))
                pq[j, :, n * 384 + k * 128:n * 384 + (k + 1) * 128] = got.astype(bf)
        q[n].start()
    xs.start()
    x_here = [local(tok, x.at[p.y])]
    raw[1].wait()
    raw[2].wait()
    for j in range(4):
        for t in range(11):
            for k, r in enumerate((rg, ru)):
                got = moved_lanes(hidden_pieces(j, t), lambda _, g: r[:, g * 128:(g + 1) * 128].astype(f))
                pgu[j, :, t * 256 + k * 128:t * 256 + (k + 1) * 128] = got.astype(bf)
    s.stage_z()
    q[0].stage_z()
    q[1].stage_z()
    for c in s_here:
        c.wait()
    for c in s_in:
        c.wait_recv()

    lane = lax.broadcasted_iota(jnp.int32, (128, 128), 1)
    low = lax.rem(lane, 64)

    freqs = jnp.zeros((1, 128), f)
    for k in range(ROT // 2):
        freqs = jnp.where(lax.rem(lane[0:1], ROT // 2) == k, 10000.0 ** (-2.0 * k / ROT), freqs)

    def table(i, _):
        allowed, places = allowed_of(segs[i, 0:1, :])
        masks[i] = jnp.where(allowed, 1.0, 0.0)
        angle = places * freqs
        tabs[i, 0] = jnp.where(low < ROT, jnp.cos(angle), 1.0)
        sine = jnp.sin(angle)
        tabs[i, 1] = jnp.where(low < ROT // 2, -sine, jnp.where(low < ROT, sine, 0.0))
        return 0

    lax.fori_loop(0, 4, table, 0)
    local(tabs, tab)
    s.stage_x()
    s.stage_c()
    q[0].stage_x()
    q[2].stage_z()
    s.finish()

    half_lane = lax.broadcasted_iota(jnp.int32, (8, 128), 1) < 64
    for i in range(16):
        z, xl, y = i // 4, (i // 2) % 2, (i % 2) * 2
        a = vs[z, xl, y, 0:16].astype(f)[0:8]
        b = pltpu.roll(vs[z, xl, y + 1, 0:16].astype(f)[0:8], 64, 1)
        gains[:, i * 128:(i + 1) * 128] = jnp.where(half_lane, a, b)
    total = jnp.zeros((16, 128), f)
    for i in range(32):
        total = total + vs[i // 8, (i // 4) % 2, i % 4, 16:32].astype(f)
    bias[...] = total

    local(gains, gains_out)

    def entry(i):
        def block(b, _):
            r = pl.ds(pl.multiple_of(b * ROWS, ROWS), ROWS)
            n, _inv = norm_rows(x[i, r].astype(f))
            xe[i, r] = (n * gains[0:1, :] + gains[1:2, :]).astype(bf)
            return 0
        lax.fori_loop(0, 128 // ROWS, block, 0)

    q[1].stage_x()
    q[3].stage_z()
    x_here[0].wait()
    entry(p.y)
    xs.relay(0)
    xs.relay(1)
    q[0].stage_c()
    q[2].stage_x()
    o.start()
    entry(lax.rem(p.y + 3, 4))
    q[1].stage_c()
    q[3].stage_x()
    d.start()
    entry(lax.rem(p.y + 1, 4))
    q[2].stage_c()
    u0.start()
    u1.start()
    xs.finish()
    cs.start()
    entry(lax.rem(p.y + 2, 4))
    c_here = [local(cot, cots.at[p.y])]
    local(xe, e1)

    def heads(n):
        q[n].finish()
        first = n * 384
        w = vq[:, :, :, :, first:first + 384].reshape(2048, 384)
        out = jnp.dot(xe[...].reshape(512, 2048), w, preferred_element_type=f)
        b = jnp.concatenate([bias[k * 4 + n:k * 4 + n + 1, :] for k in range(3)], axis=1)
        proj[...] = (out + b).reshape(4, 128, 384)

        def attend(i, _):
            allowed = masks[i] > 0.5
            allowed = jnp.concatenate([allowed, allowed], axis=0)
            cosine, sine = tabs[i, 0], tabs[i, 1]
            qr = turn(proj[i, :, 0:128], cosine, sine).astype(bf)
            kr = turn(proj[i, :, 128:256], cosine, sine).astype(bf)
            v = proj[i, :, 256:384].astype(bf)
            qkvb[i, :, first:first + 128] = qr
            qkvb[i, :, first + 128:first + 256] = kr
            qkvb[i, :, first + 256:first + 384] = v
            scores = dot_nt(stack_heads(qr), kr) * SCALE
            scores = jnp.where(allowed, scores, masked_score)
            expos = jnp.exp(scores - jnp.max(scores, axis=-1, keepdims=True))
            prob = expos / jnp.sum(expos, axis=-1, keepdims=True)
            probs[i, n] = prob
            got = jnp.dot(prob.astype(bf), v, preferred_element_type=f)
            mixed[i, :, n * 128:(n + 1) * 128] = merge_heads(got).astype(bf)
            return 0

        lax.fori_loop(0, 4, attend, 0)

    heads(0)
    q[3].stage_c()
    o.stage_x()
    heads(1)
    heads(2)
    o.stage_c()
    u0.stage_z()
    u1.stage_z()
    u2.start()
    u3.start()
    heads(3)
    d.stage_x()
    o.finish()
    ring = RingSum(p, cp, part, recv_a, relay_a)
    for n in range(4):
        cols = pl.ds(n * 512, 512)
        out = jnp.dot(mixed[...].reshape(512, 512), vo[:, :, :, cols].reshape(512, 512), preferred_element_type=f)
        part[:, :, cols] = out.astype(bf).reshape(4, 128, 512)
        if n % 2:
            ring.start((n - 1) * 512, 1024)
    ring.near()
    u2.stage_z()
    local(vo, go)
    local(vq, gq)
    local(qkvb, qkv)
    local(probs, prb)
    local(mixed, mix)
    u0.stage_x()
    ring.relay()
    u1.stage_x()
    u3.stage_z()
    d.stage_c()
    ring.finish()
    cs.relay(0)
    cs.relay(1)

    def block(i, _):
        r = pl.ds(pl.multiple_of(i * ROWS, ROWS), ROWS)
        m = own[r].astype(f) + part[p.y, r].astype(f) + recv_a[0, r].astype(f) + recv_a[1, r].astype(f)
        mid[r] = m
        n, _inv = norm_rows(m)
        ent[r] = (n * gains[2:3, :] + gains[3:4, :]).astype(bf)
        return 0

    raw[3].wait()
    lax.fori_loop(0, 128 // ROWS, block, 0)
    local(mid, mid_out)
    es = Spread(p, cp, ent, ent_out)
    es.start()
    local(ent, ent_out.at[p.y])
    u2.stage_x()
    u0.stage_c()
    u1.stage_c()
    cs.finish()
    u2.stage_c()
    for c in u3.zs:
        c.wait_recv()
    for g in (d, u0, u1, u2):
        g.finish()
    for c in es.near:
        c.wait_recv()
    cp.finish()
    for copy in locals_:
        if copy is not None and not any(copy is done for done in x_here + s_here + raw):
            copy.wait()


def first_step(*args):
    f, bf = jnp.float32, jnp.bfloat16
    S = jax.ShapeDtypeStruct
    hbm, vm = pl.BlockSpec(memory_space=pl.ANY), pl.BlockSpec(memory_space=pltpu.VMEM)
    V = pltpu.VMEM
    outs = (S((4, 128, 2048), bf), S((4, 2, 4, 64, 1536), bf), S((4, 2, 4, 64, 2816), bf), S((4, 2, 64, 2048), bf),
            S((4, 2, 176, 2048), bf), S((4, 128, 2048), bf), S((4, 128, 1536), bf), S((4, 4, 256, 128), f),
            S((4, 128, 512), bf), S((4, 2, 128, 128), f), S((8, 2048), f), S((128, 2048), f), S((4, 128, 2048), bf))
    return pl.pallas_call(
        first_kernel, out_shape=outs, in_specs=[hbm, hbm, vm, hbm] + [vm] * 5 + [hbm] * 4,
        out_specs=(hbm,) * 13,
        scratch_shapes=[
            V((64, 6144), bf), V((64, 5632), bf), V((64, 5632), bf), V((4, 32, 128), bf), V((4, 64, 1536), bf), V((4, 64, 2816), bf),
            V((4, 2, 4, 64, 1536), bf), V((4, 2, 4, 32, 128), bf), V((4, 2, 64, 2048), bf),
            V((4, 128, 2048), bf), V((4, 128, 2048), bf), V((8, 128), f), V((4, 8, 128), f), V((4, 128, 384), f),
            V((4, 128, 1536), bf), V((4, 4, 256, 128), f), V((4, 128, 512), bf),
            V((4, 2, 128, 128), f), V((4, 128, 128), f), V((4, 128, 2048), bf), V((2, 128, 2048), bf), V((2, 64, 2048), bf),
            V((128, 2048), bf), V((16, 128), f), V((8, 2048), f), V((128, 2048), f), V((128, 2048), bf),
            pltpu.SemaphoreType.DMA((131,)), pltpu.SemaphoreType.DMA((131,)), pltpu.SemaphoreType.DMA((28,))],
        compiler_params=pltpu.CompilerParams(collective_id=1, has_side_effects=True, vmem_limit_bytes=56 * 2**20),
        name="first_step",
    )(*args)


class Sum:
    def __init__(self, p, cp, terms, rx, rz, cut, rc=None, other=None):
        self.p, self.cp, self.h, self.other, self.rc, self.rx, self.rz, self.cut = p, cp, terms, other, rc, rx, rz, cut

    def start(self, first=0, stop=4):
        part = pl.ds(first, stop - first)
        self.core = ([] if first == 0 else self.core) + [self.cp.push(self.other.at[part], self.rc.at[part], self.p.at(dc=1))]

    def stage_core(self):
        h, rc = self.h, self.rc
        for c in self.core:
            c.wait_recv()

        def both(i, _):
            add_into(h.at[i], (h.at[i], rc.at[i]))
            return 0

        lax.fori_loop(0, 4, both, 0)

    def stage_x(self, piece=None):
        p, h, rc, k = self.p, self.h, self.rc, self.cut
        first, count = (0, 4) if piece is None else (2 * piece, 2)
        if rc is not None:
            for c in self.core if piece is None else self.core[piece:piece + 1]:
                c.wait_recv()

            def foreign(i, _):
                add_into(h.at[i, 1 - p.xl], (h.at[i, 1 - p.xl], rc.at[i, 1 - p.xl]))
                return 0

            lax.fori_loop(first, first + count, foreign, 0)
        blocks = pl.ds(first, count)
        here, there = h.at[blocks, 1 - p.xl], self.rx.at[blocks]
        if k is None:
            n = h.shape[-1] // 2
            lo, hi = (Ellipsis, pl.ds(0, n)), (Ellipsis, pl.ds(n, n))
        else:
            lo, hi = (slice(None), pl.ds(0, k)), (slice(None), pl.ds(k, h.shape[2] - k))
        self.xs = ([] if first == 0 else self.xs) + [
            self.cp.push(here.at[lo], there.at[lo], p.at(dx=1)), self.cp.push(here.at[hi], there.at[hi], p.at(dx=-1))]

    def stage_own(self):
        p, h, rc, rx = self.p, self.h, self.rc, self.rx
        for c in self.xs:
            c.wait_recv()

        def own(i, _):
            here = h.at[i, p.xl]
            add_into(here, (here, rx.at[i]) if rc is None else (here, rc.at[i, p.xl], rx.at[i]))
            return 0

        lax.fori_loop(0, 4, own, 0)

    def push_z(self, blocks):
        p = self.p
        self.blocks = blocks
        self.zs = [self.cp.push(blocks.at[lax.rem(p.z + d, 4)], self.rz.at[d - 1], p.at(dz=d)) for d in (1, 3, 2)]

    def stage_z(self):
        self.stage_own()
        self.push_z(self.h.at[:, self.p.xl])

    def stage_sum(self):
        rz = self.rz
        here = self.blocks.at[self.p.z]
        for c in self.zs:
            c.wait_recv()
        add_into(here, (here, rz.at[0], rz.at[1], rz.at[2]))
        return here


def second_kernel(ggu, gd, ents, cots, mid_in, cot_in, gains_in,
                  rpart, gmid_out, low_out, sums_out, hd, j0, i1,
                  vgu, vd, ent, cts, hid, dgu, gpart, recv_g, dd, d0, d1, rcd, rc0, rx0, rz0, rx1, relay_g, mid, cot, gains, gmid, low, sums,
                  send, recv, lsem, ready):
    p = Place()
    f, bf = jnp.float32, jnp.bfloat16
    sib = p.at(dc=1)
    near = [p.y, lax.rem(p.y + 3, 4), lax.rem(p.y + 1, 4)]
    far = [lax.rem(p.y + 2, 4)]
    own_load = [pltpu.make_async_copy(ents.at[i], ent.at[i], lsem.at[(0, 11, 12)[k]]) for k, i in enumerate(near)]
    loads = [pltpu.make_async_copy(a, b, lsem.at[1 + i]) for i, (a, b) in enumerate(((cots, cts), (gd, vd)))]
    tiles = []
    for n in range(3):
        cols = pl.ds(n * 512, 512)
        tiles.append(pltpu.make_async_copy(ggu.at[:, :, :, :, cols], vgu.at[:, :, :, :, cols], lsem.at[(3, 4, 13)[n]]))
    rest = [pltpu.make_async_copy(a, b, lsem.at[6 + i]) for i, (a, b) in enumerate(((mid_in, mid), (cot_in, cot), (gains_in, gains)))]
    for c in own_load + loads + tiles + rest:
        c.start()
    barrier([p.at(dy=d) for d in (1, 2, 3)] + [p.at(dz=d) for d in (1, 2, 3)] + [p.at(dx=1), p.at(dx=-1), sib])
    cp = Copies(send, recv)
    es = [cp.push(ents.at[near[2 - k], pl.ds(64 * (1 - k), 64)], ent.at[near[2 - k], pl.ds(64 * (1 - k), 64)], p.at(dy=(-1, 1)[k])) for k in (0, 1)]
    half = pl.ds(pl.multiple_of(p.c * 32, 32), 32)
    late = [pl.ds(1536, 512), pl.ds(2048, 768)]
    mine = [pltpu.make_async_copy(ggu.at[:, p.xl, :, half, cols], vgu.at[:, p.xl, :, half, cols], lsem.at[9 + i]) for i, cols in enumerate(late)]
    for c in mine:
        c.start()
    ux, uc = [], []

    def late_x(k):
        cols = late[k]
        ux.append([cp.push(ggu.at[:, p.xl, a:a + 2, half, cols], vgu.at[:, p.xl, a:a + 2, half, cols], p.at(dx=d)) for a, d in ((0, 1), (2, -1))])
        uc.append([cp.push(ggu.at[:, p.xl, :, half, cols], vgu.at[:, p.xl, :, half, cols], sib)])

    late_x(0)

    def late_c(k):
        for i in range(2):
            ux[k][i].wait_recv()
            there = vgu.at[:, 1 - p.xl, 2 * i:2 * i + 2, half, late[k]]
            uc[k].append(cp.push(there, there, sib))

    for c in loads:
        c.wait()

    def back_tile(first, width):
        out = dot_nt(cts[...].reshape(512, 2048), vd[pl.ds(first, width), :])
        hid[:, pl.ds(first, width)] = out.astype(bf)

    def back(n, _):
        back_tile(pl.multiple_of(n * 256, 256), 256)
        return 0

    lax.fori_loop(0, 5, back, 0)
    back_tile(1280, 128)

    def hidden_tile(first, width, seqs=None):
        w = vgu[:, :, :, :, pl.ds(2 * first, 2 * width)].reshape(2048, 2 * width)
        if seqs is None:
            a, rows = ent[...].reshape(512, 2048), [pl.ds(0, 512)]
        else:
            a, rows = jnp.concatenate([ent[i] for i in seqs], axis=0), [pl.ds(pl.multiple_of(i * 128, 128), 128) for i in seqs]
        gu = jnp.dot(a, w, preferred_element_type=f)
        size = gu.shape[0] // len(rows)
        for k in range(width // 128):
            cols = pl.ds(first + k * 128, 128)
            for m, r in enumerate(rows):
                part = gu[m * size:(m + 1) * size]
                gate, up = part[:, k * 256:k * 256 + 128], part[:, k * 256 + 128:k * 256 + 256]
                g = hid[r, cols].astype(f)
                sig = 1.0 / (1.0 + jnp.exp(-gate))
                silu = gate * sig
                hid[r, cols] = (silu * up).astype(bf)
                dgu[r, pl.ds(2 * first + k * 256, 128)] = (g * up * sig * (1.0 + gate * (1.0 - sig))).astype(bf)
                dgu[r, pl.ds(2 * first + k * 256 + 128, 128)] = (g * silu).astype(bf)

    def near_tile(n, _):
        hidden_tile(pl.multiple_of(n * 256, 256), 256, near)
        return 0

    def far_tile(n, _):
        hidden_tile(pl.multiple_of(n * 256, 256), 256, far)
        return 0

    def tile(n, _):
        hidden_tile(pl.multiple_of(n * 256, 256), 256)
        return 0

    for c in own_load:
        c.wait()
    late_x(1)
    for c in tiles + mine:
        c.wait()
    lax.fori_loop(0, 3, near_tile, 0)
    for c in es:
        c.wait_recv()
    late_c(0)
    lax.fori_loop(0, 3, far_tile, 0)
    for c in uc[0]:
        c.wait_recv()
    lax.fori_loop(3, 4, tile, 0)
    late_c(1)
    for c in uc[1]:
        c.wait_recv()
    lax.fori_loop(4, 5, tile, 0)
    hidden_tile(1280, 128)

    def down_half(h, start, stop):
        cols = pl.ds(pl.multiple_of(h * 1024, 1024), 1024)

        def down_tile(t, _):
            rows = pl.ds(pl.multiple_of(t * 128, 128), 128)
            out = dot_tn(hid[:, rows], cts[:, :, cols].reshape(512, 1024)).astype(bf)
            for k in range(8):
                g = t * 8 + k
                dd[h, g // 22, lax.rem(g // 11, 2), lax.rem(g, 11)] = out[k * 16:(k + 1) * 16]
            return 0

        lax.fori_loop(start, stop, down_tile, 0)

    def up_tile(first, d, start, stop):
        width = d.shape[-1]

        def body(i, _):
            rows = pl.ds(pl.multiple_of(i * 256, 256), 256)
            out = dot_tn(ent[:, :, rows].reshape(512, 256), dgu[:, first:first + width]).astype(bf).reshape(4, 2, 32, width)
            d[0, i // 2, lax.rem(i, 2)] = out[:, 0]
            d[1, i // 2, lax.rem(i, 2)] = out[:, 1]
            return 0
        lax.fori_loop(start, stop, body, 0)

    sd = Sum(p, cp, dd.at[p.c], None, None, None, rcd, dd.at[1 - p.c])
    s0 = Sum(p, cp, d0.at[p.c], rx0, rz0, 2, rc0, d0.at[1 - p.c])
    s1 = Sum(p, cp, d1.at[p.c], rx1, None, 2, vgu.at[:, :, :, 0:32, 1152:2816], d1.at[1 - p.c])
    up_tile(0, d0, 0, 4)
    s0.start(0, 2)
    up_tile(0, d0, 4, 8)
    s0.start(2, 4)
    ring = RingSum(p, cp, gpart, recv_g, relay_g)
    for n in range(4):
        out = dot_nt(dgu[...], vgu[n].reshape(512, 2816))
        gpart[:, :, n * 512:(n + 1) * 512] = out.astype(bf).reshape(4, 128, 512)
        if n < 2:
            s0.stage_x(n)
        if n % 2:
            ring.start((n - 1) * 512, 1024)
    ring.near()
    for c in sum(ux + uc, []):
        cp.sent(c)
    pl.semaphore_signal(ready, inc=1, device_id=sib, device_id_type=pl.DeviceIdType.MESH)
    up_tile(1152, d1, 0, 4)
    pl.semaphore_wait(ready, 1)
    s1.start(0, 2)
    up_tile(1152, d1, 4, 8)
    s1.start(2, 4)
    ring.relay()
    s1.stage_x(0)
    down_half(1 - p.c, 0, 6)
    s1.stage_x(1)
    down_half(1 - p.c, 6, 11)
    sd.start()
    s0.stage_z()
    down_half(p.c, 0, 11)

    def result(n, _):
        cols = pl.ds(pl.multiple_of(n * 512, 512), 512)
        out = jnp.dot(hid[...], vd[:, cols], preferred_element_type=f)
        ent[:, :, cols] = out.astype(bf).reshape(4, 128, 512)
        return 0

    lax.fori_loop(0, 4, result, 0)
    keeps = [pltpu.make_async_copy(ent, rpart, lsem.at[1])]
    keeps[0].start()
    ring.finish()
    for c in rest:
        c.wait()
    sums[...] = jnp.zeros_like(sums)

    def block(i, _):
        r = pl.ds(pl.multiple_of(i * ROWS, ROWS), ROWS)
        g = gpart[p.y, r].astype(f) + recv_g[0, r].astype(f) + recv_g[1, r].astype(f)
        m, inv = norm_rows(mid[r])
        sums[0:1] += jnp.sum(g * m, axis=0, keepdims=True)
        sums[1:2] += jnp.sum(g, axis=0, keepdims=True)
        e = g * gains[2:3, :]
        out = cot[r].astype(f) + inv * (e - jnp.mean(e, axis=-1, keepdims=True) - m * jnp.mean(e * m, axis=-1, keepdims=True))
        gmid[r] = out
        low[r] = out.astype(bf)
        return 0

    lax.fori_loop(0, 128 // ROWS, block, 0)
    for a, b in ((gmid, gmid_out), (low, low_out), (sums, sums_out)):
        keeps.append(pltpu.make_async_copy(a, b, lsem.at[1 + len(keeps)]))
        keeps[-1].start()
    sd.stage_core()
    keeps.append(pltpu.make_async_copy(dd.at[p.c], hd, lsem.at[1 + len(keeps)]))
    keeps[-1].start()
    keeps.append(pltpu.make_async_copy(s0.stage_sum(), j0, lsem.at[1 + len(keeps)]))
    keeps[-1].start()
    s1.stage_own()
    keeps.append(pltpu.make_async_copy(d1.at[p.c, :, p.xl], i1, lsem.at[1 + len(keeps)]))
    keeps[-1].start()
    cp.finish()
    for c in keeps:
        c.wait()


def second_step(ggu, gd, ent, cots, mid, cot, gains):
    f, bf = jnp.float32, jnp.bfloat16
    S = jax.ShapeDtypeStruct
    hbm, vm = pl.BlockSpec(memory_space=pl.ANY), pl.BlockSpec(memory_space=pltpu.VMEM)
    V = pltpu.VMEM
    return pl.pallas_call(
        second_kernel,
        out_shape=(S((4, 128, 2048), bf), S((128, 2048), f), S((128, 2048), bf), S((8, 2048), f),
                   S((4, 2, 11, 16, 1024), bf), S((4, 32, 1152), bf), S((4, 4, 32, 1664), bf)),
        in_specs=[hbm] * 7, out_specs=(hbm,) * 7,
        scratch_shapes=[
            V((4, 2, 4, 64, 2816), bf), V((1408, 2048), bf), V((4, 128, 2048), bf), V((4, 128, 2048), bf),
            V((512, 1408), bf), V((512, 2816), bf), V((4, 128, 2048), bf), V((2, 128, 2048), bf),
            V((2, 4, 2, 11, 16, 1024), bf), V((2, 4, 2, 4, 32, 1152), bf), V((2, 4, 2, 4, 32, 1664), bf),
            V((4, 2, 11, 16, 1024), bf), V((4, 2, 4, 32, 1152), bf), V((4, 4, 32, 1152), bf), V((3, 4, 32, 1152), bf), V((4, 4, 32, 1664), bf), V((2, 64, 2048), bf),
            V((128, 2048), f), V((128, 2048), bf), V((8, 2048), f), V((128, 2048), f), V((128, 2048), bf), V((8, 2048), f),
            pltpu.SemaphoreType.DMA((36,)), pltpu.SemaphoreType.DMA((36,)), pltpu.SemaphoreType.DMA((14,)),
            pltpu.SemaphoreType.REGULAR],
        compiler_params=pltpu.CompilerParams(collective_id=3, has_side_effects=True, vmem_limit_bytes=64 * 2**20 - 2**18),
        name="second_step",
    )(ggu, gd, ent, cots, mid, cot, gains)


class Finish:
    def __init__(self, p, cp, here, rxh, via, total, out, lsem, plane, unit=32):
        self.via, self.cut = via, (here.shape[0] + 1) // 2
        self.unit = unit
        self.p, self.cp, self.here, self.rxh, self.total, self.out, self.lsem, self.plane = p, cp, here, rxh, total, out, lsem, plane

    def stage_xh(self):
        p, k, n = self.p, self.cut, self.here.shape[0]
        self.steps = [self.cp.push(self.here.at[0:k], self.via.at[0:k], p.at(dx=1)),
                      self.cp.push(self.here.at[k:n], self.via.at[k:n], p.at(dx=-1))]

    def stage_relay(self):
        p, k, n = self.p, self.cut, self.here.shape[0]
        self.steps[0].wait_recv()
        last = [self.cp.push(self.via.at[0:k], self.rxh.at[0:k], p.at(dx=1))]
        self.steps[1].wait_recv()
        self.last_xh = last + [self.cp.push(self.via.at[k:n], self.rxh.at[k:n], p.at(dx=-1))]

    def stage_y(self):
        p, cp, out = self.p, self.cp, self.out
        for c in self.last_xh:
            c.wait_recv()
        add_into(self.total, (self.here, self.rxh))
        if self.plane:
            there = out.at[..., pl.ds(pl.multiple_of(p.c * 1024, 1024), 1024)]
            self.own = pltpu.make_async_copy(self.total, there, self.lsem)
            self.own.start()
            self.ys = [cp.push(self.total, there, p.at(dc=1))]
        else:
            half = pl.ds(pl.multiple_of(p.c * self.unit, self.unit), self.unit)
            self.own = pltpu.make_async_copy(self.total.at[p.y], out.at[p.y, half], self.lsem)
            self.own.start()
            self.ys = [cp.push(self.total.at[lax.rem(p.y + d, 4)], out.at[p.y, half], p.at(dy=d)) for d in (1, 3, 2)]

    def stage_c(self):
        p, out = self.p, self.out
        for c in self.ys:
            c.wait_recv()
        self.own.wait()
        self.last = []
        if not self.plane:
            half = pl.ds(pl.multiple_of(p.c * self.unit, self.unit), self.unit)
            self.last = [self.cp.push(out.at[:, half], out.at[:, half], p.at(dc=1))]

    def finish(self):
        for c in self.last:
            c.wait_recv()


def third_kernel(low, go, gq, e1, qkv, prb, mix, tab, rpart, mid_in, tok_in, gmid_in, gains_in, sums_in, hd, j0, i1,
                 act_out, ing_out, od, o0, o1, oq0, oq1, oo, os,
                 vgml, vo, vq, ve, vqkv, vprb, vmix, vtab, gp, gpart, recv_g, relay_g, vrp, recv_r, relay_r, wide,
                 mid, tok, gmid, gains, sums, act, ing,
                 vhd, rxxd, rzd, rxd, ved, td, vj0, rx0, ve0, t0, vi1, rz1, rx1, ve1, t1,
                 dq0, rcq0, rxq0, rzq0, rxhq0, vq0, tq0, dq1, rcq1, rxq1, rzq1, rxhq1, vq1, tq1,
                 dw, rco, rxo, rzo, rxho, veo, to, ds, rcs, rxs, rzs, rxhs, ves, ts,
                 send, recv, lsem):
    p = Place()
    f, bf = jnp.float32, jnp.bfloat16
    pairs_in = [(low, vgml.at[p.y]), (hd, vhd), (j0, vj0), (i1, vi1), (go, vo), (qkv, vqkv), (prb, vprb), (tab, vtab),
                (e1, ve), (mix, vmix), (gq, vq), (rpart, vrp),
                (mid_in, mid), (tok_in, tok), (gmid_in, gmid), (gains_in, gains), (sums_in, sums)]
    loads = [pltpu.make_async_copy(a, b, lsem.at[i]) for i, (a, b) in enumerate(pairs_in)]
    for c in loads[:8]:
        c.start()
    barrier(peers(p))
    cp = Copies(send, recv)
    ls = Spread(p, cp, low, vgml)
    ls.start()
    s1 = Sum(p, cp, None, None, rz1, 2)
    sd = Sum(p, cp, vhd, rxxd, rzd, None)
    f0 = Finish(p, cp, vj0, rx0, ve0, t0, o0, lsem.at[19], False)
    loads[1].wait()
    sd.stage_x()
    loads[2].wait()
    f0.stage_xh()
    loads[3].wait()
    s1.push_z(vi1)
    for c in loads[8:]:
        c.start()
    loads[0].wait()
    for c in loads[4:8]:
        c.wait()

    def attend(i):
        gm = dot_nt(vgml[i], vo[...].reshape(512, 2048)).astype(bf)
        cosine, sine = vtab[i, 0], -vtab[i, 1]
        for n in range(4):
            a, b, c = (slice(n * 384 + k * 128, n * 384 + (k + 1) * 128) for k in range(3))
            q, k, v = vqkv[i, :, a], vqkv[i, :, b], vqkv[i, :, c]
            prob = vprb[i, n]
            g = stack_heads(gm[:, n * 128:(n + 1) * 128])
            gv = dot_tn(prob.astype(bf), g)
            gprob = dot_nt(g, v)
            gs = (prob * (gprob - jnp.sum(prob * gprob, axis=-1, keepdims=True))).astype(bf)
            gq_ = merge_heads(jnp.dot(gs, k, preferred_element_type=f)) * SCALE
            gk = dot_tn(gs, stack_heads(q)) * SCALE
            gp[i, :, a] = turn(gq_, cosine, sine).astype(bf)
            gp[i, :, b] = turn(gk, cosine, sine).astype(bf)
            gp[i, :, c] = gv.astype(bf)

    attend(p.y)
    ls.relay(0)
    ls.relay(1)
    attend(lax.rem(p.y + 3, 4))
    attend(lax.rem(p.y + 1, 4))
    f0.stage_relay()
    f1 = Finish(p, cp, s1.stage_sum(), rx1, ve1, t1, o1, lsem.at[20], False)
    f1.stage_xh()
    ls.finish()
    loads[11].wait()
    rr = RingSum(p, cp, vrp, recv_r, relay_r)
    rr.start(0, 2048)
    rr.near()
    attend(lax.rem(p.y + 2, 4))
    sd.stage_z()
    loads[8].wait()

    def qkv_tile(first, dq):
        def body(i, _):
            rows = pl.ds(pl.multiple_of(i * 256, 256), 256)
            out = dot_tn(ve[:, :, rows].reshape(512, 256), gp[:, :, first:first + 768].reshape(512, 768))
            out = out.astype(bf).reshape(4, 2, 32, 768)
            dq[0, i // 2, lax.rem(i, 2)] = out[:, 0]
            dq[1, i // 2, lax.rem(i, 2)] = out[:, 1]
            return 0
        lax.fori_loop(0, 8, body, 0)

    qkv_tile(0, dq0)
    sq0 = Sum(p, cp, dq0.at[p.c], rxq0, rzq0, 2, rcq0, dq0.at[1 - p.c])
    sq0.start()
    f1.stage_relay()
    qkv_tile(768, dq1)
    sq1 = Sum(p, cp, dq1.at[p.c], rxq1, rzq1, 2, rcq1, dq1.at[1 - p.c])
    sq1.start()
    sq0.stage_x()
    for c in loads[9:11] + loads[12:]:
        c.wait()
    ring = RingSum(p, cp, gpart, recv_g, relay_g)
    for n in range(4):
        out = dot_nt(gp[...].reshape(512, 1536), vq[n].reshape(512, 1536))
        gpart[:, :, n * 512:(n + 1) * 512] = out.astype(bf).reshape(4, 128, 512)
        if n % 2:
            ring.start((n - 1) * 512, 1024)
    ring.near()

    def out_tile(h, _):
        cols = pl.ds(pl.multiple_of(h * 512, 512), 512)
        out = dot_tn(vmix[...].reshape(512, 512), vgml[:, :, cols].reshape(512, 512)).astype(bf)
        dw[h // 2, :, :, :, pl.ds(pl.multiple_of(lax.rem(h, 2) * 512, 512), 512)] = out.reshape(4, 2, 64, 512)
        return 0

    lax.fori_loop(0, 4, out_tile, 0)
    so = Sum(p, cp, dw.at[p.c], rxo, rzo, 32, rco, dw.at[1 - p.c])
    so.start()
    sq1.stage_x()

    rows = []
    for k in range(3):
        for n in range(4):
            first = n * 384 + k * 128
            rows.append(jnp.sum(gp[:, :, first:first + 128].reshape(512, 128).astype(f), axis=0, keepdims=True))
    rows = jnp.concatenate(rows + [jnp.zeros((4, 128), f)], axis=0).astype(bf)
    for i in range(8):
        for y in range(4):
            ds[1, i // 2, i % 2, y] = rows
    so.stage_x()
    ring.relay()
    sq0.stage_z()
    sq1.stage_z()
    fd = Finish(p, cp, sd.stage_sum(), rxd, ved, td, od, lsem.at[18], True)
    fd.stage_xh()
    wide[...] = jnp.zeros_like(wide)
    wide[2:4] = sums[0:2]
    ring.finish()

    def block(i, _):
        r = pl.ds(pl.multiple_of(i * ROWS, ROWS), ROWS)
        g = gpart[p.y, r].astype(f) + recv_g[0, r].astype(f) + recv_g[1, r].astype(f)
        m, inv = norm_rows(tok[r].astype(f))
        wide[0:1] += jnp.sum(g * m, axis=0, keepdims=True)
        wide[1:2] += jnp.sum(g, axis=0, keepdims=True)
        e = g * gains[0:1, :]
        out = gmid[r] + inv * (e - jnp.mean(e, axis=-1, keepdims=True) - m * jnp.mean(e * m, axis=-1, keepdims=True))
        ing[r] = out.astype(bf)
        return 0

    lax.fori_loop(0, 128 // ROWS, block, 0)
    keeps = [pltpu.make_async_copy(ing, ing_out, lsem.at[1])]
    keeps[0].start()
    for i in range(16):
        z, xl, y = i // 4, (i // 2) % 2, (i % 2) * 2
        piece = wide[:, i * 128:(i + 1) * 128]
        ds[0, z, xl, y] = piece.astype(bf)
        ds[0, z, xl, y + 1] = pltpu.roll(piece, 64, 1).astype(bf)
    ss = Sum(p, cp, ds.at[p.c], rxs, rzs, 2, rcs, ds.at[1 - p.c])
    ss.start()
    rr.relay()
    f0.stage_y()
    f1.stage_y()
    ss.stage_x()
    fd.stage_relay()
    fq0 = Finish(p, cp, sq0.stage_sum(), rxhq0, vq0, tq0, oq0, lsem.at[22], False)
    fq0.stage_xh()
    so.stage_z()
    ss.stage_z()
    fq1 = Finish(p, cp, sq1.stage_sum(), rxhq1, vq1, tq1, oq1, lsem.at[0], False)
    fq1.stage_xh()
    fq0.stage_relay()
    fs = Finish(p, cp, ss.stage_sum(), rxhs, ves, ts, os, lsem.at[23], False, 16)
    fs.stage_xh()
    fo = Finish(p, cp, so.stage_sum(), rxho, veo, to, oo, lsem.at[21], True)
    fo.stage_xh()
    fd.stage_y()
    fq1.stage_relay()
    fs.stage_relay()
    fq0.stage_y()
    fd.stage_c()
    f0.stage_c()
    f1.stage_c()
    fo.stage_relay()
    fq1.stage_y()
    fs.stage_y()
    fo.stage_y()
    rr.finish()

    def final(i, _):
        r = pl.ds(pl.multiple_of(i * ROWS, ROWS), ROWS)
        act[r] = (mid[r] + vrp[p.y, r].astype(f) + recv_r[0, r].astype(f) + recv_r[1, r].astype(f)).astype(bf)
        return 0

    lax.fori_loop(0, 128 // ROWS, final, 0)
    keeps.append(pltpu.make_async_copy(act, act_out, lsem.at[2]))
    keeps[1].start()
    fq0.stage_c()
    fq1.stage_c()
    fs.stage_c()
    fo.stage_c()
    for g in (fd, f0, f1, fq0, fq1, fo, fs):
        g.finish()
    cp.finish()
    for c in keeps:
        c.wait()


def third_step(*args):
    f, bf = jnp.float32, jnp.bfloat16
    S = jax.ShapeDtypeStruct
    hbm, vm = pl.BlockSpec(memory_space=pl.ANY), pl.BlockSpec(memory_space=pltpu.VMEM)
    V = pltpu.VMEM

    def sums(tail):
        return [V((2, 4, 2) + tail, bf), V((4, 2) + tail, bf), V((4,) + tail, bf), V((3,) + tail, bf), V(tail, bf), V(tail, bf), V(tail, bf)]

    return pl.pallas_call(
        third_kernel,
        out_shape=(S((128, 2048), bf), S((128, 2048), bf), S((11, 16, 2048), bf), S((4, 64, 1152), bf), S((4, 64, 1664), bf),
                   S((4, 64, 768), bf), S((4, 64, 768), bf), S((64, 2048), bf), S((4, 32, 128), bf)),
        in_specs=[hbm] * 17, out_specs=(hbm,) * 9,
        scratch_shapes=[
            V((4, 128, 2048), bf), V((4, 2, 64, 2048), bf), V((4, 2, 4, 64, 1536), bf), V((4, 128, 2048), bf),
            V((4, 128, 1536), bf), V((4, 4, 256, 128), f), V((4, 128, 512), bf), V((4, 2, 128, 128), f),
            V((4, 128, 1536), bf), V((4, 128, 2048), bf), V((2, 128, 2048), bf), V((2, 64, 2048), bf),
            V((4, 128, 2048), bf), V((2, 128, 2048), bf), V((2, 64, 2048), bf), V((16, 2048), f),
            V((128, 2048), f), V((128, 2048), bf), V((128, 2048), f), V((8, 2048), f), V((8, 2048), f), V((128, 2048), bf), V((128, 2048), bf),
            V((4, 2, 11, 16, 1024), bf), V((4, 11, 16, 1024), bf), V((3, 11, 16, 1024), bf), V((11, 16, 1024), bf), V((11, 16, 1024), bf), V((11, 16, 1024), bf),
            V((4, 32, 1152), bf), V((4, 32, 1152), bf), V((4, 32, 1152), bf), V((4, 32, 1152), bf),
            V((4, 4, 32, 1664), bf), V((3, 4, 32, 1664), bf), V((4, 32, 1664), bf), V((4, 32, 1664), bf), V((4, 32, 1664), bf)]
        + sums((4, 32, 768)) * 2 + sums((64, 1024)) + sums((4, 16, 128))
        + [pltpu.SemaphoreType.DMA((100,)), pltpu.SemaphoreType.DMA((100,)), pltpu.SemaphoreType.DMA((24,))],
        compiler_params=pltpu.CompilerParams(collective_id=4, has_side_effects=True, vmem_limit_bytes=62 * 2**20),
        name="third_step",
    )(*args)


def layout_kernel(oq0_in, oq1_in, o0_in, o1_in, oo_in, od_in, os_in, act_in, ing_in, act, ing, qkv_out, out_out, gate_out, up_out, down_out, g1, b1, g2, b2, bq,
                  oq0, oq1, o0, o1, oo, od, os, vact, ving, qkv, out, gate, up, down, sems):
    f = jnp.float32
    copies = ((oq0_in, oq0), (oq1_in, oq1), (o0_in, o0), (o1_in, o1), (oo_in, oo), (od_in, od), (os_in, os), (act_in, vact), (ing_in, ving))
    copies = [pltpu.make_async_copy(a, b, sems.at[i]) for i, (a, b) in enumerate(copies)]
    for c in copies:
        c.start()
    keeps = []

    def keep(src, dst):
        keeps.append(pltpu.make_async_copy(src, dst, sems.at[len(keeps) + 9]))
        keeps[-1].start()

    copies[0].wait()
    copies[1].wait()
    for g in range(48):
        k, h = g // 16, 2 * (g % 16)
        pieces = []
        for m in range(2):
            head = h + m
            pieces.append((m * 64, m * 64 + 64, head % 4, (head // 8) * 384 + k * 128 + ((head // 4) % 2) * 64))
        def load(j, t):
            src, at = (oq0, t) if t < 6 else (oq1, t - 6)
            return src[j, :, at * 128:(at + 1) * 128].astype(f)
        qkv[:, g * 128:(g + 1) * 128] = moved_lanes(pieces, load)
    keep(qkv, qkv_out)
    copies[2].wait()
    copies[3].wait()
    for n, dst in enumerate((gate, up)):
        def load(j, t):
            t = 2 * t + n
            src, at = (o0, t) if t < 9 else (o1, t - 9)
            return src[j, :, at * 128:(at + 1) * 128].astype(f)
        for g in range(44):
            dst[:, g * 128:(g + 1) * 128] = moved_lanes(shard_pieces(g), load)
        keep(dst, (gate_out, up_out)[n])
    for c in copies[4:]:
        c.wait()
    keep(vact, act)
    keep(ving, ing)
    out[...] = oo[...].astype(f)
    keep(out, out_out)
    down[...] = od[...].reshape(176, 2048).astype(f)
    keep(down, down_out)
    norms = os[0, 0:16].astype(f) + os[1, 0:16].astype(f) + os[2, 0:16].astype(f) + os[3, 0:16].astype(f)
    for k, v in enumerate((g1, b1, g2, b2)):
        v[...] = norms[k, 0:64]
    bias = []
    shard = (lax.axis_index("z") * 2 + lax.axis_index("xl")) * 4 + lax.axis_index("y")
    row = lax.broadcasted_iota(jnp.int32, (16, 128), 0)
    lane = lax.broadcasted_iota(jnp.int32, (16, 128), 1)
    for m in range(3):
        total = jnp.zeros((16, 128), f)
        for j in range(4):
            place = (row // 4) * 32 + (lax.rem(row, 4) * 2 + lane // 64) * 4 + j
            total = total + jnp.where((place == shard * 3 + m) & (row < 12), os[j, 16:32].astype(f), 0.0)
        total = jnp.sum(total, axis=0, keepdims=True)
        total = total + pltpu.roll(jnp.broadcast_to(total, (8, 128)), 64, 1)[0:1]
        bias.append(total[0, 0:64])
    bq[...] = jnp.concatenate(bias)
    for c in keeps:
        c.wait()


def layout_step(*args):
    f, bf = jnp.float32, jnp.bfloat16
    S = jax.ShapeDtypeStruct
    hbm, vm = pl.BlockSpec(memory_space=pl.ANY), pl.BlockSpec(memory_space=pltpu.VMEM)
    V = pltpu.VMEM
    return pl.pallas_call(
        layout_kernel,
        out_shape=(S((128, 2048), bf), S((128, 2048), bf), S((64, 6144), f), S((64, 2048), f), S((64, 5632), f), S((64, 5632), f),
                   S((176, 2048), f), S((64,), f), S((64,), f), S((64,), f), S((64,), f), S((192,), f)),
        in_specs=[hbm] * 9, out_specs=(hbm,) * 7 + (vm,) * 5,
        scratch_shapes=[V((4, 64, 768), bf), V((4, 64, 768), bf), V((4, 64, 1152), bf), V((4, 64, 1664), bf), V((64, 2048), bf),
                        V((11, 16, 2048), bf), V((4, 32, 128), bf), V((128, 2048), bf), V((128, 2048), bf), V((64, 6144), f), V((64, 2048), f), V((64, 5632), f),
                        V((64, 5632), f), V((176, 2048), f), pltpu.SemaphoreType.DMA((16,))],
        compiler_params=pltpu.CompilerParams(vmem_limit_bytes=60 * 2**20),
        name="layout_step",
    )(*args)


def local(tokens, segment_ids, cotangent, ln1_gain, ln1_bias, qkv_weight, qkv_bias, out_weight,
          ln2_gain, ln2_bias, gate_weight, up_weight, down_weight):
    cots, gq, ggu, go, gd, e1, qkv, prb, mix, tab, gains, mid, ent = first_step(
        tokens, cotangent, segment_ids, qkv_weight, ln1_gain, ln1_bias, ln2_gain, ln2_bias, qkv_bias, gate_weight, up_weight, out_weight, down_weight)
    rpart, gmid, low, sums, hd, j0, i1 = second_step(ggu, gd.reshape(1408, 2048), ent, cots, mid, cotangent, gains)
    act, ing, od, o0, o1, oq0, oq1, oo, os = third_step(
        low, go, gq, e1, qkv, prb, mix, tab, rpart, mid, tokens, gmid, gains, sums, hd, j0, i1)
    act, ing, qkv_grad, out_grad, gate_grad, up_grad, down_grad, g1, b1, g2, b2, bias = layout_step(
        oq0, oq1, o0, o1, oo, od, os, act, ing)
    return act, ing, g1, b1, qkv_grad, bias, out_grad, g2, b2, gate_grad, up_grad, down_grad


def solution(mesh):
    fine = Mesh(mesh.devices.reshape(2, 2, 4, 2, 4), AXES)
    whole, rows = P(AXES, None), P(("z", "xl", "y"), None)
    vector = P(("z", "xl", "y"))
    return jax.shard_map(
        local, mesh=fine,
        in_specs=(whole, whole, whole, vector, vector, rows, vector, rows, vector, vector, rows, rows, rows),
        out_specs=(whole, whole, vector, vector, rows, vector, rows, vector, vector, rows, rows, rows),
        check_vma=False,
    )
```

```python
import functools
import jax, jax.numpy as jnp
from jax import lax
from jax.sharding import PartitionSpec as P, Mesh
from jax.experimental import pallas as pl
from jax.experimental.pallas import tpu as pltpu

AXES = ("xh", "c", "z", "xl", "y")


class Place:
    def __init__(self):
        self.xh, self.c, self.z, self.xl, self.y = (lax.axis_index(a) for a in AXES)
        self.x = self.xh * 2 + self.xl

    def at(self, dx=0, dy=0, dz=0, dc=0):
        x = lax.rem(self.x + dx + 4, 4) if dx else self.x
        return (
            x // 2 if dx else self.xh,
            lax.rem(self.c + dc, 2) if dc else self.c,
            lax.rem(self.z + dz + 4, 4) if dz else self.z,
            lax.rem(x, 2) if dx else self.xl,
            lax.rem(self.y + dy + 4, 4) if dy else self.y,
        )


def barrier(targets):
    sem = pltpu.get_barrier_semaphore()
    for target in targets:
        pl.semaphore_signal(sem, inc=1, device_id=target, device_id_type=pl.DeviceIdType.MESH)
    pl.semaphore_wait(sem, len(targets))


class Copies:
    def __init__(self, send, recv):
        self.send, self.recv, self.used, self.all = send, recv, 0, []

    def push(self, src, dst, target):
        copy = pltpu.make_async_remote_copy(
            src_ref=src, dst_ref=dst, send_sem=self.send.at[self.used],
            recv_sem=self.recv.at[self.used], device_id=target, device_id_type=pl.DeviceIdType.MESH)
        self.used += 1
        self.all.append(copy)
        copy.start()
        return copy

    def sent(self, copy):
        copy.wait_send()
        self.all = [c for c in self.all if c is not copy]

    def finish(self):
        for copy in self.all:
            copy.wait_send()


def add_into(out, parts):
    total = parts[0][...].astype(jnp.float32)
    for part in parts[1:]:
        total = total + part[...].astype(jnp.float32)
    out[...] = total.astype(out.dtype)


def peers(p):
    return [p.at(dy=d) for d in (1, 2, 3)] + [p.at(dz=d) for d in (1, 2, 3)] + [p.at(dx=d) for d in (1, 2, -1)] + [p.at(dc=1)]


class Gather:
    def __init__(self, p, cp, src, dst, lsem, cols=None, cut=None, unit=32, part=(0, 1024)):
        self.p, self.cp, self.src, self.dst, self.lsem, self.cut = p, cp, src, dst, lsem, cut
        self.cols = cols
        if cut is None:
            self.half = pl.ds(pl.multiple_of(p.c * unit, unit), unit)
        else:
            self.half = pl.ds(pl.multiple_of(p.c * 1024 + part[0], part[1]), part[1])

    def start(self):
        p, src, dst, half = self.p, self.src, self.dst, self.half
        if self.cut is None:
            cols = self.cols
            here = dst.at[p.z, p.xl, p.y, half, cols]
            self.local = pltpu.make_async_copy(src.at[p.y, half, cols], here, self.lsem)
            self.local.start()
            self.ys = [self.cp.push(src.at[lax.rem(p.y + d, 4), half, cols], here, p.at(dy=d)) for d in (1, 3, 2)]
        else:
            here = dst.at[p.z, p.xl, :, half]
            self.local = pltpu.make_async_copy(src.at[:, half], here, self.lsem)
            self.local.start()
            self.zs = [self.cp.push(src.at[:, half], here, p.at(dz=d)) for d in (1, 3, 2)]

    def stage_y(self):
        self.local.wait()
        for c in self.ys:
            c.wait_recv()

    def stage_z(self):
        p = self.p
        self.stage_y()
        here = self.dst.at[p.z, p.xl, :, self.half, self.cols]
        self.zs = [self.cp.push(here, here, p.at(dz=d)) for d in (1, 3, 2)]

    def parts(self, xl):
        g = self.dst
        if self.cut is not None:
            k, r = self.cut, g.shape[2]
            return g.at[:, xl, 0:k, self.half], g.at[:, xl, k:r, self.half], g.at[:, xl, :, self.half]
        return (g.at[:, xl, 0:2, self.half, self.cols], g.at[:, xl, 2:4, self.half, self.cols],
                g.at[:, xl, :, self.half, self.cols])

    def stage_x(self):
        p = self.p
        if self.cut is not None:
            self.local.wait()
        for c in self.zs:
            c.wait_recv()
        lo, hi, full = self.parts(p.xl)
        self.xs = [self.cp.push(lo, lo, p.at(dx=1)), self.cp.push(hi, hi, p.at(dx=-1))]
        self.cs = [self.cp.push(full, full, p.at(dc=1))]

    def stage_c(self):
        p = self.p
        lo, hi, full = self.parts(1 - p.xl)
        self.xs[0].wait_recv()
        self.cs.append(self.cp.push(lo, lo, p.at(dc=1)))
        self.xs[1].wait_recv()
        self.cs.append(self.cp.push(hi, hi, p.at(dc=1)))

    def finish(self):
        for c in self.cs:
            c.wait_recv()


class Spread:
    def __init__(self, p, cp, src, dst):
        self.p, self.cp, self.src, self.dst = p, cp, src, dst

    def start(self):
        p = self.p
        self.near = [self.cp.push(self.src, self.dst.at[p.y], p.at(dy=d)) for d in (1, 3)]

    def relay(self, k):
        p = self.p
        self.near[k].wait_recv()
        half = self.dst.at[lax.rem(p.y + (3, 1)[k], 4), pl.ds(64 * k, 64)]
        copy = self.cp.push(half, half, p.at(dy=(1, 3)[k]))
        self.far = [copy] if k == 0 else self.far + [copy]

    def finish(self):
        for c in self.far:
            c.wait_recv()


class RingSum:
    def __init__(self, p, cp, part, recv, via):
        self.p, self.cp, self.part, self.recv, self.via, self.away = p, cp, part, recv, via, []
        self.lower, self.upper = pl.ds(0, 64), pl.ds(64, 64)
        self.next, self.far, self.prev = (lax.rem(p.y + k, 4) for k in (1, 2, 3))

    def start(self, first, width):
        cols = pl.ds(first, width)
        self.away.append([self.cp.push(self.part.at[self.far, half, cols], self.via.at[k, :, cols], self.p.at(dy=dy))
                          for k, half, dy in ((0, self.lower, 1), (1, self.upper, -1))])

    def near(self):
        self.ins = [self.cp.push(self.part.at[self.next, self.upper], self.recv.at[0, self.upper], self.p.at(dy=1)),
                    self.cp.push(self.part.at[self.prev, self.lower], self.recv.at[1, self.lower], self.p.at(dy=-1))]

    def relay(self):
        for k, half, seq, dy in ((0, self.lower, self.next, 1), (1, self.upper, self.prev, -1)):
            for pair in self.away:
                pair[k].wait_recv()
            here = self.part.at[seq, half]
            add_into(here, (here, self.via.at[k]))
            self.ins.append(self.cp.push(here, self.recv.at[k, half], self.p.at(dy=dy)))

    def finish(self):
        for c in self.ins:
            c.wait_recv()


ROWS = 16
norm_epsilon = 1e-05
masked_score = -1000000000.0
HEADS = 8
HEAD_DIM = 64
ROT = 16
SCALE = HEAD_DIM ** (-0.5)


def norm_rows(m):
    m = m - jnp.mean(m, axis=-1, keepdims=True)
    inv = lax.rsqrt(jnp.mean(m * m, axis=-1, keepdims=True) + norm_epsilon)
    return m * inv, inv


def allowed_of(seg_row):
    keys = jnp.broadcast_to(seg_row, (128, 128))
    queries = jnp.transpose(keys)
    q = lax.broadcasted_iota(jnp.int32, (128, 128), 0)
    k = lax.broadcasted_iota(jnp.int32, (128, 128), 1)
    same = keys == queries
    places = jnp.sum(jnp.where(same & (k < q), 1.0, 0.0), axis=-1, keepdims=True)
    return same & (k <= q), places


def turn(x, cosine, sine):
    lane = lax.broadcasted_iota(jnp.int32, (128, 128), 1)
    other = jnp.where(lax.rem(lane, 64) < 8, pltpu.roll(x, 120, 1), pltpu.roll(x, 8, 1))
    return x * cosine + other * sine


def stack_heads(x):
    lane = lax.broadcasted_iota(jnp.int32, (128, 128), 1)
    zero = jnp.zeros_like(x)
    return jnp.concatenate([jnp.where(lane < 64, x, zero), jnp.where(lane < 64, zero, x)], axis=0)


def merge_heads(x):
    lane = lax.broadcasted_iota(jnp.int32, (128, 128), 1)
    return jnp.where(lane < 64, x[:128], x[128:])


def dot_nt(a, b):
    return lax.dot_general(a, b, (((1,), (1,)), ((), ())), preferred_element_type=jnp.float32)


def dot_tn(a, b):
    return lax.dot_general(a, b, (((0,), (0,)), ((), ())), preferred_element_type=jnp.float32)


def moved_lanes(pieces, load):
    out = None
    for first, end, source, column in pieces:
        while first < end:
            group, at = divmod(column, 128)
            width = min(end - first, 128 - at)
            value = load(source, group)
            shift = (first - at) % 128
            if shift:
                value = pltpu.roll(value, shift, 1)
            if out is None:
                out = value
            else:
                lane = lax.broadcasted_iota(jnp.int32, value.shape, 1)
                out = jnp.where((lane >= first) & (lane < first + width), value, out)
            first, column = first + width, column + width
    return out


def hidden_pieces(part, group):
    pieces, at = [], 0
    while at < 128:
        block, rest = divmod(group * 128 + at, 176)
        width = min(128 - at, 176 - rest)
        pieces.append((at, at + width, 0, (4 * block + part) * 176 + rest))
        at += width
    return pieces


def shard_pieces(group):
    pieces, at = [], 0
    while at < 128:
        shard, rest = divmod(group * 128 + at, 176)
        width = min(128 - at, 176 - rest)
        pieces.append((at, at + width, shard % 4, (shard // 4) * 176 + rest))
        at += width
    return pieces


def small_parameters(p, out, g1, b1, g2, b2, bq):
    f, bf = jnp.float32, jnp.bfloat16
    shard = (p.z * 2 + p.xl) * 4 + p.y
    row = lax.broadcasted_iota(jnp.int32, (16, 128), 0)
    lane = lax.broadcasted_iota(jnp.int32, (16, 128), 1)

    def twice(v):
        v = v.astype(f).reshape(1, 64)
        return jnp.concatenate([v, v], axis=1)

    norms = jnp.zeros((16, 128), f)
    for k, v in enumerate((g1, b1, g2, b2)):
        norms = jnp.where((row == k) & (lane < 64), twice(v[...]), norms)
    for j in range(4):
        place = (row // 4) * 32 + (lax.rem(row, 4) * 2 + lane // 64) * 4 + j
        bias = jnp.zeros((16, 128), f)
        for k in range(3):
            bias = jnp.where((place == shard * 3 + k) & (row < 12), twice(bq[k * 64:(k + 1) * 64]), bias)
        out[j, 0:16] = norms.astype(bf)
        out[j, 16:32] = bias.astype(bf)


def first_kernel(tok, cot, seg, wq, g1, b1, g2, b2, bq, wg, wu, wo, wd,
                 cots, gq, ggu, go, gd, e1, qkv, prb, mix, tab, gains_out, mid_out, ent_out,
                 rq, rg, ru, sm, pq, pgu, vq, vs, vo, x, xe, segv, segs, proj, qkvb, probs, mixed, tabs, masks, part, recv_a, relay_a, own, bias, gains, mid, ent,
                 send, recv, lsem):
    p = Place()
    f, bf = jnp.float32, jnp.bfloat16
    locals_ = []

    def local(src, dst):
        copy = pltpu.make_async_copy(src, dst, lsem.at[len(locals_)])
        copy.start()
        locals_.append(copy)
        return copy

    def sem():
        locals_.append(None)
        return lsem.at[len(locals_) - 1]

    raw = [local(wq, rq), local(wg, rg), local(wu, ru), local(tok, own)]
    barrier([p.at(dy=d) for d in (1, 2, 3)] + [p.at(dz=d) for d in (1, 2, 3)] + [p.at(dx=1), p.at(dx=-1), p.at(dc=1)])
    cp = Copies(send, recv)

    def share(src, dst):
        return [local(src, dst.at[p.y])], [cp.push(src, dst.at[p.y], p.at(dy=d)) for d in (1, 3, 2)]

    q = [Gather(p, cp, pq, vq, sem(), cols=pl.ds(n * 384, 384)) for n in range(4)]
    s = Gather(p, cp, sm, vs, sem(), cols=pl.ds(0, 128), unit=16)
    u0 = Gather(p, cp, pgu, ggu, sem(), cols=pl.ds(0, 512))
    u1 = Gather(p, cp, pgu, ggu, sem(), cols=pl.ds(512, 512))
    u2 = Gather(p, cp, pgu, ggu, sem(), cols=pl.ds(1024, 512))
    u3 = Gather(p, cp, pgu, ggu, sem(), cols=pl.ds(1536, 512))
    u4 = Gather(p, cp, pgu, ggu, sem(), cols=pl.ds(2048, 768))
    o = Gather(p, cp, wo, vo, sem(), cut=32)
    d, e = (Gather(p, cp, wd, gd, sem(), cut=96, part=(k * 512, 512)) for k in range(2))
    xs = Spread(p, cp, tok, x)
    cs = Spread(p, cp, cot, cots)

    small_parameters(p, sm, g1, b1, g2, b2, bq)
    s.start()
    segv[...] = jnp.broadcast_to(seg[...].astype(f), (8, 128))
    s_here, s_in = share(segv, segs)
    raw[0].wait()
    for n in range(4):
        for j in range(4):
            for k in range(3):
                pieces = [(0, 64, 0, k * 2048 + (8 * n + j) * 64), (64, 128, 0, k * 2048 + (8 * n + 4 + j) * 64)]
                got = moved_lanes(pieces, lambda _, g: rq[:, g * 128:(g + 1) * 128].astype(f))
                pq[j, :, n * 384 + k * 128:n * 384 + (k + 1) * 128] = got.astype(bf)
        q[n].start()
    xs.start()
    x_here = [local(tok, x.at[p.y])]
    raw[1].wait()
    raw[2].wait()
    for j in range(4):
        for t in range(11):
            for k, r in enumerate((rg, ru)):
                got = moved_lanes(hidden_pieces(j, t), lambda _, g: r[:, g * 128:(g + 1) * 128].astype(f))
                pgu[j, :, t * 256 + k * 128:t * 256 + (k + 1) * 128] = got.astype(bf)
    s.stage_z()
    q[0].stage_z()
    q[1].stage_z()
    for c in s_here:
        c.wait()
    for c in s_in:
        c.wait_recv()

    lane = lax.broadcasted_iota(jnp.int32, (128, 128), 1)
    low = lax.rem(lane, 64)

    freqs = jnp.zeros((1, 128), f)
    for k in range(ROT // 2):
        freqs = jnp.where(lax.rem(lane[0:1], ROT // 2) == k, 10000.0 ** (-2.0 * k / ROT), freqs)

    def table(i, _):
        allowed, places = allowed_of(segs[i, 0:1, :])
        masks[i] = jnp.where(allowed, 1.0, 0.0)
        angle = places * freqs
        tabs[i, 0] = jnp.where(low < ROT, jnp.cos(angle), 1.0)
        sine = jnp.sin(angle)
        tabs[i, 1] = jnp.where(low < ROT // 2, -sine, jnp.where(low < ROT, sine, 0.0))
        return 0

    lax.fori_loop(0, 4, table, 0)
    local(tabs, tab)
    s.stage_x()
    s.stage_c()
    q[0].stage_x()
    q[2].stage_z()
    s.finish()

    half_lane = lax.broadcasted_iota(jnp.int32, (8, 128), 1) < 64
    for i in range(16):
        z, xl, y = i // 4, (i // 2) % 2, (i % 2) * 2
        a = vs[z, xl, y, 0:16].astype(f)[0:8]
        b = pltpu.roll(vs[z, xl, y + 1, 0:16].astype(f)[0:8], 64, 1)
        gains[:, i * 128:(i + 1) * 128] = jnp.where(half_lane, a, b)
    total = jnp.zeros((16, 128), f)
    for i in range(32):
        total = total + vs[i // 8, (i // 4) % 2, i % 4, 16:32].astype(f)
    bias[...] = total

    local(gains, gains_out)

    def entry(i):
        def block(b, _):
            r = pl.ds(pl.multiple_of(b * ROWS, ROWS), ROWS)
            n, _inv = norm_rows(x[i, r].astype(f))
            xe[i, r] = (n * gains[0:1, :] + gains[1:2, :]).astype(bf)
            return 0
        lax.fori_loop(0, 128 // ROWS, block, 0)

    q[1].stage_x()
    q[3].stage_z()
    x_here[0].wait()
    entry(p.y)
    xs.relay(0)
    xs.relay(1)
    q[0].stage_c()
    q[2].stage_x()
    o.start()
    entry(lax.rem(p.y + 3, 4))
    q[1].stage_c()
    q[3].stage_x()
    d.start()
    e.start()
    entry(lax.rem(p.y + 1, 4))
    q[2].stage_c()
    u0.start()
    u1.start()
    xs.finish()
    cs.start()
    entry(lax.rem(p.y + 2, 4))
    c_here = [local(cot, cots.at[p.y])]
    local(xe, e1)

    def heads(n):
        q[n].finish()
        first = n * 384
        w = vq[:, :, :, :, first:first + 384].reshape(2048, 384)
        out = jnp.dot(xe[...].reshape(512, 2048), w, preferred_element_type=f)
        b = jnp.concatenate([bias[k * 4 + n:k * 4 + n + 1, :] for k in range(3)], axis=1)
        proj[...] = (out + b).reshape(4, 128, 384)

        def attend(i, _):
            allowed = masks[i] > 0.5
            allowed = jnp.concatenate([allowed, allowed], axis=0)
            cosine, sine = tabs[i, 0], tabs[i, 1]
            qr = turn(proj[i, :, 0:128], cosine, sine).astype(bf)
            kr = turn(proj[i, :, 128:256], cosine, sine).astype(bf)
            v = proj[i, :, 256:384].astype(bf)
            qkvb[i, :, first:first + 128] = qr
            qkvb[i, :, first + 128:first + 256] = kr
            qkvb[i, :, first + 256:first + 384] = v
            scores = dot_nt(stack_heads(qr), kr) * SCALE
            scores = jnp.where(allowed, scores, masked_score)
            expos = jnp.exp(scores - jnp.max(scores, axis=-1, keepdims=True))
            prob = expos / jnp.sum(expos, axis=-1, keepdims=True)
            probs[i, n] = prob
            got = jnp.dot(prob.astype(bf), v, preferred_element_type=f)
            mixed[i, :, n * 128:(n + 1) * 128] = merge_heads(got).astype(bf)
            return 0

        lax.fori_loop(0, 4, attend, 0)

    heads(0)
    q[3].stage_c()
    o.stage_x()
    heads(1)
    heads(2)
    o.stage_c()
    d.stage_x()
    u0.stage_z()
    u2.start()
    u3.start()
    u4.start()
    heads(3)
    e.stage_x()
    u1.stage_z()
    o.finish()
    ring = RingSum(p, cp, part, recv_a, relay_a)
    for n in range(4):
        cols = pl.ds(n * 512, 512)
        out = jnp.dot(mixed[...].reshape(512, 512), vo[:, :, :, cols].reshape(512, 512), preferred_element_type=f)
        part[:, :, cols] = out.astype(bf).reshape(4, 128, 512)
        if n % 2:
            ring.start((n - 1) * 512, 1024)
    ring.near()
    u2.stage_z()
    local(vo, go)
    local(vq, gq)
    local(qkvb, qkv)
    local(probs, prb)
    local(mixed, mix)
    u0.stage_x()
    ring.relay()
    u1.stage_x()
    u3.stage_z()
    d.stage_c()
    e.stage_c()
    u2.stage_x()
    u4.stage_z()
    ring.finish()
    cs.relay(0)
    cs.relay(1)

    def block(i, _):
        r = pl.ds(pl.multiple_of(i * ROWS, ROWS), ROWS)
        m = own[r].astype(f) + part[p.y, r].astype(f) + recv_a[0, r].astype(f) + recv_a[1, r].astype(f)
        mid[r] = m
        n, _inv = norm_rows(m)
        ent[r] = (n * gains[2:3, :] + gains[3:4, :]).astype(bf)
        return 0

    raw[3].wait()
    lax.fori_loop(0, 128 // ROWS, block, 0)
    local(mid, mid_out)
    es = Spread(p, cp, ent, ent_out)
    es.start()
    local(ent, ent_out.at[p.y])
    u3.stage_x()
    u0.stage_c()
    u1.stage_c()
    cs.finish()
    u2.stage_c()
    u3.stage_c()
    for c in u4.zs:
        c.wait_recv()
    for g in (d, e, u0, u1, u2, u3):
        g.finish()
    for c in es.near:
        c.wait_recv()
    cp.finish()
    for copy in locals_:
        if copy is not None and not any(copy is done for done in x_here + s_here + raw):
            copy.wait()


def first_step(*args):
    f, bf = jnp.float32, jnp.bfloat16
    S = jax.ShapeDtypeStruct
    hbm, vm = pl.BlockSpec(memory_space=pl.ANY), pl.BlockSpec(memory_space=pltpu.VMEM)
    V = pltpu.VMEM
    outs = (S((4, 128, 2048), bf), S((4, 2, 4, 64, 1536), bf), S((4, 2, 4, 64, 2816), bf), S((4, 2, 64, 2048), bf),
            S((4, 2, 176, 2048), bf), S((4, 128, 2048), bf), S((4, 128, 1536), bf), S((4, 4, 256, 128), f),
            S((4, 128, 512), bf), S((4, 2, 128, 128), f), S((8, 2048), f), S((128, 2048), f), S((4, 128, 2048), bf))
    return pl.pallas_call(
        first_kernel, out_shape=outs, in_specs=[hbm, hbm, vm, hbm] + [vm] * 5 + [hbm] * 4,
        out_specs=(hbm,) * 13,
        scratch_shapes=[
            V((64, 6144), bf), V((64, 5632), bf), V((64, 5632), bf), V((4, 32, 128), bf), V((4, 64, 1536), bf), V((4, 64, 2816), bf),
            V((4, 2, 4, 64, 1536), bf), V((4, 2, 4, 32, 128), bf), V((4, 2, 64, 2048), bf),
            V((4, 128, 2048), bf), V((4, 128, 2048), bf), V((8, 128), f), V((4, 8, 128), f), V((4, 128, 384), f),
            V((4, 128, 1536), bf), V((4, 4, 256, 128), f), V((4, 128, 512), bf),
            V((4, 2, 128, 128), f), V((4, 128, 128), f), V((4, 128, 2048), bf), V((2, 128, 2048), bf), V((2, 64, 2048), bf),
            V((128, 2048), bf), V((16, 128), f), V((8, 2048), f), V((128, 2048), f), V((128, 2048), bf),
            pltpu.SemaphoreType.DMA((150,)), pltpu.SemaphoreType.DMA((150,)), pltpu.SemaphoreType.DMA((30,))],
        compiler_params=pltpu.CompilerParams(collective_id=1, has_side_effects=True, vmem_limit_bytes=56 * 2**20),
        name="first_step",
    )(*args)


class Sum:
    def __init__(self, p, cp, terms, rx, rz, cut, rc=None, other=None):
        self.p, self.cp, self.h, self.other, self.rc, self.rx, self.rz, self.cut = p, cp, terms, other, rc, rx, rz, cut

    def start(self, first=0, stop=4):
        part = pl.ds(first, stop - first)
        self.core = ([] if first == 0 else self.core) + [self.cp.push(self.other.at[part], self.rc.at[part], self.p.at(dc=1))]

    def stage_core(self):
        h, rc = self.h, self.rc
        for c in self.core:
            c.wait_recv()

        def both(i, _):
            add_into(h.at[i], (h.at[i], rc.at[i]))
            return 0

        lax.fori_loop(0, 4, both, 0)

    def stage_x(self, piece=None):
        p, h, rc, k = self.p, self.h, self.rc, self.cut
        first, count = (0, 4) if piece is None else (2 * piece, 2)
        if rc is not None:
            for c in self.core if piece is None else self.core[piece:piece + 1]:
                c.wait_recv()

            def foreign(i, _):
                add_into(h.at[i, 1 - p.xl], (h.at[i, 1 - p.xl], rc.at[i, 1 - p.xl]))
                return 0

            lax.fori_loop(first, first + count, foreign, 0)
        blocks = pl.ds(first, count)
        here, there = h.at[blocks, 1 - p.xl], self.rx.at[blocks]
        if k is None:
            n = h.shape[-1] // 2
            lo, hi = (Ellipsis, pl.ds(0, n)), (Ellipsis, pl.ds(n, n))
        else:
            lo, hi = (slice(None), pl.ds(0, k)), (slice(None), pl.ds(k, h.shape[2] - k))
        self.xs = ([] if first == 0 else self.xs) + [
            self.cp.push(here.at[lo], there.at[lo], p.at(dx=1)), self.cp.push(here.at[hi], there.at[hi], p.at(dx=-1))]

    def stage_own(self):
        p, h, rc, rx = self.p, self.h, self.rc, self.rx
        for c in self.xs:
            c.wait_recv()

        def own(i, _):
            here = h.at[i, p.xl]
            add_into(here, (here, rx.at[i]) if rc is None else (here, rc.at[i, p.xl], rx.at[i]))
            return 0

        lax.fori_loop(0, 4, own, 0)

    def push_z(self, blocks):
        p = self.p
        self.blocks = blocks
        self.zs = [self.cp.push(blocks.at[lax.rem(p.z + d, 4)], self.rz.at[d - 1], p.at(dz=d)) for d in (1, 3, 2)]

    def stage_z(self):
        self.stage_own()
        self.push_z(self.h.at[:, self.p.xl])

    def stage_sum(self):
        rz = self.rz
        here = self.blocks.at[self.p.z]
        for c in self.zs:
            c.wait_recv()
        add_into(here, (here, rz.at[0], rz.at[1], rz.at[2]))
        return here


def second_kernel(ggu, gd, ents, cots, mid_in, cot_in, gains_in,
                  rpart, gmid_out, low_out, sums_out, hd, j0, i1,
                  vgu, vd, ent, cts, hid, dgu, gpart, recv_g, dd, d0, d1, rcd, rc0, rx0, rz0, rx1, relay_g, mid, cot, gains, gmid, low, sums,
                  send, recv, lsem, ready):
    p = Place()
    f, bf = jnp.float32, jnp.bfloat16
    sib = p.at(dc=1)
    near = [p.y, lax.rem(p.y + 3, 4), lax.rem(p.y + 1, 4)]
    far = [lax.rem(p.y + 2, 4)]
    own_load = [pltpu.make_async_copy(ents.at[i], ent.at[i], lsem.at[(0, 11, 12)[k]]) for k, i in enumerate(near)]
    loads = [pltpu.make_async_copy(a, b, lsem.at[1 + i]) for i, (a, b) in enumerate(((cots, cts), (gd, vd)))]
    tiles = []
    for n in range(4):
        cols = pl.ds(n * 512, 512)
        tiles.append(pltpu.make_async_copy(ggu.at[:, :, :, :, cols], vgu.at[:, :, :, :, cols], lsem.at[(3, 4, 13, 10)[n]]))
    rest = [pltpu.make_async_copy(a, b, lsem.at[6 + i]) for i, (a, b) in enumerate(((mid_in, mid), (cot_in, cot), (gains_in, gains)))]
    for c in loads:
        c.start()
    barrier([p.at(dy=d) for d in (1, 2, 3)] + [p.at(dz=d) for d in (1, 2, 3)] + [p.at(dx=1), p.at(dx=-1), sib])
    cp = Copies(send, recv)
    es = [cp.push(ents.at[near[2 - k], pl.ds(64 * (1 - k), 64)], ent.at[near[2 - k], pl.ds(64 * (1 - k), 64)], p.at(dy=(-1, 1)[k])) for k in (0, 1)]
    half = pl.ds(pl.multiple_of(p.c * 32, 32), 32)
    late = [pl.ds(2048, 768)]
    mine = [pltpu.make_async_copy(ggu.at[:, p.xl, :, half, cols], vgu.at[:, p.xl, :, half, cols], lsem.at[9 + i]) for i, cols in enumerate(late)]
    ux, uc = [], []

    def late_x(k):
        cols = late[k]
        ux.append([cp.push(ggu.at[:, p.xl, a:a + 2, half, cols], vgu.at[:, p.xl, a:a + 2, half, cols], p.at(dx=d)) for a, d in ((0, 1), (2, -1))])
        uc.append([cp.push(ggu.at[:, p.xl, :, half, cols], vgu.at[:, p.xl, :, half, cols], sib)])

    late_x(0)

    def late_c(k):
        for i in range(2):
            ux[k][i].wait_recv()
            there = vgu.at[:, 1 - p.xl, 2 * i:2 * i + 2, half, late[k]]
            uc[k].append(cp.push(there, there, sib))

    for c in loads:
        c.wait()
    for c in own_load + tiles + mine + rest:
        c.start()

    def back_tile(first, width):
        out = dot_nt(cts[...].reshape(512, 2048), vd[pl.ds(first, width), :])
        hid[:, pl.ds(first, width)] = out.astype(bf)

    def back(n, _):
        back_tile(pl.multiple_of(n * 256, 256), 256)
        return 0

    lax.fori_loop(0, 5, back, 0)
    back_tile(1280, 128)

    def hidden_tile(first, width, seqs=None):
        w = vgu[:, :, :, :, pl.ds(2 * first, 2 * width)].reshape(2048, 2 * width)
        if seqs is None:
            a, rows = ent[...].reshape(512, 2048), [pl.ds(0, 512)]
        else:
            a, rows = jnp.concatenate([ent[i] for i in seqs], axis=0), [pl.ds(pl.multiple_of(i * 128, 128), 128) for i in seqs]
        gu = jnp.dot(a, w, preferred_element_type=f)
        size = gu.shape[0] // len(rows)
        for k in range(width // 128):
            cols = pl.ds(first + k * 128, 128)
            for m, r in enumerate(rows):
                part = gu[m * size:(m + 1) * size]
                gate, up = part[:, k * 256:k * 256 + 128], part[:, k * 256 + 128:k * 256 + 256]
                g = hid[r, cols].astype(f)
                sig = 1.0 / (1.0 + jnp.exp(-gate))
                silu = gate * sig
                hid[r, cols] = (silu * up).astype(bf)
                dgu[r, pl.ds(2 * first + k * 256, 128)] = (g * up * sig * (1.0 + gate * (1.0 - sig))).astype(bf)
                dgu[r, pl.ds(2 * first + k * 256 + 128, 128)] = (g * silu).astype(bf)

    def near_tile(n, _):
        hidden_tile(pl.multiple_of(n * 256, 256), 256, near)
        return 0

    def far_tile(n, _):
        hidden_tile(pl.multiple_of(n * 256, 256), 256, far)
        return 0

    def tile(n, _):
        hidden_tile(pl.multiple_of(n * 256, 256), 256)
        return 0

    for c in own_load:
        c.wait()
    for c in tiles + mine:
        c.wait()
    lax.fori_loop(0, 4, near_tile, 0)
    late_c(0)
    for c in es:
        c.wait_recv()
    lax.fori_loop(0, 4, far_tile, 0)

    def down_half(h, start, stop):
        cols = pl.ds(pl.multiple_of(h * 1024, 1024), 1024)

        def down_tile(t, _):
            rows = pl.ds(pl.multiple_of(t * 128, 128), 128)
            out = dot_tn(hid[:, rows], cts[:, :, cols].reshape(512, 1024)).astype(bf)
            for k in range(8):
                g = t * 8 + k
                dd[h, g // 22, lax.rem(g // 11, 2), lax.rem(g, 11)] = out[k * 16:(k + 1) * 16]
            return 0

        lax.fori_loop(start, stop, down_tile, 0)

    def up_tile(first, d, start, stop):
        width = d.shape[-1]

        def body(i, _):
            rows = pl.ds(pl.multiple_of(i * 256, 256), 256)
            out = dot_tn(ent[:, :, rows].reshape(512, 256), dgu[:, first:first + width]).astype(bf).reshape(4, 2, 32, width)
            d[0, i // 2, lax.rem(i, 2)] = out[:, 0]
            d[1, i // 2, lax.rem(i, 2)] = out[:, 1]
            return 0
        lax.fori_loop(start, stop, body, 0)

    sd = Sum(p, cp, dd.at[p.c], None, None, None, rcd, dd.at[1 - p.c])
    s0 = Sum(p, cp, d0.at[p.c], rx0, rz0, 2, rc0, d0.at[1 - p.c])
    s1 = Sum(p, cp, d1.at[p.c], rx1, None, 2, vgu.at[:, :, :, 0:32, 1280:2816], d1.at[1 - p.c])
    up_tile(0, d0, 0, 4)
    s0.start(0, 2)
    up_tile(0, d0, 4, 8)
    s0.start(2, 4)
    for c in uc[0]:
        c.wait_recv()
    lax.fori_loop(4, 5, tile, 0)
    s0.stage_x(0)
    hidden_tile(1280, 128)
    s0.stage_x(1)
    ring = RingSum(p, cp, gpart, recv_g, relay_g)
    for n in range(4):
        out = dot_nt(dgu[...], vgu[n].reshape(512, 2816))
        gpart[:, :, n * 512:(n + 1) * 512] = out.astype(bf).reshape(4, 128, 512)
        if n % 2:
            ring.start((n - 1) * 512, 1024)
    ring.near()
    for c in sum(ux + uc, []):
        cp.sent(c)
    pl.semaphore_signal(ready, inc=1, device_id=sib, device_id_type=pl.DeviceIdType.MESH)
    up_tile(1280, d1, 0, 4)
    pl.semaphore_wait(ready, 1)
    s1.start(0, 2)
    up_tile(1280, d1, 4, 8)
    s1.start(2, 4)
    ring.relay()
    s1.stage_x(0)
    s0.stage_z()
    down_half(1 - p.c, 0, 6)
    s1.stage_x(1)
    down_half(1 - p.c, 6, 11)
    sd.start()
    down_half(p.c, 0, 11)

    def result(n, _):
        cols = pl.ds(pl.multiple_of(n * 512, 512), 512)
        out = jnp.dot(hid[...], vd[:, cols], preferred_element_type=f)
        ent[:, :, cols] = out.astype(bf).reshape(4, 128, 512)
        return 0

    lax.fori_loop(0, 4, result, 0)
    keeps = [pltpu.make_async_copy(ent, rpart, lsem.at[1])]
    keeps[0].start()
    sd.stage_core()
    keeps.append(pltpu.make_async_copy(dd.at[p.c], hd, lsem.at[1 + len(keeps)]))
    keeps[-1].start()
    ring.finish()
    for c in rest:
        c.wait()
    sums[...] = jnp.zeros_like(sums)

    def block(i, _):
        r = pl.ds(pl.multiple_of(i * ROWS, ROWS), ROWS)
        g = gpart[p.y, r].astype(f) + recv_g[0, r].astype(f) + recv_g[1, r].astype(f)
        m, inv = norm_rows(mid[r])
        sums[0:1] += jnp.sum(g * m, axis=0, keepdims=True)
        sums[1:2] += jnp.sum(g, axis=0, keepdims=True)
        e = g * gains[2:3, :]
        out = cot[r].astype(f) + inv * (e - jnp.mean(e, axis=-1, keepdims=True) - m * jnp.mean(e * m, axis=-1, keepdims=True))
        gmid[r] = out
        low[r] = out.astype(bf)
        return 0

    lax.fori_loop(0, 128 // ROWS, block, 0)
    for a, b in ((gmid, gmid_out), (low, low_out), (sums, sums_out)):
        keeps.append(pltpu.make_async_copy(a, b, lsem.at[1 + len(keeps)]))
        keeps[-1].start()
    keeps.append(pltpu.make_async_copy(s0.stage_sum(), j0, lsem.at[1 + len(keeps)]))
    keeps[-1].start()
    s1.stage_own()
    keeps.append(pltpu.make_async_copy(d1.at[p.c, :, p.xl], i1, lsem.at[1 + len(keeps)]))
    keeps[-1].start()
    cp.finish()
    for c in keeps:
        c.wait()


def second_step(ggu, gd, ent, cots, mid, cot, gains):
    f, bf = jnp.float32, jnp.bfloat16
    S = jax.ShapeDtypeStruct
    hbm, vm = pl.BlockSpec(memory_space=pl.ANY), pl.BlockSpec(memory_space=pltpu.VMEM)
    V = pltpu.VMEM
    return pl.pallas_call(
        second_kernel,
        out_shape=(S((4, 128, 2048), bf), S((128, 2048), f), S((128, 2048), bf), S((8, 2048), f),
                   S((4, 2, 11, 16, 1024), bf), S((4, 32, 1280), bf), S((4, 4, 32, 1536), bf)),
        in_specs=[hbm] * 7, out_specs=(hbm,) * 7,
        scratch_shapes=[
            V((4, 2, 4, 64, 2816), bf), V((1408, 2048), bf), V((4, 128, 2048), bf), V((4, 128, 2048), bf),
            V((512, 1408), bf), V((512, 2816), bf), V((4, 128, 2048), bf), V((2, 128, 2048), bf),
            V((2, 4, 2, 11, 16, 1024), bf), V((2, 4, 2, 4, 32, 1280), bf), V((2, 4, 2, 4, 32, 1536), bf),
            V((4, 2, 11, 16, 1024), bf), V((4, 2, 4, 32, 1280), bf), V((4, 4, 32, 1280), bf), V((3, 4, 32, 1280), bf), V((4, 4, 32, 1536), bf), V((2, 64, 2048), bf),
            V((128, 2048), f), V((128, 2048), bf), V((8, 2048), f), V((128, 2048), f), V((128, 2048), bf), V((8, 2048), f),
            pltpu.SemaphoreType.DMA((31,)), pltpu.SemaphoreType.DMA((31,)), pltpu.SemaphoreType.DMA((14,)),
            pltpu.SemaphoreType.REGULAR],
        compiler_params=pltpu.CompilerParams(collective_id=3, has_side_effects=True, vmem_limit_bytes=64 * 2**20 - 2**18),
        name="second_step",
    )(ggu, gd, ent, cots, mid, cot, gains)


class Finish:
    def __init__(self, p, cp, here, rxh, via, total, out, lsem, plane, unit=32):
        self.via, self.cut = via, (here.shape[0] + 1) // 2
        self.unit = unit
        self.p, self.cp, self.here, self.rxh, self.total, self.out, self.lsem, self.plane = p, cp, here, rxh, total, out, lsem, plane

    def stage_xh(self):
        p, k, n = self.p, self.cut, self.here.shape[0]
        self.steps = [self.cp.push(self.here.at[0:k], self.via.at[0:k], p.at(dx=1)),
                      self.cp.push(self.here.at[k:n], self.via.at[k:n], p.at(dx=-1))]

    def stage_relay(self):
        p, k, n = self.p, self.cut, self.here.shape[0]
        self.steps[0].wait_recv()
        last = [self.cp.push(self.via.at[0:k], self.rxh.at[0:k], p.at(dx=1))]
        self.steps[1].wait_recv()
        self.last_xh = last + [self.cp.push(self.via.at[k:n], self.rxh.at[k:n], p.at(dx=-1))]

    def stage_y(self):
        p, cp, out = self.p, self.cp, self.out
        for c in self.last_xh:
            c.wait_recv()
        add_into(self.total, (self.here, self.rxh))
        if self.plane:
            there = out.at[..., pl.ds(pl.multiple_of(p.c * 1024, 1024), 1024)]
            self.own = pltpu.make_async_copy(self.total, there, self.lsem)
            self.own.start()
            self.ys = [cp.push(self.total, there, p.at(dc=1))]
        else:
            half = pl.ds(pl.multiple_of(p.c * self.unit, self.unit), self.unit)
            self.own = pltpu.make_async_copy(self.total.at[p.y], out.at[p.y, half], self.lsem)
            self.own.start()
            self.ys = [cp.push(self.total.at[lax.rem(p.y + d, 4)], out.at[p.y, half], p.at(dy=d)) for d in (1, 3, 2)]

    def stage_c(self):
        p, out = self.p, self.out
        for c in self.ys:
            c.wait_recv()
        self.own.wait()
        self.last = []
        if not self.plane:
            half = pl.ds(pl.multiple_of(p.c * self.unit, self.unit), self.unit)
            self.last = [self.cp.push(out.at[:, half], out.at[:, half], p.at(dc=1))]

    def finish(self):
        for c in self.last:
            c.wait_recv()


def third_kernel(low, go, gq, e1, qkv, prb, mix, tab, rpart, mid_in, tok_in, gmid_in, gains_in, sums_in, hd, j0, i1,
                 act_out, ing_out, od, o0, o1, oq0, oq1, oo, os,
                 vgml, vo, vq, ve, vqkv, vprb, vmix, vtab, gp, gpart, recv_g, relay_g, vrp, recv_r, relay_r, wide,
                 mid, tok, gmid, gains, sums, act, ing,
                 vhd, rxxd, rzd, rxd, ved, td, vj0, rx0, ve0, t0, vi1, rz1, rx1, ve1, t1,
                 dq0, rcq0, rxq0, rzq0, rxhq0, vq0, tq0, dq1, rcq1, rxq1, rzq1, rxhq1, vq1, tq1,
                 dw, rco, rxo, rzo, rxho, veo, to, ds, rcs, rxs, rzs, rxhs, ves, ts,
                 send, recv, lsem):
    p = Place()
    f, bf = jnp.float32, jnp.bfloat16
    pairs_in = [(low, vgml.at[p.y]), (hd, vhd), (j0, vj0), (i1, vi1), (go, vo), (qkv, vqkv), (prb, vprb), (tab, vtab),
                (e1, ve), (mix, vmix), (gq, vq), (rpart, vrp),
                (mid_in, mid), (tok_in, tok), (gmid_in, gmid), (gains_in, gains), (sums_in, sums)]
    loads = [pltpu.make_async_copy(a, b, lsem.at[i]) for i, (a, b) in enumerate(pairs_in)]
    for c in loads[:8]:
        c.start()
    barrier(peers(p))
    cp = Copies(send, recv)
    ls = Spread(p, cp, low, vgml)
    ls.start()
    s1 = Sum(p, cp, None, None, rz1, 2)
    sd = Sum(p, cp, vhd, rxxd, rzd, None)
    f0 = Finish(p, cp, vj0, rx0, ve0, t0, o0, lsem.at[19], False)
    loads[1].wait()
    sd.stage_x()
    loads[2].wait()
    f0.stage_xh()
    loads[3].wait()
    s1.push_z(vi1)
    for c in loads[8:]:
        c.start()
    loads[0].wait()
    for c in loads[4:8]:
        c.wait()

    def attend(i):
        gm = dot_nt(vgml[i], vo[...].reshape(512, 2048)).astype(bf)
        cosine, sine = vtab[i, 0], -vtab[i, 1]
        for n in range(4):
            a, b, c = (slice(n * 384 + k * 128, n * 384 + (k + 1) * 128) for k in range(3))
            q, k, v = vqkv[i, :, a], vqkv[i, :, b], vqkv[i, :, c]
            prob = vprb[i, n]
            g = stack_heads(gm[:, n * 128:(n + 1) * 128])
            gv = dot_tn(prob.astype(bf), g)
            gprob = dot_nt(g, v)
            gs = (prob * (gprob - jnp.sum(prob * gprob, axis=-1, keepdims=True))).astype(bf)
            gq_ = merge_heads(jnp.dot(gs, k, preferred_element_type=f)) * SCALE
            gk = dot_tn(gs, stack_heads(q)) * SCALE
            gp[i, :, a] = turn(gq_, cosine, sine).astype(bf)
            gp[i, :, b] = turn(gk, cosine, sine).astype(bf)
            gp[i, :, c] = gv.astype(bf)

    attend(p.y)
    ls.relay(0)
    ls.relay(1)
    attend(lax.rem(p.y + 3, 4))
    attend(lax.rem(p.y + 1, 4))
    f0.stage_relay()
    f1 = Finish(p, cp, s1.stage_sum(), rx1, ve1, t1, o1, lsem.at[20], False)
    f1.stage_xh()
    ls.finish()
    loads[11].wait()
    rr = RingSum(p, cp, vrp, recv_r, relay_r)
    rr.start(0, 2048)
    rr.near()
    attend(lax.rem(p.y + 2, 4))
    sd.stage_z()
    loads[8].wait()

    def qkv_tile(first, dq):
        def body(i, _):
            rows = pl.ds(pl.multiple_of(i * 256, 256), 256)
            out = dot_tn(ve[:, :, rows].reshape(512, 256), gp[:, :, first:first + 768].reshape(512, 768))
            out = out.astype(bf).reshape(4, 2, 32, 768)
            dq[0, i // 2, lax.rem(i, 2)] = out[:, 0]
            dq[1, i // 2, lax.rem(i, 2)] = out[:, 1]
            return 0
        lax.fori_loop(0, 8, body, 0)

    qkv_tile(0, dq0)
    sq0 = Sum(p, cp, dq0.at[p.c], rxq0, rzq0, 2, rcq0, dq0.at[1 - p.c])
    sq0.start()
    f1.stage_relay()
    qkv_tile(768, dq1)
    sq1 = Sum(p, cp, dq1.at[p.c], rxq1, rzq1, 2, rcq1, dq1.at[1 - p.c])
    sq1.start()
    sq0.stage_x()
    for c in loads[9:11] + loads[12:]:
        c.wait()
    ring = RingSum(p, cp, gpart, recv_g, relay_g)
    for n in range(4):
        out = dot_nt(gp[...].reshape(512, 1536), vq[n].reshape(512, 1536))
        gpart[:, :, n * 512:(n + 1) * 512] = out.astype(bf).reshape(4, 128, 512)
        if n % 2:
            ring.start((n - 1) * 512, 1024)
    ring.near()

    def out_tile(h, _):
        cols = pl.ds(pl.multiple_of(h * 512, 512), 512)
        out = dot_tn(vmix[...].reshape(512, 512), vgml[:, :, cols].reshape(512, 512)).astype(bf)
        dw[h // 2, :, :, :, pl.ds(pl.multiple_of(lax.rem(h, 2) * 512, 512), 512)] = out.reshape(4, 2, 64, 512)
        return 0

    lax.fori_loop(0, 4, out_tile, 0)
    so = Sum(p, cp, dw.at[p.c], rxo, rzo, 32, rco, dw.at[1 - p.c])
    so.start()
    sq1.stage_x()

    rows = []
    for k in range(3):
        for n in range(4):
            first = n * 384 + k * 128
            rows.append(jnp.sum(gp[:, :, first:first + 128].reshape(512, 128).astype(f), axis=0, keepdims=True))
    rows = jnp.concatenate(rows + [jnp.zeros((4, 128), f)], axis=0).astype(bf)
    for i in range(8):
        for y in range(4):
            ds[1, i // 2, i % 2, y] = rows
    so.stage_x()
    ring.relay()
    sq0.stage_z()
    sq1.stage_z()
    fd = Finish(p, cp, sd.stage_sum(), rxd, ved, td, od, lsem.at[18], True)
    fd.stage_xh()
    wide[...] = jnp.zeros_like(wide)
    wide[2:4] = sums[0:2]
    ring.finish()

    def block(i, _):
        r = pl.ds(pl.multiple_of(i * ROWS, ROWS), ROWS)
        g = gpart[p.y, r].astype(f) + recv_g[0, r].astype(f) + recv_g[1, r].astype(f)
        m, inv = norm_rows(tok[r].astype(f))
        wide[0:1] += jnp.sum(g * m, axis=0, keepdims=True)
        wide[1:2] += jnp.sum(g, axis=0, keepdims=True)
        e = g * gains[0:1, :]
        out = gmid[r] + inv * (e - jnp.mean(e, axis=-1, keepdims=True) - m * jnp.mean(e * m, axis=-1, keepdims=True))
        ing[r] = out.astype(bf)
        return 0

    lax.fori_loop(0, 128 // ROWS, block, 0)
    keeps = [pltpu.make_async_copy(ing, ing_out, lsem.at[1])]
    keeps[0].start()
    for i in range(16):
        z, xl, y = i // 4, (i // 2) % 2, (i % 2) * 2
        piece = wide[:, i * 128:(i + 1) * 128]
        ds[0, z, xl, y] = piece.astype(bf)
        ds[0, z, xl, y + 1] = pltpu.roll(piece, 64, 1).astype(bf)
    ss = Sum(p, cp, ds.at[p.c], rxs, rzs, 2, rcs, ds.at[1 - p.c])
    ss.start()
    rr.relay()
    f0.stage_y()
    f1.stage_y()
    ss.stage_x()
    fd.stage_relay()
    fq0 = Finish(p, cp, sq0.stage_sum(), rxhq0, vq0, tq0, oq0, lsem.at[22], False)
    fq0.stage_xh()
    so.stage_z()
    ss.stage_z()
    fq1 = Finish(p, cp, sq1.stage_sum(), rxhq1, vq1, tq1, oq1, lsem.at[0], False)
    fq1.stage_xh()
    fq0.stage_relay()
    fs = Finish(p, cp, ss.stage_sum(), rxhs, ves, ts, os, lsem.at[23], False, 16)
    fs.stage_xh()
    fo = Finish(p, cp, so.stage_sum(), rxho, veo, to, oo, lsem.at[21], True)
    fo.stage_xh()
    fd.stage_y()
    fq1.stage_relay()
    fs.stage_relay()
    fq0.stage_y()
    fd.stage_c()
    f0.stage_c()
    f1.stage_c()
    fo.stage_relay()
    fq1.stage_y()
    fs.stage_y()
    fo.stage_y()
    rr.finish()

    def final(i, _):
        r = pl.ds(pl.multiple_of(i * ROWS, ROWS), ROWS)
        act[r] = (mid[r] + vrp[p.y, r].astype(f) + recv_r[0, r].astype(f) + recv_r[1, r].astype(f)).astype(bf)
        return 0

    lax.fori_loop(0, 128 // ROWS, final, 0)
    keeps.append(pltpu.make_async_copy(act, act_out, lsem.at[2]))
    keeps[1].start()
    fq0.stage_c()
    fq1.stage_c()
    fs.stage_c()
    fo.stage_c()
    for g in (fd, f0, f1, fq0, fq1, fo, fs):
        g.finish()
    cp.finish()
    for c in keeps:
        c.wait()


def third_step(*args):
    f, bf = jnp.float32, jnp.bfloat16
    S = jax.ShapeDtypeStruct
    hbm, vm = pl.BlockSpec(memory_space=pl.ANY), pl.BlockSpec(memory_space=pltpu.VMEM)
    V = pltpu.VMEM

    def sums(tail):
        return [V((2, 4, 2) + tail, bf), V((4, 2) + tail, bf), V((4,) + tail, bf), V((3,) + tail, bf), V(tail, bf), V(tail, bf), V(tail, bf)]

    return pl.pallas_call(
        third_kernel,
        out_shape=(S((128, 2048), bf), S((128, 2048), bf), S((11, 16, 2048), bf), S((4, 64, 1280), bf), S((4, 64, 1536), bf),
                   S((4, 64, 768), bf), S((4, 64, 768), bf), S((64, 2048), bf), S((4, 32, 128), bf)),
        in_specs=[hbm] * 17, out_specs=(hbm,) * 9,
        scratch_shapes=[
            V((4, 128, 2048), bf), V((4, 2, 64, 2048), bf), V((4, 2, 4, 64, 1536), bf), V((4, 128, 2048), bf),
            V((4, 128, 1536), bf), V((4, 4, 256, 128), f), V((4, 128, 512), bf), V((4, 2, 128, 128), f),
            V((4, 128, 1536), bf), V((4, 128, 2048), bf), V((2, 128, 2048), bf), V((2, 64, 2048), bf),
            V((4, 128, 2048), bf), V((2, 128, 2048), bf), V((2, 64, 2048), bf), V((16, 2048), f),
            V((128, 2048), f), V((128, 2048), bf), V((128, 2048), f), V((8, 2048), f), V((8, 2048), f), V((128, 2048), bf), V((128, 2048), bf),
            V((4, 2, 11, 16, 1024), bf), V((4, 11, 16, 1024), bf), V((3, 11, 16, 1024), bf), V((11, 16, 1024), bf), V((11, 16, 1024), bf), V((11, 16, 1024), bf),
            V((4, 32, 1280), bf), V((4, 32, 1280), bf), V((4, 32, 1280), bf), V((4, 32, 1280), bf),
            V((4, 4, 32, 1536), bf), V((3, 4, 32, 1536), bf), V((4, 32, 1536), bf), V((4, 32, 1536), bf), V((4, 32, 1536), bf)]
        + sums((4, 32, 768)) * 2 + sums((64, 1024)) + sums((4, 16, 128))
        + [pltpu.SemaphoreType.DMA((100,)), pltpu.SemaphoreType.DMA((100,)), pltpu.SemaphoreType.DMA((24,))],
        compiler_params=pltpu.CompilerParams(collective_id=4, has_side_effects=True, vmem_limit_bytes=62 * 2**20),
        name="third_step",
    )(*args)


def layout_kernel(oq0_in, oq1_in, o0_in, o1_in, oo_in, od_in, os_in, act_in, ing_in, act, ing, qkv_out, out_out, gate_out, up_out, down_out, g1, b1, g2, b2, bq,
                  oq0, oq1, o0, o1, oo, od, os, vact, ving, qkv, out, gate, up, down, sems):
    f = jnp.float32
    copies = ((oq0_in, oq0), (oq1_in, oq1), (o0_in, o0), (o1_in, o1), (oo_in, oo), (od_in, od), (os_in, os), (act_in, vact), (ing_in, ving))
    copies = [pltpu.make_async_copy(a, b, sems.at[i]) for i, (a, b) in enumerate(copies)]
    for c in copies:
        c.start()
    keeps = []

    def keep(src, dst):
        keeps.append(pltpu.make_async_copy(src, dst, sems.at[len(keeps) + 9]))
        keeps[-1].start()

    copies[0].wait()
    copies[1].wait()
    for g in range(48):
        k, h = g // 16, 2 * (g % 16)
        pieces = []
        for m in range(2):
            head = h + m
            pieces.append((m * 64, m * 64 + 64, head % 4, (head // 8) * 384 + k * 128 + ((head // 4) % 2) * 64))
        def load(j, t):
            src, at = (oq0, t) if t < 6 else (oq1, t - 6)
            return src[j, :, at * 128:(at + 1) * 128].astype(f)
        qkv[:, g * 128:(g + 1) * 128] = moved_lanes(pieces, load)
    keep(qkv, qkv_out)
    copies[2].wait()
    copies[3].wait()
    for n, dst in enumerate((gate, up)):
        def load(j, t):
            t = 2 * t + n
            src, at = (o0, t) if t < 10 else (o1, t - 10)
            return src[j, :, at * 128:(at + 1) * 128].astype(f)
        for g in range(44):
            dst[:, g * 128:(g + 1) * 128] = moved_lanes(shard_pieces(g), load)
        keep(dst, (gate_out, up_out)[n])
    for c in copies[4:]:
        c.wait()
    keep(vact, act)
    keep(ving, ing)
    out[...] = oo[...].astype(f)
    keep(out, out_out)
    down[...] = od[...].reshape(176, 2048).astype(f)
    keep(down, down_out)
    norms = os[0, 0:16].astype(f) + os[1, 0:16].astype(f) + os[2, 0:16].astype(f) + os[3, 0:16].astype(f)
    for k, v in enumerate((g1, b1, g2, b2)):
        v[...] = norms[k, 0:64]
    bias = []
    shard = (lax.axis_index("z") * 2 + lax.axis_index("xl")) * 4 + lax.axis_index("y")
    row = lax.broadcasted_iota(jnp.int32, (16, 128), 0)
    lane = lax.broadcasted_iota(jnp.int32, (16, 128), 1)
    for m in range(3):
        total = jnp.zeros((16, 128), f)
        for j in range(4):
            place = (row // 4) * 32 + (lax.rem(row, 4) * 2 + lane // 64) * 4 + j
            total = total + jnp.where((place == shard * 3 + m) & (row < 12), os[j, 16:32].astype(f), 0.0)
        total = jnp.sum(total, axis=0, keepdims=True)
        total = total + pltpu.roll(jnp.broadcast_to(total, (8, 128)), 64, 1)[0:1]
        bias.append(total[0, 0:64])
    bq[...] = jnp.concatenate(bias)
    for c in keeps:
        c.wait()


def layout_step(*args):
    f, bf = jnp.float32, jnp.bfloat16
    S = jax.ShapeDtypeStruct
    hbm, vm = pl.BlockSpec(memory_space=pl.ANY), pl.BlockSpec(memory_space=pltpu.VMEM)
    V = pltpu.VMEM
    return pl.pallas_call(
        layout_kernel,
        out_shape=(S((128, 2048), bf), S((128, 2048), bf), S((64, 6144), f), S((64, 2048), f), S((64, 5632), f), S((64, 5632), f),
                   S((176, 2048), f), S((64,), f), S((64,), f), S((64,), f), S((64,), f), S((192,), f)),
        in_specs=[hbm] * 9, out_specs=(hbm,) * 7 + (vm,) * 5,
        scratch_shapes=[V((4, 64, 768), bf), V((4, 64, 768), bf), V((4, 64, 1280), bf), V((4, 64, 1536), bf), V((64, 2048), bf),
                        V((11, 16, 2048), bf), V((4, 32, 128), bf), V((128, 2048), bf), V((128, 2048), bf), V((64, 6144), f), V((64, 2048), f), V((64, 5632), f),
                        V((64, 5632), f), V((176, 2048), f), pltpu.SemaphoreType.DMA((16,))],
        compiler_params=pltpu.CompilerParams(vmem_limit_bytes=60 * 2**20),
        name="layout_step",
    )(*args)


def local(tokens, segment_ids, cotangent, ln1_gain, ln1_bias, qkv_weight, qkv_bias, out_weight,
          ln2_gain, ln2_bias, gate_weight, up_weight, down_weight):
    cots, gq, ggu, go, gd, e1, qkv, prb, mix, tab, gains, mid, ent = first_step(
        tokens, cotangent, segment_ids, qkv_weight, ln1_gain, ln1_bias, ln2_gain, ln2_bias, qkv_bias, gate_weight, up_weight, out_weight, down_weight)
    rpart, gmid, low, sums, hd, j0, i1 = second_step(ggu, gd.reshape(1408, 2048), ent, cots, mid, cotangent, gains)
    act, ing, od, o0, o1, oq0, oq1, oo, os = third_step(
        low, go, gq, e1, qkv, prb, mix, tab, rpart, mid, tokens, gmid, gains, sums, hd, j0, i1)
    act, ing, qkv_grad, out_grad, gate_grad, up_grad, down_grad, g1, b1, g2, b2, bias = layout_step(
        oq0, oq1, o0, o1, oo, od, os, act, ing)
    return act, ing, g1, b1, qkv_grad, bias, out_grad, g2, b2, gate_grad, up_grad, down_grad


def solution(mesh):
    fine = Mesh(mesh.devices.reshape(2, 2, 4, 2, 4), AXES)
    whole, rows = P(AXES, None), P(("z", "xl", "y"), None)
    vector = P(("z", "xl", "y"))
    return jax.shard_map(
        local, mesh=fine,
        in_specs=(whole, whole, whole, vector, vector, rows, vector, rows, vector, vector, rows, rows, rows),
        out_specs=(whole, whole, vector, vector, rows, vector, rows, vector, vector, rows, rows, rows),
        check_vma=False,
    )
```
